128 devices in a mesh: dp: 4 (over x), seq: 32 (over z, y, core).
Axes of the slice: x: 4, y: 4, z: 4, core: 2. Of those that a mesh axis runs over, the one named last changes fastest.
Arguments:
- ssm_input: bfloat16 [4, 8192, 3072], P('dp', 'seq'), may hold values from -6 to 6
- gate_input: bfloat16 [4, 8192, 3072], P('dp', 'seq'), may hold values from -6 to 6
- input_map: bfloat16 [4, 8192, 128], P('dp', 'seq'), may hold values from -0.52734375 to 0.52734375
- output_map: bfloat16 [4, 8192, 128], P('dp', 'seq'), may hold values from -6 to 6
- step_logit: bfloat16 [4, 8192, 48], P('dp', 'seq'), may hold values from -5 to 5
- step_bias: float32 [48], replicated, may hold values from -1 to 1
- decay_rate: float32 [48], replicated, may hold values from 6.1035156e-07 to 0.05
- skip_gain: float32 [48], replicated, may hold values from 0.5 to 1.5
- norm_gain: float32 [3072], replicated, may hold values from 0.1 to 1.9
- out_weight: bfloat16 [3072, 1536], replicated, may hold values from -0.109375 to 0.109375
- resets: int32 [4, 4], P('dp'), may hold values from 1 to 8191
- out_grad: bfloat16 [4, 8192, 1536], P('dp', 'seq'), may hold values from -6 to 6
Outputs:
- mixed_out: bfloat16 [4, 8192, 1536], P('dp', 'seq')
- grad_input: bfloat16 [4, 8192, 3072], P('dp', 'seq')
- grad_gate: bfloat16 [4, 8192, 3072], P('dp', 'seq')
- grad_inmap: bfloat16 [4, 8192, 128], P('dp', 'seq')
- grad_outmap: bfloat16 [4, 8192, 128], P('dp', 'seq')
- grad_step: bfloat16 [4, 8192, 48], P('dp', 'seq')
- grad_bias: float32 [48], replicated
- grad_rate: float32 [48], replicated
- grad_skip: float32 [48], replicated
- grad_gain: float32 [3072], replicated
- grad_weight: float32 [3072, 1536], P('seq')
The draws below stay inside these ranges and needn't reach their ends.
All inputs are finite; a program needn't handle non-finite values.
Results may differ from the reference program's by a relative error of at most 0.0049.
Values sent between devices are 32-bit elements; how exact they have to be, the bound alone decides.
A program may use at most 384 MiB of HBM per device.

```python
import jax
import jax.numpy as jnp
from jax import lax

D = 1536
H = 48
NS = 128
HP = 3072
SPAN = 128
RESETS = 4
TRAJS = 4
TRAJ_LEN = 8192


def draw_decay_rate(key, part):
    lowest = 0.005 / TRAJ_LEN
    fastest = 0.05
    low_log = jnp.log(jnp.float32(lowest))
    high_log = jnp.log(jnp.float32(fastest))
    spots = jax.random.uniform(jax.random.fold_in(key, 11), (H,), jnp.float32)
    log_rates = low_log + spots * (high_log - low_log)
    order = jax.random.permutation(jax.random.fold_in(key, 13), H)
    log_rates = log_rates.at[order[0]].set(low_log).at[order[1]].set(high_log)
    return jnp.clip(jnp.exp(log_rates), lowest, fastest).astype(jnp.float32)


def plant(array, own_key, least, largest):
    extent = array.shape
    place = [jax.random.randint(jax.random.fold_in(own_key, axis), (), 0, extent[axis]) for axis in range(len(extent))]
    array = array.at[tuple(place)].set(least)
    longest = extent.index(max(extent))
    place[longest] = (place[longest] + 1) % extent[longest]
    return array.at[tuple(place)].set(largest)


def steps_of(own_key, dims, split, smallest, high):
    factor_of = 1.0
    for position, shards_of in split:
        steps = jax.random.uniform(jax.random.fold_in(jax.random.fold_in(own_key, 6), position), (shards_of,), jnp.float32, smallest / len(split), high / len(split))
        factor_of = factor_of * jnp.repeat(jnp.exp(steps), dims[position] // shards_of).reshape((-1,) + (1,) * (len(dims) - 1 - position))
    return factor_of


def centred(rng, shape, spread, limit, shards=(), kind=jnp.bfloat16):
    values = jax.random.normal(rng, shape, jnp.float32) * spread
    if len(shards) > 0:
        values = steps_of(rng, shape, shards, -0.22, 0.18) * values
    return jnp.clip(values, min=-limit, max=limit).astype(kind)


def setup_inputs(seed: int = 0) -> dict:
    splits = jax.random.split(jax.random.key(seed), 13)
    return {
        "ssm_input": centred(splits[0], (TRAJS, TRAJ_LEN, HP), 1.0, 6.0, ((0, 4), (1, 32))),
        "gate_input": centred(splits[1], (TRAJS, TRAJ_LEN, HP), 1.0, 6.0, ((0, 4), (1, 32))),
        "input_map": centred(splits[2], (TRAJS, TRAJ_LEN, NS), (NS ** -0.5), 0.52734375, ((0, 4), (1, 32))),
        "output_map": centred(splits[3], (TRAJS, TRAJ_LEN, NS), 1.0, 6.0, ((0, 4), (1, 32))),
        "step_logit": centred(splits[4], (TRAJS, TRAJ_LEN, H), 1.0, 5.0, ((0, 4), (1, 32))),
        "step_bias": jnp.clip(jax.random.uniform(splits[5], (H,), jnp.float32, -1.0, 1.0), -1.0, 1.0),
        "decay_rate": draw_decay_rate(jax.random.fold_in(splits[12], 71), 0),
        "skip_gain": jnp.clip(jax.random.uniform(splits[7], (H,), jnp.float32, 0.5, 1.5), 0.5, 1.5),
        "norm_gain": jnp.clip(1.0 + 0.18 * jax.random.normal(splits[8], (HP,), jnp.float32), 0.1, 1.9),
        "out_weight": centred(splits[9], (HP, D), HP ** -0.5, 0.109375),
        "resets": plant(jax.random.randint(splits[10], (TRAJS, RESETS), 1, TRAJ_LEN), jax.random.fold_in(splits[10], 1), 1, TRAJ_LEN - 1).astype(jnp.int32),
        "out_grad": centred(splits[11], (TRAJS, TRAJ_LEN, D), 1.0, 6.0, ((0, 4), (1, 32))),
    }


highest = lax.Precision.HIGHEST

def block_step(state_in, inputs):
    x_blk, b_blk, c_blk, step_blk, decay_blk, flag_blk = inputs
    cumulative = jnp.cumsum(decay_blk, axis=0)
    counts = jnp.cumsum(flag_blk)
    block_len = flag_blk.shape[0]
    row_ids = lax.broadcasted_iota(jnp.int32, (block_len, block_len), 0)
    col_ids = lax.broadcasted_iota(jnp.int32, (block_len, block_len), 1)
    in_mask = ((row_ids >= col_ids) & (counts[:, None] == counts[None, :]))[:, :, None]
    gap_vals = cumulative[:, None, :] - cumulative[None, :, :]
    decay_mat = jnp.where(in_mask, jnp.exp(jnp.where(in_mask, gap_vals, 0.0)), 0.0)
    gram_mat = jnp.einsum('in,jn->ij', c_blk, b_blk, precision=highest)
    mixing = gram_mat[:, :, None] * decay_mat * step_blk[None, :, :]
    y_blk = jnp.einsum('ijh,jhp->ihp', mixing, x_blk, precision=highest)
    opened = (counts == 0)[:, None]
    from_start = jnp.where(opened, jnp.exp(jnp.where(opened, cumulative, 0.0)), 0.0)
    y_blk = y_blk + from_start[:, :, None] * jnp.einsum('in,hpn->ihp', c_blk, state_in, precision=highest)
    keep_mask = (counts == counts[-1])[:, None]
    tail_weights = jnp.where(keep_mask, jnp.exp(jnp.where(keep_mask, cumulative[-1][None, :] - cumulative, 0.0)), 0.0) * step_blk
    whole_decay = jnp.where(counts[-1] == 0, jnp.exp(cumulative[-1]), 0.0)
    new_state = whole_decay[:, None, None] * state_in + jnp.einsum('jhp,jn->hpn', tail_weights[:, :, None] * x_blk, b_blk, precision=highest)
    return (new_state, y_blk)

def ssd_blocks(x_heads, b_float, c_float, step_vals, log_decay, flags, state_in):
    num_blocks = x_heads.shape[0] // SPAN

    def to_blocks(values):
        return values.reshape((num_blocks, SPAN) + values.shape[1:])
    final_state, y_blocks = lax.scan(block_step, state_in, (to_blocks(x_heads), to_blocks(b_float), to_blocks(c_float), to_blocks(step_vals), to_blocks(log_decay), to_blocks(flags)))
    return (final_state, y_blocks.reshape(x_heads.shape))

def gate_norm(y_ssd, x_float, z_float, skip_gain, norm_gain):
    num_heads = skip_gain.shape[0]
    rows_here = x_float.shape[0]
    y_full = y_ssd.reshape(rows_here, -1) + (x_float.reshape(rows_here, num_heads, -1) * skip_gain[None, :, None]).reshape(x_float.shape)
    gated_vals = y_full * jax.nn.silu(z_float)
    scale_inv = lax.rsqrt(lax.optimization_barrier(jnp.mean(gated_vals * gated_vals, axis=-1, keepdims=True)) + 1e-05)
    return gated_vals * scale_inv * norm_gain

def mixer(x_float, z_float, b_float, c_float, logit_float, step_bias, decay_rate, skip_gain, norm_gain, flags):
    num_heads = step_bias.shape[0]
    step_vals = jax.nn.softplus(logit_float + step_bias)
    log_decay = -decay_rate * step_vals
    x_heads = x_float.reshape(x_float.shape[0], num_heads, -1)
    state_in = jnp.zeros((num_heads, x_heads.shape[2], b_float.shape[1]), jnp.float32)
    final_state, y_ssd = ssd_blocks(x_heads, b_float, c_float, step_vals, log_decay, flags, state_in)
    return gate_norm(y_ssd, x_float, z_float, skip_gain, norm_gain)

def reference(ssm_input, gate_input, input_map, output_map, step_logit, step_bias, decay_rate, skip_gain, norm_gain, out_weight, resets, out_grad):
    length = ssm_input.shape[1]
    positions = jnp.arange(length, dtype=jnp.int32)
    out_rows, gx_rows, gz_rows, gb_rows, gc_rows, gs_rows = ([], [], [], [], [], [])
    weight_sum = jnp.zeros(out_weight.shape, jnp.float32)
    bias_sum = jnp.zeros(step_bias.shape, jnp.float32)
    rate_sum = jnp.zeros(decay_rate.shape, jnp.float32)
    skip_sum = jnp.zeros(skip_gain.shape, jnp.float32)
    gain_sum = jnp.zeros(norm_gain.shape, jnp.float32)
    for member in range(ssm_input.shape[0]):
        flags = lax.optimization_barrier(jnp.max((positions[:, None] == resets[member][None, :]).astype(jnp.int32), axis=1))

        def local_fn(x_float, z_float, b_float, c_float, logit_float, bias_in, rate_in, skip_in, gain_in):
            return mixer(x_float, z_float, b_float, c_float, logit_float, bias_in, rate_in, skip_in, gain_in, flags)
        normed_f, pullback = jax.vjp(local_fn, ssm_input[member].astype(jnp.float32), gate_input[member].astype(jnp.float32), input_map[member].astype(jnp.float32), output_map[member].astype(jnp.float32), step_logit[member].astype(jnp.float32), step_bias, decay_rate, skip_gain, norm_gain)
        normed = normed_f.astype(jnp.bfloat16)
        out_rows.append(jnp.dot(normed, out_weight, preferred_element_type=jnp.float32).astype(jnp.bfloat16))
        normed_grad = jnp.dot(out_grad[member], out_weight.T, preferred_element_type=jnp.float32)
        gradients = pullback(normed_grad)
        gx_rows.append(gradients[0].astype(jnp.bfloat16))
        gz_rows.append(gradients[1].astype(jnp.bfloat16))
        gb_rows.append(gradients[2].astype(jnp.bfloat16))
        gc_rows.append(gradients[3].astype(jnp.bfloat16))
        gs_rows.append(gradients[4].astype(jnp.bfloat16))
        bias_sum = bias_sum + gradients[5]
        rate_sum = rate_sum + gradients[6]
        skip_sum = skip_sum + gradients[7]
        gain_sum = gain_sum + gradients[8]
        weight_sum = weight_sum + jnp.dot(normed.T, out_grad[member], preferred_element_type=jnp.float32)
    return (jnp.stack(out_rows), jnp.stack(gx_rows), jnp.stack(gz_rows), jnp.stack(gb_rows), jnp.stack(gc_rows), jnp.stack(gs_rows), bias_sum, rate_sum, skip_sum, gain_sum, weight_sum)
```

```python
import functools

import jax
import jax.numpy as jnp
from jax import lax
from jax.experimental import pallas as pl
from jax.experimental.pallas import tpu as pltpu
from jax.sharding import PartitionSpec as P

MESH = pl.DeviceIdType.MESH
HIGHEST = lax.Precision.HIGHEST
VMEM_LIMIT = 60 * 1024 * 1024


def bdot(a, b, ca, cb):
    return lax.dot_general(
        a, b, (((ca,), (cb,)), ((), ())), preferred_element_type=jnp.float32
    )


def split(v):
    hi = v.astype(jnp.bfloat16)
    return hi, (v - hi.astype(jnp.float32)).astype(jnp.bfloat16)


def dot2(a, b, ca, cb):
    if isinstance(a, tuple) and isinstance(b, tuple):
        return bdot(a[0], b[0], ca, cb) + (bdot(a[0], b[1], ca, cb) + bdot(a[1], b[0], ca, cb))
    if isinstance(a, tuple):
        return bdot(a[0], b, ca, cb) + bdot(a[1], b, ca, cb)
    if isinstance(b, tuple):
        return bdot(a, b[0], ca, cb) + bdot(a, b[1], ca, cb)
    return bdot(a, b, ca, cb)


def exact(a, b):
    return jnp.dot(a, b, precision=HIGHEST, preferred_element_type=jnp.float32)


def scan_kernel(n, reverse, s_ref, thr_ref, spread_ref, out_ref, recv, stage, thr_buf, thr_wide,
                s_send, s_recv, t_send, t_recv, o_send, o_recv):
    me = lax.axis_index("seq")
    ns, width = s_ref.shape
    rows = ns // (n // 2)
    half = width // 2

    def place(k):
        r0 = pl.multiple_of(lax.div(k, 2) * rows, 8)
        l0 = pl.multiple_of(lax.rem(k, 2) * half, 128)
        return pl.ds(r0, rows), pl.ds(l0, half)

    barrier = pltpu.get_barrier_semaphore()

    def greet(i, _):
        peer = lax.rem(me + 1 + i, n)
        pl.semaphore_signal(barrier, inc=1, device_id={"seq": peer}, device_id_type=MESH)
        return 0

    lax.fori_loop(0, n - 1, greet, 0)
    pl.semaphore_wait(barrier, n - 1)

    def thr_copy(k, slot):
        return pltpu.make_async_remote_copy(
            src_ref=thr_ref, dst_ref=thr_buf.at[slot], send_sem=t_send.at[k],
            recv_sem=t_recv.at[slot], device_id={"seq": k}, device_id_type=MESH)

    def s_copy(k, slot):
        r, l = place(k)
        return pltpu.make_async_remote_copy(
            src_ref=s_ref.at[r, l], dst_ref=recv.at[slot], send_sem=s_send.at[k],
            recv_sem=s_recv.at[slot], device_id={"seq": k}, device_id_type=MESH)

    def o_copy(k, owner):
        r, l = place(owner)
        return pltpu.make_async_remote_copy(
            src_ref=stage.at[k], dst_ref=out_ref.at[r, l], send_sem=o_send.at[k],
            recv_sem=o_recv.at[owner], device_id={"seq": k}, device_id_type=MESH)

    def send(i, _):
        k = lax.rem(me + 1 + i, n)
        thr_copy(k, me).start()
        s_copy(k, me).start()
        return 0

    lax.fori_loop(0, n - 1, send, 0)
    my_r, my_l = place(me)
    recv[me] = s_ref[my_r, my_l]
    thr_buf[me] = thr_ref[...]

    def arrive(i, _):
        thr_copy(me, lax.rem(me + 1 + i, n)).wait_recv()
        return 0

    lax.fori_loop(0, n - 1, arrive, 0)
    thr_wide[...] = jnp.dot(thr_buf[:, 0, :], spread_ref[:, my_l], precision=HIGHEST,
                            preferred_element_type=jnp.float32)

    def hop(i, state):
        j = n - 1 - i if reverse else i

        @pl.when(j != me)
        def _():
            s_copy(me, j).wait_recv()

        stage[j] = state

        @pl.when(j != me)
        def _():
            o_copy(j, me).start()

        return thr_wide[pl.ds(j, 1), :] * state + recv[j]

    lax.fori_loop(0, n, hop, jnp.zeros((rows, half), jnp.float32))
    out_ref[my_r, my_l] = stage[me]

    def finish(i, _):
        k = lax.rem(me + 1 + i, n)
        o_copy(me, k).wait_recv()
        thr_copy(k, me).wait_send()
        s_copy(k, me).wait_send()
        o_copy(k, me).wait_send()
        return 0

    lax.fori_loop(0, n - 1, finish, 0)


def state_scan(n, state, thr, spread, reverse):
    ns, width = state.shape
    rows, half = ns // (n // 2), width // 2
    vmem = pl.BlockSpec(memory_space=pltpu.VMEM)
    return pl.pallas_call(
        functools.partial(scan_kernel, n, reverse),
        out_shape=jax.ShapeDtypeStruct((ns, width), jnp.float32),
        in_specs=[vmem] * 3,
        out_specs=vmem,
        scratch_shapes=[
            pltpu.VMEM((n, rows, half), jnp.float32),
            pltpu.VMEM((n, rows, half), jnp.float32),
            pltpu.VMEM((n, 8, 128), jnp.float32),
            pltpu.VMEM((n, half), jnp.float32),
        ] + [pltpu.SemaphoreType.DMA((n,))] * 6,
        compiler_params=pltpu.CompilerParams(
            collective_id=2 if reverse else 1, has_side_effects=True,
            vmem_limit_bytes=VMEM_LIMIT),
        name="scan_back" if reverse else "scan_ahead",
    )(state, thr, spread)


ORDERS = ((2, 1, 0), (1, 0, 2), (0, 2, 1))


def reduce_kernel(nt_ref, og_ref, small_ref, out_ref, small_out, part, nt_got, og_got,
                  agg1, full1, agg2, full2, agg3, full3, slots_c, slots_a, total,
                  c_send, c_recv, r_send, r_recv, x_send, x_recv, m_send, m_recv):
    xi = lax.axis_index("dp")
    s = lax.axis_index("seq")
    zi, yi, core = lax.div(s, 8), lax.rem(lax.div(s, 2), 4), lax.rem(s, 2)
    here = (zi, yi, xi)
    cols = part.shape[-1]
    third = cols // 3
    half = third // 2

    def at(axis, index):
        if axis == 2:
            return {"dp": index}
        z, y = (index, yi) if axis == 0 else (zi, index)
        return {"seq": (z * 4 + y) * 2 + core}

    sibling = {"seq": s + 1 - 2 * core}
    barrier = pltpu.get_barrier_semaphore()
    pl.semaphore_signal(barrier, inc=1, device_id=sibling, device_id_type=MESH)
    for axis in range(3):
        for d in range(1, 4):
            pl.semaphore_signal(barrier, inc=1, device_id=at(axis, lax.rem(here[axis] + d, 4)),
                                device_id_type=MESH)
    pl.semaphore_wait(barrier, 10)

    def remote(src, dst, ss, rs, to):
        return pltpu.make_async_remote_copy(src_ref=src, dst_ref=dst, send_sem=ss, recv_sem=rs,
                                            device_id=to, device_id_type=MESH)

    started = []

    copies = [
        remote(og_ref, og_got, c_send.at[0], c_recv.at[0], sibling),
        remote(nt_ref.at[:, 1 - core], nt_got, c_send.at[1], c_recv.at[1], sibling),
        remote(small_ref, slots_c.at[core], c_send.at[2], c_recv.at[2], sibling),
    ]
    for c in copies:
        c.start()
    slots_c[core] = small_ref[...]
    og = og_ref[...].astype(jnp.bfloat16)

    def own(b, _):
        z, y = lax.div(b, 4), lax.rem(b, 4)
        lhs = nt_ref[b, core].astype(jnp.bfloat16)
        part[z, y] = bdot(lhs, og, 1, 0).reshape(part.shape[2:])
        return 0

    lax.fori_loop(0, 16, own, 0)
    for c in copies:
        c.wait_recv()
    og2 = og_got[...].astype(jnp.bfloat16)

    def theirs(b, _):
        z, y = lax.div(b, 4), lax.rem(b, 4)
        lhs = nt_got[b].astype(jnp.bfloat16)
        part[z, y] += bdot(lhs, og2, 1, 0).reshape(part.shape[2:])
        return 0

    lax.fori_loop(0, 16, theirs, 0)
    total[...] = slots_c[0] + slots_c[1]

    bufs = ((agg1, full1), (agg2, full2), (agg3, full3))
    small_axes = (2, 1, 0)
    for step in range(3):
        agg, full = bufs[step]

        def small_copy(d):
            axis = small_axes[step]
            return remote(total, slots_a.at[step, here[axis]], m_send.at[step, d - 1],
                          m_recv.at[step, d - 1], at(axis, lax.rem(here[axis] + d, 4)))

        smalls = [small_copy(d) for d in (1, 2, 3)]
        for c in smalls:
            c.start()
        slots_a[step, here[small_axes[step]]] = total[...]

        def region(p, t, h=None):
            order = ORDERS[p]
            index = [slice(None)] * 3
            for done in order[:step]:
                index[done] = here[done]
            index[order[step]] = t
            lo = p * third + (0 if h in (None, 0) else half)
            return (*index, slice(None), pl.ds(lo, third if h is None else half))

        def sem(p, k):
            return r_send.at[step, p, k], r_recv.at[step, p, k]

        first, second, last = [], [], []
        for p in range(3):
            axis = ORDERS[p][step]
            me = here[axis]
            up, down, far = lax.rem(me + 1, 4), lax.rem(me + 3, 4), lax.rem(me + 2, 4)
            a = [
                remote(part.at[region(p, far, 0)], agg.at[p, 0], *sem(p, 0), at(axis, up)),
                remote(part.at[region(p, far, 1)], agg.at[p, 1], *sem(p, 1), at(axis, down)),
            ]
            b = [
                remote(part.at[region(p, up, 1)], full.at[p, 0, ..., pl.ds(half, half)], *sem(p, 2), at(axis, up)),
                remote(part.at[region(p, down, 0)], full.at[p, 1, ..., pl.ds(0, half)], *sem(p, 3), at(axis, down)),
            ]
            c = [
                remote(part.at[region(p, up, 0)], full.at[p, 0, ..., pl.ds(0, half)], *sem(p, 4), at(axis, up)),
                remote(part.at[region(p, down, 1)], full.at[p, 1, ..., pl.ds(half, half)], *sem(p, 5), at(axis, down)),
            ]
            first.append(a)
            second.append(b)
            last.append(c)
        for p in range(3):
            for c in first[p]:
                c.start()
        for p in range(3):
            for c in second[p]:
                c.start()
        for p in range(3):
            axis = ORDERS[p][step]
            me = here[axis]
            up, down = lax.rem(me + 1, 4), lax.rem(me + 3, 4)
            first[p][0].wait_recv()
            part[region(p, up, 0)] += agg[p, 0]
            last[p][0].start()
            first[p][1].wait_recv()
            part[region(p, down, 1)] += agg[p, 1]
            last[p][1].start()
        for p in range(3):
            axis = ORDERS[p][step]
            for c in second[p] + last[p]:
                c.wait_recv()
            part[region(p, here[axis])] += full[p, 0] + full[p, 1]
        for c in smalls:
            c.wait_recv()
            c.wait_send()
        for p in range(3):
            started += first[p] + second[p] + last[p]
        total_now = (slots_a[step, 0] + slots_a[step, 1]) + (slots_a[step, 2] + slots_a[step, 3])
        if step < 2:
            total[...] = total_now
        else:
            small_out[...] = total_now

    mine = part[zi, yi, xi]
    out_ref[xi] = mine
    spread = []
    for d in (1, 2, 3):
        c = remote(out_ref.at[xi], out_ref.at[xi], x_send.at[d - 1], x_recv.at[d - 1],
                   {"dp": lax.rem(xi + d, 4)})
        c.start()
        spread.append(c)
    for d in (1, 2, 3):
        came = lax.rem(xi + 4 - d, 4)
        remote(out_ref.at[came], out_ref.at[came], x_send.at[d - 1], x_recv.at[d - 1],
               {"dp": came}).wait_recv()
    for c in spread + copies + started:
        c.wait_send()


def reduce_weight(nt, og, small):
    rows = nt.shape[2]
    cols = og.shape[1]
    quarter = rows // 4
    third, half = cols // 3, cols // 6
    vmem = pl.BlockSpec(memory_space=pltpu.VMEM)
    f32 = jnp.float32
    out, sums = pl.pallas_call(
        reduce_kernel,
        out_shape=(jax.ShapeDtypeStruct((4, quarter, cols), f32), jax.ShapeDtypeStruct(small.shape, f32)),
        in_specs=[vmem] * 3,
        out_specs=(vmem, vmem),
        scratch_shapes=[
            pltpu.VMEM((4, 4, 4, quarter, cols), f32),
            pltpu.VMEM((16, rows, nt.shape[3]), f32),
            pltpu.VMEM(og.shape, f32),
            pltpu.VMEM((3, 2, 4, 4, quarter, half), f32),
            pltpu.VMEM((3, 2, 4, 4, quarter, third), f32),
            pltpu.VMEM((3, 2, 4, quarter, half), f32),
            pltpu.VMEM((3, 2, 4, quarter, third), f32),
            pltpu.VMEM((3, 2, quarter, half), f32),
            pltpu.VMEM((3, 2, quarter, third), f32),
            pltpu.VMEM((2, *small.shape), f32),
            pltpu.VMEM((3, 4, *small.shape), f32),
            pltpu.VMEM(small.shape, f32),
            pltpu.SemaphoreType.DMA((3,)),
            pltpu.SemaphoreType.DMA((3,)),
            pltpu.SemaphoreType.DMA((3, 3, 6)),
            pltpu.SemaphoreType.DMA((3, 3, 6)),
            pltpu.SemaphoreType.DMA((3,)),
            pltpu.SemaphoreType.DMA((3,)),
            pltpu.SemaphoreType.DMA((3, 3)),
            pltpu.SemaphoreType.DMA((3, 3)),
        ],
        compiler_params=pltpu.CompilerParams(
            collective_id=3, has_side_effects=True, vmem_limit_bytes=VMEM_LIMIT),
        name="reduce_weight",
    )(nt, og, small)
    return out.reshape(rows, cols), sums


def per_device(scan, reduce_all, ssm_input, gate_input, input_map, output_map, step_logit, step_bias,
               decay_rate, skip_gain, norm_gain, out_weight, resets, out_grad):
    f32, bf16 = jnp.float32, jnp.bfloat16
    x, z, bmap, cmap, og = ssm_input[0], gate_input[0], input_map[0], output_map[0], out_grad[0]
    rows, width = x.shape
    heads = step_bias.shape[0]
    per_head = width // heads

    start = lax.axis_index("seq") * rows
    ri = lax.broadcasted_iota(jnp.int32, (rows, rows), 0)
    ci = lax.broadcasted_iota(jnp.int32, (rows, rows), 1)
    below = ri >= ci
    tri = below.astype(f32)
    at_col = start + lax.broadcasted_iota(jnp.int32, (rows, 1), 0)
    at_row = start + lax.broadcasted_iota(jnp.int32, (1, rows), 1)
    flag_col = jnp.zeros((rows, 1), jnp.bool_)
    flag_row = jnp.zeros((1, rows), jnp.bool_)
    for k in range(resets.shape[1]):
        flag_col |= at_col == resets[0, k]
        flag_row |= at_row == resets[0, k]
    count_col = jnp.sum(jnp.where(below & flag_row, 1.0, 0.0), axis=1, keepdims=True)
    count_row = jnp.sum(jnp.where((ri <= ci) & flag_col, 1.0, 0.0), axis=0, keepdims=True)
    count_all = jnp.sum(flag_row.astype(f32))
    mask = below & (count_col == count_row)
    opened = count_col == 0
    keep = count_col == count_all

    spread = (
        lax.broadcasted_iota(jnp.int32, (heads, width), 0)
        == lax.broadcasted_iota(jnp.int32, (heads, width), 1) // per_head
    ).astype(f32)
    gather = spread.T

    raw = step_logit[0].astype(f32) + step_bias
    step = jax.nn.softplus(raw)
    cum = exact(tri, -decay_rate * step)
    last = cum[rows - 1 :]
    mid = cum[rows // 2 : rows // 2 + 1]
    through = jnp.where(count_all == 0, jnp.exp(last), 0.0)
    e_head = jnp.exp(cum - mid)
    f_head = step * jnp.exp(mid - cum)
    wide = exact(
        jnp.concatenate([e_head, f_head, jnp.exp(last - mid), jnp.exp(mid), skip_gain[None], through], axis=0),
        spread,
    )
    e, f = wide[:rows], wide[rows : 2 * rows]
    tail, lead, skip, through_wide = (wide[2 * rows + k : 2 * rows + k + 1] for k in range(4))

    xf = x.astype(f32)
    fx_f = f * xf
    fx2 = split(fx_f)
    fx = fx2[0]
    gm2 = split(jnp.where(mask, bdot(cmap, bmap, 1, 1), 0.0))
    gm = gm2[0]
    b_keep = jnp.where(keep, bmap, jnp.zeros_like(bmap))
    c_open = jnp.where(opened, cmap, jnp.zeros_like(cmap))
    s_own = dot2(b_keep, fx2, 0, 0)
    thr = jnp.zeros((8, 128), f32).at[:, :heads].set(jnp.broadcast_to(through, (8, heads)))
    spread_pad = jnp.zeros((128, width), f32).at[:heads].set(spread)
    incoming = scan(tail * s_own, thr, spread_pad, False)
    s_in2 = split(lead * incoming)
    s_in = s_in2[0]

    u = dot2(gm2, fx2, 1, 0) + dot2(c_open, s_in2, 1, 0)
    y = e * u + skip * xf
    zf = z.astype(f32)
    sig = jax.nn.sigmoid(zf)
    silu = zf * sig
    g = y * silu
    r = lax.rsqrt(jnp.mean(g * g, axis=1, keepdims=True) + 1e-05)
    ghat = g * r
    normed = (ghat * norm_gain).astype(bf16)
    mixed = bdot(normed, out_weight, 1, 0).astype(bf16)
    dn = bdot(og, out_weight, 1, 1)
    gain_grad = jnp.sum(dn * ghat, axis=0)
    q = dn * norm_gain
    dg = r * (q - ghat * jnp.mean(q * ghat, axis=1, keepdims=True))
    dy = dg * silu
    dz = (dg * y * (sig * (1.0 + zf * (1.0 - sig)))).astype(bf16)
    du_f = e * dy
    du2 = split(du_f)
    du = du2[0]
    later = scan(lead * dot2(c_open, du2, 0, 0), thr, spread_pad, True)
    ds_f = tail * later
    ds2 = split(ds_f)
    ds = ds2[0]

    dfx = dot2(gm2, du2, 0, 0) + dot2(b_keep, ds2, 1, 0)
    dx = (f * dfx + skip * dy).astype(bf16)
    dgm2 = split(jnp.where(mask, bdot(du, fx, 1, 1), 0.0))
    dc = dot2(dgm2, bmap, 1, 0) + jnp.where(opened, bdot(du, s_in, 1, 1), 0.0)
    db = dot2(dgm2, cmap, 0, 0) + jnp.where(keep, bdot(fx, ds, 1, 1), 0.0)
    skip_row = jnp.sum(dy * xf, axis=0, keepdims=True)
    end_row = jnp.sum(ds_f * s_own + through_wide * later * incoming, axis=0, keepdims=True)
    a_wide = fx_f * dfx
    per = exact(jnp.concatenate([a_wide, du_f * u - a_wide, skip_row, end_row], axis=0), gather)
    a, ba = per[:rows], per[rows : 2 * rows]
    skip_grad, end = per[2 * rows], per[2 * rows + 1 :]
    d_decay = exact((ri <= ci).astype(f32), ba) + end
    dlogit = (a / step - decay_rate * d_decay) * jax.nn.sigmoid(raw)
    bias_grad = jnp.sum(dlogit, axis=0)
    rate_grad = jnp.sum(-step * d_decay, axis=0)

    small = jnp.concatenate([gain_grad, bias_grad, rate_grad, skip_grad])
    size = small.shape[0]
    lines = -(-size // 1024) * 8
    small = jnp.pad(small, (0, lines * 128 - size)).reshape(lines, 128)
    weight_grad, sums = reduce_all(normed, og, small)
    sums = sums.reshape(-1)
    gain_sum = sums[:width]
    bias_sum, rate_sum, skip_sum = (sums[width + k * heads : width + (k + 1) * heads] for k in range(3))
    return (
        mixed[None],
        dx[None],
        dz[None],
        dc_cast(db)[None],
        dc_cast(dc)[None],
        dc_cast(dlogit)[None],
        bias_sum,
        rate_sum,
        skip_sum,
        gain_sum,
        weight_grad,
    )


def dc_cast(values):
    return values.astype(jnp.bfloat16)


def solution(mesh):
    n = mesh.shape["seq"]

    def scan(state, thr, spread, reverse):
        return state_scan(n, state, thr, spread, reverse)

    def reduce_all(normed, og, small):
        rows, width = normed.shape
        nt = normed.T.astype(jnp.float32).reshape(16, 2, width // 32, rows)
        return reduce_weight(nt, og.astype(jnp.float32), small)

    by_rows = P("dp", "seq", None)
    return jax.shard_map(
        functools.partial(per_device, scan, reduce_all),
        mesh=mesh,
        in_specs=(by_rows,) * 5 + (P(),) * 5 + (P("dp", None), by_rows),
        out_specs=(by_rows,) * 6 + (P(),) * 4 + (P("seq", None),),
        check_vma=False,
    )
```

```python
import functools

import jax
import jax.numpy as jnp
from jax import lax
from jax.experimental import pallas as pl
from jax.experimental.pallas import tpu as pltpu
from jax.sharding import PartitionSpec as P

MESH = pl.DeviceIdType.MESH
HIGHEST = lax.Precision.HIGHEST
VMEM_LIMIT = 60 * 1024 * 1024


def bdot(a, b, ca, cb):
    return lax.dot_general(
        a, b, (((ca,), (cb,)), ((), ())), preferred_element_type=jnp.float32
    )


def split(v):
    hi = v.astype(jnp.bfloat16)
    return hi, (v - hi.astype(jnp.float32)).astype(jnp.bfloat16)


def dot2(a, b, ca, cb):
    if isinstance(a, tuple) and isinstance(b, tuple):
        return bdot(a[0], b[0], ca, cb) + (bdot(a[0], b[1], ca, cb) + bdot(a[1], b[0], ca, cb))
    if isinstance(a, tuple):
        return bdot(a[0], b, ca, cb) + bdot(a[1], b, ca, cb)
    if isinstance(b, tuple):
        return bdot(a, b[0], ca, cb) + bdot(a, b[1], ca, cb)
    return bdot(a, b, ca, cb)


def exact(a, b):
    return jnp.dot(a, b, precision=HIGHEST, preferred_element_type=jnp.float32)


class Scan:
    def __init__(self, n, reverse, s_ref, thr_ref, spread_ref, out_ref, pair, mine, recv, stage, back, give,
                 thr_pair, thr_own, thr_buf, thr_wide, first_wide, sems):
        me = lax.axis_index("seq")
        self.chips, self.reverse = n // 2, reverse
        self.core, self.chip = lax.rem(me, 2), lax.div(me, 2)
        self.s_ref, self.thr_ref, self.spread_ref, self.out_ref = s_ref, thr_ref, spread_ref, out_ref
        self.pair, self.mine, self.recv, self.stage, self.back, self.give = pair, mine, recv, stage, back, give
        self.thr_pair, self.thr_own, self.thr_buf = thr_pair, thr_own, thr_buf
        self.thr_wide, self.first_wide = thr_wide, first_wide
        (self.ps, self.pr, self.ss, self.sr, self.ts, self.tr, self.bs, self.br, self.gs, self.gr, self.qs, self.qr) = sems
        ns, width = s_ref.shape
        self.rows, self.half = ns // self.chips, width // 2

    def lanes(self, core):
        return pl.ds(pl.multiple_of(core * self.half, 128), self.half)

    def band(self, k):
        return pl.ds(pl.multiple_of(k * self.rows, 8), self.rows)

    def copy(self, src, dst, ss, rs, to):
        return pltpu.make_async_remote_copy(src_ref=src, dst_ref=dst, send_sem=ss, recv_sem=rs,
                                            device_id={"seq": to}, device_id_type=MESH)

    def sibling(self):
        return self.chip * 2 + 1 - self.core

    def peer(self, k):
        return k * 2 + self.core

    def greet(self, barrier):
        pl.semaphore_signal(barrier, inc=1, device_id={"seq": self.sibling()}, device_id_type=MESH)

        def one(i, _):
            k = lax.rem(self.chip + 1 + i, self.chips)
            pl.semaphore_signal(barrier, inc=1, device_id={"seq": self.peer(k)}, device_id_type=MESH)
            return 0

        lax.fori_loop(0, self.chips - 1, one, 0)
        return self.chips

    def pair_copy(self, k):
        return self.copy(self.s_ref.at[self.band(k), self.lanes(1 - self.core)], self.pair.at[k],
                         self.ps.at[k], self.pr.at[k], self.sibling())

    def thr_pair_copy(self):
        return self.copy(self.thr_ref, self.thr_pair, self.qs, self.qr, self.sibling())

    def thr_copy(self, k, slot):
        return self.copy(self.thr_own, self.thr_buf.at[slot], self.ts.at[k], self.tr.at[slot], self.peer(k))

    def chunk_copy(self, k, slot):
        return self.copy(self.mine.at[k], self.recv.at[slot], self.ss.at[k], self.sr.at[slot], self.peer(k))

    def back_copy(self, k, slot):
        return self.copy(self.stage.at[k], self.back.at[slot], self.bs.at[k], self.br.at[slot], self.peer(k))

    def give_copy(self, k, core):
        return self.copy(self.give.at[k], self.out_ref.at[self.band(k), self.lanes(core)], self.gs.at[k], self.gr.at[k],
                         self.sibling())

    def begin(self):
        self.thr_pair_copy().start()

        def one(i, _):
            self.pair_copy(lax.rem(self.chip + 1 + i, self.chips)).start()
            return 0

        lax.fori_loop(0, self.chips, one, 0)

    def exchange(self):
        first = 1 if self.reverse else 0
        self.thr_pair_copy().wait_recv()
        mine_first = self.core == first
        thr_first = jnp.where(mine_first, self.thr_ref[...], self.thr_pair[...])
        thr_second = jnp.where(mine_first, self.thr_pair[...], self.thr_ref[...])
        self.thr_own[...] = thr_first * thr_second
        self.thr_buf[self.chip] = thr_first * thr_second

        def tell(i, _):
            self.thr_copy(lax.rem(self.chip + 1 + i, self.chips), self.chip).start()
            return 0

        lax.fori_loop(0, self.chips - 1, tell, 0)
        both = jnp.concatenate([thr_first, thr_second], axis=0)
        wide = jnp.dot(both, self.spread_ref[:, self.lanes(self.core)], precision=HIGHEST,
                       preferred_element_type=jnp.float32)
        self.first_wide[...] = wide[0:8]
        second_wide = wide[8:16]

        def one(i, _):
            k = lax.rem(self.chip + 1 + i, self.chips)
            self.pair_copy(k).wait_recv()
            own = self.s_ref[self.band(k), self.lanes(self.core)]
            other = self.pair[k]
            early = jnp.where(mine_first, own, other)
            late = jnp.where(mine_first, other, own)
            self.mine[k] = second_wide * early + late

            @pl.when(k != self.chip)
            def _():
                self.chunk_copy(k, self.chip).start()

            return 0

        lax.fori_loop(0, self.chips, one, 0)
        self.recv[self.chip] = self.mine[self.chip]

    def hops(self):
        def arrive(i, _):
            self.thr_copy(self.chip, lax.rem(self.chip + 1 + i, self.chips)).wait_recv()
            return 0

        lax.fori_loop(0, self.chips - 1, arrive, 0)
        self.thr_wide[...] = jnp.dot(self.thr_buf[:, 0, :], self.spread_ref[:, self.lanes(self.core)],
                                     precision=HIGHEST, preferred_element_type=jnp.float32)

        def hop(i, state):
            j = self.chips - 1 - i if self.reverse else i

            @pl.when(j != self.chip)
            def _():
                self.chunk_copy(self.chip, j).wait_recv()

            self.stage[j] = state

            @pl.when(j != self.chip)
            def _():
                self.back_copy(j, self.chip).start()

            return self.thr_wide[pl.ds(j, 1), :] * state + self.recv[j]

        lax.fori_loop(0, self.chips, hop, jnp.zeros((self.rows, self.half), jnp.float32))
        self.back[self.chip] = self.stage[self.chip]

    def deliver(self):
        mine_first = self.core == (1 if self.reverse else 0)

        def one(i, _):
            k = lax.rem(self.chip + i, self.chips)

            @pl.when(k != self.chip)
            def _():
                self.back_copy(self.chip, k).wait_recv()

            early = self.back[k]
            own = self.s_ref[self.band(k), self.lanes(self.core)]
            late = self.first_wide[...] * early + jnp.where(mine_first, own, self.pair[k])
            self.out_ref[self.band(k), self.lanes(self.core)] = jnp.where(mine_first, early, late)
            self.give[k] = jnp.where(mine_first, late, early)
            self.give_copy(k, self.core).start()
            return 0

        lax.fori_loop(0, self.chips, one, 0)

        def got(k, _):
            self.give_copy(k, 1 - self.core).wait_recv()
            return 0

        lax.fori_loop(0, self.chips, got, 0)

    def finish(self):
        self.thr_pair_copy().wait_send()

        def one(i, _):
            k = lax.rem(self.chip + 1 + i, self.chips)
            self.pair_copy(k).wait_send()
            self.give_copy(k, self.core).wait_send()

            @pl.when(k != self.chip)
            def _():
                self.thr_copy(k, self.chip).wait_send()
                self.chunk_copy(k, self.chip).wait_send()
                self.back_copy(k, self.chip).wait_send()

            return 0

        lax.fori_loop(0, self.chips, one, 0)


def scan_scratch(n, ns, width):
    chips = n // 2
    chunk = pltpu.VMEM((chips, ns // chips, width // 2), jnp.float32)
    tile = pltpu.VMEM((8, 128), jnp.float32)
    return [chunk] * 6 + [
        tile,
        tile,
        pltpu.VMEM((chips, 8, 128), jnp.float32),
        pltpu.VMEM((chips, width // 2), jnp.float32),
        pltpu.VMEM((8, width // 2), jnp.float32),
    ] + [pltpu.SemaphoreType.DMA((chips,))] * 10 + [pltpu.SemaphoreType.DMA] * 2


SCAN_SCRATCH = 11 + 12


def make_scan(n, reverse, s_ref, thr_ref, spread_ref, out_ref, scratch):
    return Scan(n, reverse, s_ref, thr_ref, spread_ref, out_ref, *scratch[:11], scratch[11:])


def scan_kernel(n, reverse, s_ref, thr_ref, spread_ref, out_ref, *scratch):
    scan = make_scan(n, reverse, s_ref, thr_ref, spread_ref, out_ref, scratch)
    barrier = pltpu.get_barrier_semaphore()
    pl.semaphore_wait(barrier, scan.greet(barrier))
    scan.begin()
    scan.exchange()
    scan.hops()
    scan.deliver()
    scan.finish()


def state_scan(n, state, thr, spread, reverse):
    ns, width = state.shape
    vmem = pl.BlockSpec(memory_space=pltpu.VMEM)
    return pl.pallas_call(
        functools.partial(scan_kernel, n, reverse),
        out_shape=jax.ShapeDtypeStruct((ns, width), jnp.float32),
        in_specs=[vmem] * 3,
        out_specs=vmem,
        scratch_shapes=scan_scratch(n, ns, width),
        compiler_params=pltpu.CompilerParams(
            collective_id=2 if reverse else 1, has_side_effects=True,
            vmem_limit_bytes=VMEM_LIMIT),
        name="scan_back" if reverse else "scan_ahead",
    )(state, thr, spread)


ORDERS = ((2, 1, 0), (1, 0, 2), (0, 2, 1))


def reduce_kernel(nt_ref, og_ref, small_ref, out_ref, small_out, part, nt_got, og_got,
                  agg1, full1, agg2, full2, agg3, full3, slots_c, slots_a, total,
                  c_send, c_recv, r_send, r_recv, x_send, x_recv, m_send, m_recv):
    xi = lax.axis_index("dp")
    s = lax.axis_index("seq")
    zi, yi, core = lax.div(s, 8), lax.rem(lax.div(s, 2), 4), lax.rem(s, 2)
    here = (zi, yi, xi)
    cols = part.shape[-1]
    third = cols // 3
    half = third // 2

    def at(axis, index):
        if axis == 2:
            return {"dp": index}
        z, y = (index, yi) if axis == 0 else (zi, index)
        return {"seq": (z * 4 + y) * 2 + core}

    sibling = {"seq": s + 1 - 2 * core}
    barrier = pltpu.get_barrier_semaphore()
    pl.semaphore_signal(barrier, inc=1, device_id=sibling, device_id_type=MESH)
    for axis in range(3):
        for d in range(1, 4):
            pl.semaphore_signal(barrier, inc=1, device_id=at(axis, lax.rem(here[axis] + d, 4)),
                                device_id_type=MESH)
    pl.semaphore_wait(barrier, 10)

    def remote(src, dst, ss, rs, to):
        return pltpu.make_async_remote_copy(src_ref=src, dst_ref=dst, send_sem=ss, recv_sem=rs,
                                            device_id=to, device_id_type=MESH)

    started = []

    copies = [
        remote(og_ref, og_got, c_send.at[0], c_recv.at[0], sibling),
        remote(nt_ref.at[:, 1 - core], nt_got, c_send.at[1], c_recv.at[1], sibling),
        remote(small_ref, slots_c.at[core], c_send.at[2], c_recv.at[2], sibling),
    ]
    for c in copies:
        c.start()
    slots_c[core] = small_ref[...]
    og = og_ref[...].astype(jnp.bfloat16)

    def own(b, _):
        z, y = lax.div(b, 4), lax.rem(b, 4)
        lhs = nt_ref[b, core].astype(jnp.bfloat16)
        part[z, y] = bdot(lhs, og, 1, 0).reshape(part.shape[2:])
        return 0

    lax.fori_loop(0, 16, own, 0)
    for c in copies:
        c.wait_recv()
    og2 = og_got[...].astype(jnp.bfloat16)

    def theirs(b, _):
        z, y = lax.div(b, 4), lax.rem(b, 4)
        lhs = nt_got[b].astype(jnp.bfloat16)
        part[z, y] += bdot(lhs, og2, 1, 0).reshape(part.shape[2:])
        return 0

    lax.fori_loop(0, 16, theirs, 0)
    total[...] = slots_c[0] + slots_c[1]

    bufs = ((agg1, full1), (agg2, full2), (agg3, full3))
    small_axes = (2, 1, 0)
    for step in range(3):
        agg, full = bufs[step]

        def small_copy(d):
            axis = small_axes[step]
            return remote(total, slots_a.at[step, here[axis]], m_send.at[step, d - 1],
                          m_recv.at[step, d - 1], at(axis, lax.rem(here[axis] + d, 4)))

        smalls = [small_copy(d) for d in (1, 2, 3)]
        for c in smalls:
            c.start()
        slots_a[step, here[small_axes[step]]] = total[...]

        def region(p, t, h=None):
            order = ORDERS[p]
            index = [slice(None)] * 3
            for done in order[:step]:
                index[done] = here[done]
            index[order[step]] = t
            lo = p * third + (0 if h in (None, 0) else half)
            return (*index, slice(None), pl.ds(lo, third if h is None else half))

        def sem(p, k):
            return r_send.at[step, p, k], r_recv.at[step, p, k]

        first, second, last = [], [], []
        for p in range(3):
            axis = ORDERS[p][step]
            me = here[axis]
            up, down, far = lax.rem(me + 1, 4), lax.rem(me + 3, 4), lax.rem(me + 2, 4)
            a = [
                remote(part.at[region(p, far, 0)], agg.at[p, 0], *sem(p, 0), at(axis, up)),
                remote(part.at[region(p, far, 1)], agg.at[p, 1], *sem(p, 1), at(axis, down)),
            ]
            b = [
                remote(part.at[region(p, up, 1)], full.at[p, 0, ..., pl.ds(half, half)], *sem(p, 2), at(axis, up)),
                remote(part.at[region(p, down, 0)], full.at[p, 1, ..., pl.ds(0, half)], *sem(p, 3), at(axis, down)),
            ]
            c = [
                remote(part.at[region(p, up, 0)], full.at[p, 0, ..., pl.ds(0, half)], *sem(p, 4), at(axis, up)),
                remote(part.at[region(p, down, 1)], full.at[p, 1, ..., pl.ds(half, half)], *sem(p, 5), at(axis, down)),
            ]
            first.append(a)
            second.append(b)
            last.append(c)
        for p in range(3):
            for c in first[p]:
                c.start()
        for p in range(3):
            for c in second[p]:
                c.start()
        for p in range(3):
            axis = ORDERS[p][step]
            me = here[axis]
            up, down = lax.rem(me + 1, 4), lax.rem(me + 3, 4)
            first[p][0].wait_recv()
            part[region(p, up, 0)] += agg[p, 0]
            last[p][0].start()
            first[p][1].wait_recv()
            part[region(p, down, 1)] += agg[p, 1]
            last[p][1].start()
        for p in range(3):
            axis = ORDERS[p][step]
            for c in second[p] + last[p]:
                c.wait_recv()
            part[region(p, here[axis])] += full[p, 0] + full[p, 1]
        for c in smalls:
            c.wait_recv()
            c.wait_send()
        for p in range(3):
            started += first[p] + second[p] + last[p]
        total_now = (slots_a[step, 0] + slots_a[step, 1]) + (slots_a[step, 2] + slots_a[step, 3])
        if step < 2:
            total[...] = total_now
        else:
            small_out[...] = total_now

    mine = part[zi, yi, xi]
    out_ref[xi] = mine
    spread = []
    for d in (1, 2, 3):
        c = remote(out_ref.at[xi], out_ref.at[xi], x_send.at[d - 1], x_recv.at[d - 1],
                   {"dp": lax.rem(xi + d, 4)})
        c.start()
        spread.append(c)
    for d in (1, 2, 3):
        came = lax.rem(xi + 4 - d, 4)
        remote(out_ref.at[came], out_ref.at[came], x_send.at[d - 1], x_recv.at[d - 1],
               {"dp": came}).wait_recv()
    for c in spread + copies + started:
        c.wait_send()


def reduce_weight(nt, og, small):
    rows = nt.shape[2]
    cols = og.shape[1]
    quarter = rows // 4
    third, half = cols // 3, cols // 6
    vmem = pl.BlockSpec(memory_space=pltpu.VMEM)
    f32 = jnp.float32
    out, sums = pl.pallas_call(
        reduce_kernel,
        out_shape=(jax.ShapeDtypeStruct((4, quarter, cols), f32), jax.ShapeDtypeStruct(small.shape, f32)),
        in_specs=[vmem] * 3,
        out_specs=(vmem, vmem),
        scratch_shapes=[
            pltpu.VMEM((4, 4, 4, quarter, cols), f32),
            pltpu.VMEM((16, rows, nt.shape[3]), f32),
            pltpu.VMEM(og.shape, f32),
            pltpu.VMEM((3, 2, 4, 4, quarter, half), f32),
            pltpu.VMEM((3, 2, 4, 4, quarter, third), f32),
            pltpu.VMEM((3, 2, 4, quarter, half), f32),
            pltpu.VMEM((3, 2, 4, quarter, third), f32),
            pltpu.VMEM((3, 2, quarter, half), f32),
            pltpu.VMEM((3, 2, quarter, third), f32),
            pltpu.VMEM((2, *small.shape), f32),
            pltpu.VMEM((3, 4, *small.shape), f32),
            pltpu.VMEM(small.shape, f32),
            pltpu.SemaphoreType.DMA((3,)),
            pltpu.SemaphoreType.DMA((3,)),
            pltpu.SemaphoreType.DMA((3, 3, 6)),
            pltpu.SemaphoreType.DMA((3, 3, 6)),
            pltpu.SemaphoreType.DMA((3,)),
            pltpu.SemaphoreType.DMA((3,)),
            pltpu.SemaphoreType.DMA((3, 3)),
            pltpu.SemaphoreType.DMA((3, 3)),
        ],
        compiler_params=pltpu.CompilerParams(
            collective_id=3, has_side_effects=True, vmem_limit_bytes=VMEM_LIMIT),
        name="reduce_weight",
    )(nt, og, small)
    return out.reshape(rows, cols), sums


def per_device(scan, reduce_all, ssm_input, gate_input, input_map, output_map, step_logit, step_bias,
               decay_rate, skip_gain, norm_gain, out_weight, resets, out_grad):
    f32, bf16 = jnp.float32, jnp.bfloat16
    x, z, bmap, cmap, og = ssm_input[0], gate_input[0], input_map[0], output_map[0], out_grad[0]
    rows, width = x.shape
    heads = step_bias.shape[0]
    per_head = width // heads

    start = lax.axis_index("seq") * rows
    ri = lax.broadcasted_iota(jnp.int32, (rows, rows), 0)
    ci = lax.broadcasted_iota(jnp.int32, (rows, rows), 1)
    below = ri >= ci
    tri = below.astype(f32)
    at_col = start + lax.broadcasted_iota(jnp.int32, (rows, 1), 0)
    at_row = start + lax.broadcasted_iota(jnp.int32, (1, rows), 1)
    flag_col = jnp.zeros((rows, 1), jnp.bool_)
    flag_row = jnp.zeros((1, rows), jnp.bool_)
    for k in range(resets.shape[1]):
        flag_col |= at_col == resets[0, k]
        flag_row |= at_row == resets[0, k]
    count_col = jnp.sum(jnp.where(below & flag_row, 1.0, 0.0), axis=1, keepdims=True)
    count_row = jnp.sum(jnp.where((ri <= ci) & flag_col, 1.0, 0.0), axis=0, keepdims=True)
    count_all = jnp.sum(flag_row.astype(f32))
    mask = below & (count_col == count_row)
    opened = count_col == 0
    keep = count_col == count_all

    spread = (
        lax.broadcasted_iota(jnp.int32, (heads, width), 0)
        == lax.broadcasted_iota(jnp.int32, (heads, width), 1) // per_head
    ).astype(f32)
    gather = spread.T

    raw = step_logit[0].astype(f32) + step_bias
    step = jax.nn.softplus(raw)
    cum = exact(tri, -decay_rate * step)
    last = cum[rows - 1 :]
    mid = cum[rows // 2 : rows // 2 + 1]
    through = jnp.where(count_all == 0, jnp.exp(last), 0.0)
    e_head = jnp.exp(cum - mid)
    f_head = step * jnp.exp(mid - cum)
    wide = exact(
        jnp.concatenate([e_head, f_head, jnp.exp(last - mid), jnp.exp(mid), skip_gain[None], through], axis=0),
        spread,
    )
    e, f = wide[:rows], wide[rows : 2 * rows]
    tail, lead, skip, through_wide = (wide[2 * rows + k : 2 * rows + k + 1] for k in range(4))

    xf = x.astype(f32)
    fx_f = f * xf
    fx2 = split(fx_f)
    fx = fx2[0]
    gm2 = split(jnp.where(mask, bdot(cmap, bmap, 1, 1), 0.0))
    gm = gm2[0]
    b_keep = jnp.where(keep, bmap, jnp.zeros_like(bmap))
    c_open = jnp.where(opened, cmap, jnp.zeros_like(cmap))
    s_own = dot2(b_keep, fx2, 0, 0)
    thr = jnp.zeros((8, 128), f32).at[:, :heads].set(jnp.broadcast_to(through, (8, heads)))
    spread_pad = jnp.zeros((128, width), f32).at[:heads].set(spread)
    incoming = scan(tail * s_own, thr, spread_pad, False)
    s_in2 = split(lead * incoming)
    s_in = s_in2[0]

    u = dot2(gm2, fx2, 1, 0) + dot2(c_open, s_in2, 1, 0)
    y = e * u + skip * xf
    zf = z.astype(f32)
    sig = jax.nn.sigmoid(zf)
    silu = zf * sig
    g = y * silu
    r = lax.rsqrt(jnp.mean(g * g, axis=1, keepdims=True) + 1e-05)
    ghat = g * r
    normed = (ghat * norm_gain).astype(bf16)
    mixed = bdot(normed, out_weight, 1, 0).astype(bf16)
    dn = bdot(og, out_weight, 1, 1)
    gain_grad = jnp.sum(dn * ghat, axis=0)
    q = dn * norm_gain
    dg = r * (q - ghat * jnp.mean(q * ghat, axis=1, keepdims=True))
    dy = dg * silu
    dz = (dg * y * (sig * (1.0 + zf * (1.0 - sig)))).astype(bf16)
    du_f = e * dy
    du2 = split(du_f)
    du = du2[0]
    later = scan(lead * dot2(c_open, du2, 0, 0), thr, spread_pad, True)
    ds_f = tail * later
    ds2 = split(ds_f)
    ds = ds2[0]

    dfx = dot2(gm2, du2, 0, 0) + dot2(b_keep, ds2, 1, 0)
    dx = (f * dfx + skip * dy).astype(bf16)
    dgm2 = split(jnp.where(mask, dot2(du2, fx, 1, 1), 0.0))
    dc = dot2(dgm2, bmap, 1, 0) + jnp.where(opened, dot2(du2, s_in, 1, 1), 0.0)
    db = dot2(dgm2, cmap, 0, 0) + jnp.where(keep, dot2(fx, ds2, 1, 1), 0.0)
    skip_row = jnp.sum(dy * xf, axis=0, keepdims=True)
    end_row = jnp.sum(ds_f * s_own + through_wide * later * incoming, axis=0, keepdims=True)
    a_wide = fx_f * dfx
    per = exact(jnp.concatenate([a_wide, du_f * u - a_wide, skip_row, end_row], axis=0), gather)
    a, ba = per[:rows], per[rows : 2 * rows]
    skip_grad, end = per[2 * rows], per[2 * rows + 1 :]
    d_decay = exact((ri <= ci).astype(f32), ba) + end
    dlogit = (a / step - decay_rate * d_decay) * jax.nn.sigmoid(raw)
    bias_grad = jnp.sum(dlogit, axis=0)
    rate_grad = jnp.sum(-step * d_decay, axis=0)

    small = jnp.concatenate([gain_grad, bias_grad, rate_grad, skip_grad])
    size = small.shape[0]
    lines = -(-size // 1024) * 8
    small = jnp.pad(small, (0, lines * 128 - size)).reshape(lines, 128)
    weight_grad, sums = reduce_all(normed, og, small)
    sums = sums.reshape(-1)
    gain_sum = sums[:width]
    bias_sum, rate_sum, skip_sum = (sums[width + k * heads : width + (k + 1) * heads] for k in range(3))
    return (
        mixed[None],
        dx[None],
        dz[None],
        dc_cast(db)[None],
        dc_cast(dc)[None],
        dc_cast(dlogit)[None],
        bias_sum,
        rate_sum,
        skip_sum,
        gain_sum,
        weight_grad,
    )


def dc_cast(values):
    return values.astype(jnp.bfloat16)


def solution(mesh):
    n = mesh.shape["seq"]

    def scan(state, thr, spread, reverse):
        return state_scan(n, state, thr, spread, reverse)

    def reduce_all(normed, og, small):
        rows, width = normed.shape
        nt = normed.T.astype(jnp.float32).reshape(16, 2, width // 32, rows)
        return reduce_weight(nt, og.astype(jnp.float32), small)

    by_rows = P("dp", "seq", None)
    return jax.shard_map(
        functools.partial(per_device, scan, reduce_all),
        mesh=mesh,
        in_specs=(by_rows,) * 5 + (P(),) * 5 + (P("dp", None), by_rows),
        out_specs=(by_rows,) * 6 + (P(),) * 4 + (P("seq", None),),
        check_vma=False,
    )
```

```python
import functools

import jax
import jax.numpy as jnp
from jax import lax
from jax.experimental import pallas as pl
from jax.experimental.pallas import tpu as pltpu
from jax.sharding import PartitionSpec as P

MESH = pl.DeviceIdType.MESH
HIGHEST = lax.Precision.HIGHEST
VMEM_LIMIT = 60 * 1024 * 1024


def bdot(a, b, ca, cb):
    return lax.dot_general(
        a, b, (((ca,), (cb,)), ((), ())), preferred_element_type=jnp.float32
    )


def split_wide(v):
    hi = lax.reduce_precision(v, exponent_bits=8, mantissa_bits=7)
    return hi.astype(jnp.bfloat16), (v - hi).astype(jnp.bfloat16)


def split(v):
    hi = v.astype(jnp.bfloat16)
    return hi, (v - hi.astype(jnp.float32)).astype(jnp.bfloat16)


def dot2(a, b, ca, cb):
    if isinstance(a, tuple) and isinstance(b, tuple):
        return bdot(a[0], b[0], ca, cb) + (bdot(a[0], b[1], ca, cb) + bdot(a[1], b[0], ca, cb))
    if isinstance(a, tuple):
        return bdot(a[0], b, ca, cb) + bdot(a[1], b, ca, cb)
    if isinstance(b, tuple):
        return bdot(a, b[0], ca, cb) + bdot(a, b[1], ca, cb)
    return bdot(a, b, ca, cb)


def exact(a, b):
    return jnp.dot(a, b, precision=HIGHEST, preferred_element_type=jnp.float32)


class Scan:
    def __init__(self, n, reverse, s_ref, thr_ref, spread_ref, out_ref, pair, mine, recv, stage, back, give,
                 thr_pair, thr_own, thr_buf, thr_wide, first_wide, sems):
        me = lax.axis_index("seq")
        self.chips, self.reverse = n // 2, reverse
        self.core, self.chip = lax.rem(me, 2), lax.div(me, 2)
        self.s_ref, self.thr_ref, self.spread_ref, self.out_ref = s_ref, thr_ref, spread_ref, out_ref
        self.pair, self.mine, self.recv, self.stage, self.back, self.give = pair, mine, recv, stage, back, give
        self.thr_pair, self.thr_own, self.thr_buf = thr_pair, thr_own, thr_buf
        self.thr_wide, self.first_wide = thr_wide, first_wide
        (self.ps, self.pr, self.ss, self.sr, self.ts, self.tr, self.bs, self.br, self.gs, self.gr, self.qs, self.qr) = sems
        ns, width = s_ref.shape
        self.rows, self.half = ns // self.chips, width // 2

    def lanes(self, core):
        return pl.ds(pl.multiple_of(core * self.half, 128), self.half)

    def band(self, k):
        return pl.ds(pl.multiple_of(k * self.rows, 8), self.rows)

    def copy(self, src, dst, ss, rs, to):
        return pltpu.make_async_remote_copy(src_ref=src, dst_ref=dst, send_sem=ss, recv_sem=rs,
                                            device_id={"seq": to}, device_id_type=MESH)

    def sibling(self):
        return self.chip * 2 + 1 - self.core

    def peer(self, k):
        return k * 2 + self.core

    def greet(self, barrier):
        pl.semaphore_signal(barrier, inc=1, device_id={"seq": self.sibling()}, device_id_type=MESH)

        def one(i, _):
            k = lax.rem(self.chip + 1 + i, self.chips)
            pl.semaphore_signal(barrier, inc=1, device_id={"seq": self.peer(k)}, device_id_type=MESH)
            return 0

        lax.fori_loop(0, self.chips - 1, one, 0)
        return self.chips

    def pair_copy(self, k):
        return self.copy(self.s_ref.at[self.band(k), self.lanes(1 - self.core)], self.pair.at[k],
                         self.ps.at[k], self.pr.at[k], self.sibling())

    def thr_pair_copy(self):
        return self.copy(self.thr_ref, self.thr_pair, self.qs, self.qr, self.sibling())

    def thr_copy(self, k, slot):
        return self.copy(self.thr_own, self.thr_buf.at[slot], self.ts.at[k], self.tr.at[slot], self.peer(k))

    def chunk_copy(self, k, slot):
        return self.copy(self.mine.at[k], self.recv.at[slot], self.ss.at[k], self.sr.at[slot], self.peer(k))

    def back_copy(self, k, slot):
        return self.copy(self.stage.at[k], self.back.at[slot], self.bs.at[k], self.br.at[slot], self.peer(k))

    def give_copy(self, k, core):
        return self.copy(self.give.at[k], self.out_ref.at[self.band(k), self.lanes(core)], self.gs.at[k], self.gr.at[k],
                         self.sibling())

    def begin(self):
        self.thr_pair_copy().start()

        def one(i, _):
            self.pair_copy(lax.rem(self.chip + 1 + i, self.chips)).start()
            return 0

        lax.fori_loop(0, self.chips, one, 0)

    def exchange(self):
        first = 1 if self.reverse else 0
        self.thr_pair_copy().wait_recv()
        mine_first = self.core == first
        thr_first = jnp.where(mine_first, self.thr_ref[...], self.thr_pair[...])
        thr_second = jnp.where(mine_first, self.thr_pair[...], self.thr_ref[...])
        self.thr_own[...] = thr_first * thr_second
        self.thr_buf[self.chip] = thr_first * thr_second

        def tell(i, _):
            self.thr_copy(lax.rem(self.chip + 1 + i, self.chips), self.chip).start()
            return 0

        lax.fori_loop(0, self.chips - 1, tell, 0)
        both = jnp.concatenate([thr_first, thr_second], axis=0)
        wide = jnp.dot(both, self.spread_ref[:, self.lanes(self.core)], precision=HIGHEST,
                       preferred_element_type=jnp.float32)
        self.first_wide[...] = wide[0:8]
        second_wide = wide[8:16]

        def one(i, _):
            k = lax.rem(self.chip + 1 + i, self.chips)
            self.pair_copy(k).wait_recv()
            own = self.s_ref[self.band(k), self.lanes(self.core)]
            other = self.pair[k]
            early = jnp.where(mine_first, own, other)
            late = jnp.where(mine_first, other, own)
            self.mine[k] = second_wide * early + late

            @pl.when(k != self.chip)
            def _():
                self.chunk_copy(k, self.chip).start()

            return 0

        lax.fori_loop(0, self.chips, one, 0)
        self.recv[self.chip] = self.mine[self.chip]

    def hops(self):
        def arrive(i, _):
            self.thr_copy(self.chip, lax.rem(self.chip + 1 + i, self.chips)).wait_recv()
            return 0

        lax.fori_loop(0, self.chips - 1, arrive, 0)
        self.thr_wide[...] = jnp.dot(self.thr_buf[:, 0, :], self.spread_ref[:, self.lanes(self.core)],
                                     precision=HIGHEST, preferred_element_type=jnp.float32)

        def hop(i, state):
            j = self.chips - 1 - i if self.reverse else i

            @pl.when(j != self.chip)
            def _():
                self.chunk_copy(self.chip, j).wait_recv()

            self.stage[j] = state

            @pl.when(j != self.chip)
            def _():
                self.back_copy(j, self.chip).start()

            return self.thr_wide[pl.ds(j, 1), :] * state + self.recv[j]

        lax.fori_loop(0, self.chips, hop, jnp.zeros((self.rows, self.half), jnp.float32))
        self.back[self.chip] = self.stage[self.chip]

    def deliver(self):
        mine_first = self.core == (1 if self.reverse else 0)

        def one(i, _):
            k = lax.rem(self.chip + i, self.chips)

            @pl.when(k != self.chip)
            def _():
                self.back_copy(self.chip, k).wait_recv()

            early = self.back[k]
            own = self.s_ref[self.band(k), self.lanes(self.core)]
            late = self.first_wide[...] * early + jnp.where(mine_first, own, self.pair[k])
            self.out_ref[self.band(k), self.lanes(self.core)] = jnp.where(mine_first, early, late)
            self.give[k] = jnp.where(mine_first, late, early)
            self.give_copy(k, self.core).start()
            return 0

        lax.fori_loop(0, self.chips, one, 0)

        def got(k, _):
            self.give_copy(k, 1 - self.core).wait_recv()
            return 0

        lax.fori_loop(0, self.chips, got, 0)

    def finish(self):
        self.thr_pair_copy().wait_send()

        def one(i, _):
            k = lax.rem(self.chip + 1 + i, self.chips)
            self.pair_copy(k).wait_send()
            self.give_copy(k, self.core).wait_send()

            @pl.when(k != self.chip)
            def _():
                self.thr_copy(k, self.chip).wait_send()
                self.chunk_copy(k, self.chip).wait_send()
                self.back_copy(k, self.chip).wait_send()

            return 0

        lax.fori_loop(0, self.chips, one, 0)


def scan_scratch(n, ns, width):
    chips = n // 2
    chunk = pltpu.VMEM((chips, ns // chips, width // 2), jnp.float32)
    tile = pltpu.VMEM((8, 128), jnp.float32)
    return [chunk] * 6 + [
        tile,
        tile,
        pltpu.VMEM((chips, 8, 128), jnp.float32),
        pltpu.VMEM((chips, width // 2), jnp.float32),
        pltpu.VMEM((8, width // 2), jnp.float32),
    ] + [pltpu.SemaphoreType.DMA((chips,))] * 10 + [pltpu.SemaphoreType.DMA] * 2


SCAN_SCRATCH = 11 + 12


def make_scan(n, reverse, s_ref, thr_ref, spread_ref, out_ref, scratch):
    return Scan(n, reverse, s_ref, thr_ref, spread_ref, out_ref, *scratch[:11], scratch[11:])


def scan_kernel(n, reverse, s_ref, thr_ref, spread_ref, out_ref, *scratch):
    scan = make_scan(n, reverse, s_ref, thr_ref, spread_ref, out_ref, scratch)
    barrier = pltpu.get_barrier_semaphore()
    pl.semaphore_wait(barrier, scan.greet(barrier))
    scan.begin()
    scan.exchange()
    scan.hops()
    scan.deliver()
    scan.finish()


def state_scan(n, state, thr, spread, reverse):
    ns, width = state.shape
    vmem = pl.BlockSpec(memory_space=pltpu.VMEM)
    return pl.pallas_call(
        functools.partial(scan_kernel, n, reverse),
        out_shape=jax.ShapeDtypeStruct((ns, width), jnp.float32),
        in_specs=[vmem] * 3,
        out_specs=vmem,
        scratch_shapes=scan_scratch(n, ns, width),
        compiler_params=pltpu.CompilerParams(
            collective_id=2 if reverse else 1, has_side_effects=True,
            vmem_limit_bytes=VMEM_LIMIT),
        name="scan_back" if reverse else "scan_ahead",
    )(state, thr, spread)


ORDERS = ((2, 1, 0), (1, 0, 2), (0, 2, 1))


class Ring:
    def __init__(self, nt_ref, og_ref, out_ref, small, small_out, part, nt_got, og_got, agg1, full1, agg2, full2,
                 agg3, full3, slots_c, slots_a, total, sems):
        (self.cs, self.cr, self.rs, self.rr, self.xs, self.xr, self.ms, self.mr) = sems
        self.xi = lax.axis_index("dp")
        s = lax.axis_index("seq")
        self.core = lax.rem(s, 2)
        self.here = (lax.div(s, 8), lax.rem(lax.div(s, 2), 4), self.xi)
        self.sibling = {"seq": s + 1 - 2 * self.core}
        self.nt_ref, self.og_ref, self.out_ref = nt_ref, og_ref, out_ref
        self.small, self.small_out = small, small_out
        self.part, self.nt_got, self.og_got = part, nt_got, og_got
        self.bufs = ((agg1, full1), (agg2, full2), (agg3, full3))
        self.slots_c, self.slots_a, self.total = slots_c, slots_a, total
        self.third = part.shape[-1] // 3
        self.half = self.third // 2
        self.started = []
        self.steps = {}

    def at(self, axis, index):
        if axis == 2:
            return {"dp": index}
        z, y = (index, self.here[1]) if axis == 0 else (self.here[0], index)
        return {"seq": (z * 4 + y) * 2 + self.core}

    def remote(self, src, dst, ss, rs, to):
        return pltpu.make_async_remote_copy(src_ref=src, dst_ref=dst, send_sem=ss, recv_sem=rs,
                                            device_id=to, device_id_type=MESH)

    def start(self, copies):
        for c in copies:
            c.start()
        self.started += copies
        return copies

    def pair_begin(self):
        self.pair = self.start([
            self.remote(self.og_ref, self.og_got, self.cs.at[0], self.cr.at[0], self.sibling),
            self.remote(self.nt_ref.at[:, 1 - self.core], self.nt_got, self.cs.at[1], self.cr.at[1], self.sibling),
        ])

    def own(self):
        og = self.og_ref[...].astype(jnp.bfloat16)

        def one(b, _):
            z, y = lax.div(b, 4), lax.rem(b, 4)
            lhs = self.nt_ref[b, self.core].astype(jnp.bfloat16)
            self.part[z, y] = bdot(lhs, og, 1, 0).reshape(self.part.shape[2:])
            return 0

        lax.fori_loop(0, 16, one, 0)

    def theirs(self):
        for c in self.pair:
            c.wait_recv()
        og = self.og_got[...].astype(jnp.bfloat16)

        def one(b, _):
            z, y = lax.div(b, 4), lax.rem(b, 4)
            lhs = self.nt_got[b].astype(jnp.bfloat16)
            self.part[z, y] += bdot(lhs, og, 1, 0).reshape(self.part.shape[2:])
            return 0

        lax.fori_loop(0, 16, one, 0)

    def region(self, step, p, t, h=None):
        order = ORDERS[p]
        index = [slice(None)] * 3
        for done in order[:step]:
            index[done] = self.here[done]
        index[order[step]] = t
        lo = p * self.third + (0 if h in (None, 0) else self.half)
        return (*index, slice(None), pl.ds(lo, self.third if h is None else self.half))

    def ways(self, step, p):
        axis = ORDERS[p][step]
        me = self.here[axis]
        return axis, lax.rem(me + 1, 4), lax.rem(me + 3, 4), lax.rem(me + 2, 4)

    def begin(self, step):
        agg, full = self.bufs[step]
        first, second, last = [], [], []
        lo, hi = pl.ds(0, self.half), pl.ds(self.half, self.half)
        for p in range(3):
            axis, up, down, far = self.ways(step, p)

            def go(t, h, dst, k, to):
                return self.remote(self.part.at[self.region(step, p, t, h)], dst, self.rs.at[step, p, k],
                                   self.rr.at[step, p, k], self.at(axis, to))

            first.append([go(far, 0, agg.at[p, 0], 0, up), go(far, 1, agg.at[p, 1], 1, down)])
            second.append([go(up, 1, full.at[p, 0, ..., hi], 2, up), go(down, 0, full.at[p, 1, ..., lo], 3, down)])
            last.append([go(up, 0, full.at[p, 0, ..., lo], 4, up), go(down, 1, full.at[p, 1, ..., hi], 5, down)])
        for p in range(3):
            self.start(first[p])
        for p in range(3):
            self.start(second[p])
        self.steps[step] = (first, second, last)

    def middle(self, step):
        agg, _ = self.bufs[step]
        first, _, last = self.steps[step]
        for p in range(3):
            _, up, down, _ = self.ways(step, p)
            first[p][0].wait_recv()
            self.part[self.region(step, p, up, 0)] += agg[p, 0]
            self.start([last[p][0]])
            first[p][1].wait_recv()
            self.part[self.region(step, p, down, 1)] += agg[p, 1]
            self.start([last[p][1]])

    def end(self, step):
        _, full = self.bufs[step]
        _, second, last = self.steps[step]
        for p in range(3):
            for c in second[p] + last[p]:
                c.wait_recv()
            here = self.region(step, p, self.here[ORDERS[p][step]])
            self.part[here] += full[p, 0] + full[p, 1]

    def small_pair_begin(self):
        self.small_pair = self.start([
            self.remote(self.small, self.slots_c.at[self.core], self.cs.at[2], self.cr.at[2], self.sibling)])
        self.slots_c[self.core] = self.small[...]

    def small_pair_end(self):
        self.small_pair[0].wait_recv()
        self.total[0] = self.slots_c[0] + self.slots_c[1]

    def small_begin(self, k):
        axis = (2, 1, 0)[k]
        me = self.here[axis]
        self.smalls = self.start([
            self.remote(self.total.at[k], self.slots_a.at[k, me], self.ms.at[k, d - 1], self.mr.at[k, d - 1],
                        self.at(axis, lax.rem(me + d, 4)))
            for d in (1, 2, 3)])
        self.slots_a[k, me] = self.total[k]

    def small_end(self, k):
        for c in self.smalls:
            c.wait_recv()
        now = (self.slots_a[k, 0] + self.slots_a[k, 1]) + (self.slots_a[k, 2] + self.slots_a[k, 3])
        if k < 2:
            self.total[k + 1] = now
        else:
            self.small_out[...] = now

    def share_begin(self):
        z, y, x = self.here
        self.out_ref[x] = self.part[z, y, x]
        self.start([
            self.remote(self.out_ref.at[x], self.out_ref.at[x], self.xs.at[d - 1], self.xr.at[d - 1],
                        {"dp": lax.rem(x + d, 4)})
            for d in (1, 2, 3)])

    def share_end(self):
        for d in (1, 2, 3):
            came = lax.rem(self.xi + 4 - d, 4)
            self.remote(self.out_ref.at[came], self.out_ref.at[came], self.xs.at[d - 1], self.xr.at[d - 1],
                        {"dp": came}).wait_recv()

    def finish(self):
        for c in self.started:
            c.wait_send()


def ring_scratch(rows, cols, span, lines):
    f32 = jnp.float32
    quarter, third, half = rows // 4, cols // 3, cols // 6
    return [
        pltpu.VMEM((4, 4, 4, quarter, cols), f32),
        pltpu.VMEM((16, rows, span), f32),
        pltpu.VMEM((span, cols), f32),
        pltpu.VMEM((3, 2, 4, 4, quarter, half), f32),
        pltpu.VMEM((3, 2, 4, 4, quarter, third), f32),
        pltpu.VMEM((3, 2, 4, quarter, half), f32),
        pltpu.VMEM((3, 2, 4, quarter, third), f32),
        pltpu.VMEM((3, 2, quarter, half), f32),
        pltpu.VMEM((3, 2, quarter, third), f32),
        pltpu.VMEM((2, lines, 128), f32),
        pltpu.VMEM((3, 4, lines, 128), f32),
        pltpu.VMEM((3, lines, 128), f32),
        pltpu.SemaphoreType.DMA((3,)),
        pltpu.SemaphoreType.DMA((3,)),
        pltpu.SemaphoreType.DMA((3, 3, 6)),
        pltpu.SemaphoreType.DMA((3, 3, 6)),
        pltpu.SemaphoreType.DMA((3,)),
        pltpu.SemaphoreType.DMA((3,)),
        pltpu.SemaphoreType.DMA((3, 3)),
        pltpu.SemaphoreType.DMA((3, 3)),
    ]


BLOCK = 512


def backward_kernel(n, sg_ref, thr_ref, spread_ref, nt_ref, og_ref, dy_ref, u_ref, x_ref, e_ref, f_ref, gt_hi, gt_lo,
                    s_in_ref, s_end_ref, lanes_ref, b_ref, c_ref, mask_ref, keep_ref, open_ref, step_ref, sig_ref,
                    rate_ref, gain_ref, w_out, small_out, dx_out, db_out, dc_out, dlogit_out, *scratch):
    later, dfx, dg_acc, dc_acc, db_acc, a_acc, b_acc, skip_acc, end_acc, small = scratch[:10]
    scan = make_scan(n, True, sg_ref, thr_ref, spread_ref, later, scratch[10 : 10 + SCAN_SCRATCH])
    rest = scratch[10 + SCAN_SCRATCH :]
    ring = Ring(nt_ref, og_ref, w_out, small, small_out, *rest[:12], rest[12:])
    f32, bf16 = jnp.float32, jnp.bfloat16
    span, width = x_ref.shape

    barrier = pltpu.get_barrier_semaphore()
    count = scan.greet(barrier)
    for d in (1, 2, 3):
        pl.semaphore_signal(barrier, inc=1, device_id={"dp": lax.rem(ring.xi + d, 4)}, device_id_type=MESH)
    pl.semaphore_wait(barrier, count + 3)

    def block(i):
        return pl.ds(pl.multiple_of(i * BLOCK, BLOCK), BLOCK)

    def pass_one(i, _):
        at = block(i)
        sp = spread_ref[:, at].astype(bf16)
        dy, xb = dy_ref[:, at], x_ref[:, at].astype(f32)
        du = dot2(split(e_ref[...]), sp, 1, 0) * dy
        fx = (dot2(split(f_ref[...]), sp, 1, 0) * xb).astype(bf16)
        du2 = split(du)
        dfx[:, at] = dot2((gt_hi[...], gt_lo[...]), du2, 1, 0)
        dg_acc[...] += dot2(du2, fx, 1, 1)
        dc_acc[...] += dot2(du2, s_in_ref[:, at], 1, 1)
        b_acc[...] += dot2(split(du * u_ref[:, at]), sp, 1, 1)
        row = jnp.broadcast_to(jnp.sum(dy * xb, axis=0, keepdims=True), (8, BLOCK))
        skip_acc[...] += dot2(split(row), sp, 1, 1)
        return 0

    def pass_two(i, _):
        at = block(i)
        sp = spread_ref[:, at].astype(bf16)
        f = dot2(split(f_ref[...]), sp, 1, 0)
        fx = f * x_ref[:, at].astype(f32)
        late = later[:, at]
        ds2 = split(lanes_ref[0:1, at] * late)
        d = dfx[:, at] + dot2(b_ref[...] * keep_ref[...].astype(bf16), ds2, 1, 0)
        dx_out[:, at] = (f * d + lanes_ref[1:2, at] * dy_ref[:, at]).astype(bf16)
        a_acc[...] += dot2(split(fx * d), sp, 1, 1)
        db_acc[...] += dot2(fx.astype(bf16), ds2, 1, 1)
        row = jnp.broadcast_to(jnp.sum(late * s_end_ref[:, at], axis=0, keepdims=True), (8, BLOCK))
        end_acc[...] += dot2(split(row), sp, 1, 1)
        return 0

    scan.begin()
    ring.pair_begin()
    scan.exchange()
    ring.own()
    scan.hops()
    ring.theirs()
    ring.begin(0)
    for acc in (dg_acc, dc_acc, db_acc, a_acc, b_acc, skip_acc, end_acc):
        acc[...] = jnp.zeros_like(acc)
    lax.fori_loop(0, width // BLOCK, pass_one, 0)
    scan.deliver()
    ring.middle(0)
    lax.fori_loop(0, width // BLOCK, pass_two, 0)

    a = a_acc[...]
    rows = lax.broadcasted_iota(jnp.int32, (span, span), 0)
    cols = lax.broadcasted_iota(jnp.int32, (span, span), 1)
    upper = jnp.where(rows <= cols, 1.0, 0.0).astype(f32)
    d_decay = jnp.dot(upper, b_acc[...] - a, precision=HIGHEST, preferred_element_type=f32) + end_acc[0:1]
    dlogit = (a / step_ref[...] - rate_ref[0:1] * d_decay) * sig_ref[...]
    heads = dlogit_out.shape[1]
    dlogit_out[...] = dlogit[:, :heads].astype(bf16)
    small[...] = jnp.zeros_like(small)
    lines = width // 128
    small[0:lines] = gain_ref[...]
    small[lines : lines + 1] = jnp.sum(dlogit, axis=0, keepdims=True)
    small[lines + 1 : lines + 2] = jnp.sum(-step_ref[...] * d_decay, axis=0, keepdims=True)
    small[lines + 2 : lines + 3] = skip_acc[0:1]
    ring.small_pair_begin()
    ring.end(0)
    ring.begin(1)
    ring.small_pair_end()
    ring.small_begin(0)
    dg = dg_acc[...] * mask_ref[...]
    dc_out[...] = (dot2(split(dg), b_ref[...], 1, 0) + open_ref[...] * dc_acc[...]).astype(bf16)
    db_out[...] = (dot2(split(dg.T), c_ref[...], 1, 0) + keep_ref[...] * db_acc[...]).astype(bf16)
    ring.middle(1)
    ring.small_end(0)
    ring.small_begin(1)
    ring.end(1)
    ring.begin(2)
    ring.small_end(1)
    ring.small_begin(2)
    ring.middle(2)
    ring.end(2)
    ring.share_begin()
    ring.small_end(2)
    ring.share_end()
    ring.finish()
    scan.finish()


def backward(n, heads, sg, thr, spread, nt, og, dy, *rest):
    f32, bf16 = jnp.float32, jnp.bfloat16
    ns, width = sg.shape
    span, cols = og.shape
    rows = nt.shape[2]
    lines = -(-(width // 128 + 3) // 8) * 8
    vmem = pl.BlockSpec(memory_space=pltpu.VMEM)
    wide = pltpu.VMEM((span, 128), f32)
    out = pl.pallas_call(
        functools.partial(backward_kernel, n),
        out_shape=(
            jax.ShapeDtypeStruct((4, rows // 4, cols), f32),
            jax.ShapeDtypeStruct((lines, 128), f32),
            jax.ShapeDtypeStruct((span, width), bf16),
            jax.ShapeDtypeStruct((span, ns), bf16),
            jax.ShapeDtypeStruct((span, ns), bf16),
            jax.ShapeDtypeStruct((span, heads), bf16),
        ),
        in_specs=[vmem] * (6 + len(rest)),
        out_specs=(vmem,) * 6,
        scratch_shapes=[
            pltpu.VMEM((ns, width), f32),
            pltpu.VMEM((span, width), f32),
            pltpu.VMEM((span, span), f32),
            pltpu.VMEM((span, ns), f32),
            pltpu.VMEM((span, ns), f32),
            wide,
            wide,
            pltpu.VMEM((8, 128), f32),
            pltpu.VMEM((8, 128), f32),
            pltpu.VMEM((lines, 128), f32),
        ] + scan_scratch(n, ns, width) + ring_scratch(rows, cols, span, lines),
        compiler_params=pltpu.CompilerParams(
            collective_id=2, has_side_effects=True, vmem_limit_bytes=VMEM_LIMIT),
        name="backward",
    )(sg, thr, spread, nt, og, dy, *rest)
    return out


def per_device(scan, back, ssm_input, gate_input, input_map, output_map, step_logit, step_bias,
               decay_rate, skip_gain, norm_gain, out_weight, resets, out_grad):
    f32, bf16 = jnp.float32, jnp.bfloat16
    x, z, bmap, cmap, og = ssm_input[0], gate_input[0], input_map[0], output_map[0], out_grad[0]
    rows, width = x.shape
    heads = step_bias.shape[0]
    per_head = width // heads

    start = lax.axis_index("seq") * rows
    ri = lax.broadcasted_iota(jnp.int32, (rows, rows), 0)
    ci = lax.broadcasted_iota(jnp.int32, (rows, rows), 1)
    below = ri >= ci
    tri = below.astype(f32)
    at_col = start + lax.broadcasted_iota(jnp.int32, (rows, 1), 0)
    at_row = start + lax.broadcasted_iota(jnp.int32, (1, rows), 1)
    flag_col = jnp.zeros((rows, 1), jnp.bool_)
    flag_row = jnp.zeros((1, rows), jnp.bool_)
    for k in range(resets.shape[1]):
        flag_col |= at_col == resets[0, k]
        flag_row |= at_row == resets[0, k]
    count_col = jnp.sum(jnp.where(below & flag_row, 1.0, 0.0), axis=1, keepdims=True)
    count_row = jnp.sum(jnp.where((ri <= ci) & flag_col, 1.0, 0.0), axis=0, keepdims=True)
    count_all = jnp.sum(flag_row.astype(f32))
    mask = below & (count_col == count_row)
    opened = count_col == 0
    keep = count_col == count_all

    spread = (
        lax.broadcasted_iota(jnp.int32, (heads, width), 0)
        == lax.broadcasted_iota(jnp.int32, (heads, width), 1) // per_head
    ).astype(f32)

    raw = step_logit[0].astype(f32) + step_bias
    step = jax.nn.softplus(raw)
    cum = exact(tri, -decay_rate * step)
    last = cum[rows - 1 :]
    mid = cum[rows // 2 : rows // 2 + 1]
    through = jnp.where(count_all == 0, jnp.exp(last), 0.0)
    e_head = jnp.exp(cum - mid)
    f_head = step * jnp.exp(mid - cum)
    wide = exact(
        jnp.concatenate([e_head, f_head, jnp.exp(last - mid), jnp.exp(mid), skip_gain[None], through], axis=0),
        spread,
    )
    e, f = wide[:rows], wide[rows : 2 * rows]
    tail, lead, skip, through_wide = (wide[2 * rows + k : 2 * rows + k + 1] for k in range(4))

    xf = x.astype(f32)
    fx_f = f * xf
    fx2 = split_wide(fx_f)
    fx = fx2[0]
    gm2 = split_wide(jnp.where(mask, bdot(cmap, bmap, 1, 1), 0.0))
    gm = gm2[0]
    b_keep = jnp.where(keep, bmap, jnp.zeros_like(bmap))
    c_open = jnp.where(opened, cmap, jnp.zeros_like(cmap))
    s_own = dot2(b_keep, fx2, 0, 0)
    thr = jnp.zeros((8, 128), f32).at[:, :heads].set(jnp.broadcast_to(through, (8, heads)))
    spread_pad = jnp.zeros((128, width), f32).at[:heads].set(spread)
    incoming = scan(tail * s_own, thr, spread_pad, False)
    s_in2 = split_wide(lead * incoming)
    s_in = s_in2[0]

    u = dot2(gm2, fx2, 1, 0) + dot2(c_open, s_in2, 1, 0)
    y = e * u + skip * xf
    zf = z.astype(f32)
    sig = jax.nn.sigmoid(zf)
    silu = zf * sig
    g = y * silu
    r = lax.rsqrt(jnp.mean(g * g, axis=1, keepdims=True) + 1e-05)
    ghat = g * r
    normed = (ghat * norm_gain).astype(bf16)
    mixed = bdot(normed, out_weight, 1, 0).astype(bf16)
    dn = bdot(og, out_weight, 1, 1)
    gain_grad = jnp.sum(dn * ghat, axis=0)
    q = dn * norm_gain
    dg = r * (q - ghat * jnp.mean(q * ghat, axis=1, keepdims=True))
    dy = dg * silu
    dz = (dg * y * (sig * (1.0 + zf * (1.0 - sig)))).astype(bf16)
    du_f = e * dy
    du2 = split_wide(du_f)
    sg = lead * dot2(c_open, du2, 0, 0)

    def padded(values, fill=0.0):
        return jnp.pad(values, ((0, 0), (0, 128 - heads)), constant_values=fill)

    gt2 = split_wide(jnp.where((ri <= ci) & (count_col == count_row), bdot(bmap, cmap, 1, 1), 0.0))
    nt = normed.T.astype(f32).reshape(16, 2, width // 32, rows)
    s_end = through_wide * incoming + tail * s_own
    lanes = jnp.concatenate([tail, skip, jnp.zeros((6, width), f32)], axis=0)
    weight_grad, sums, dx, db, dc, dlogit = back(
        heads, sg, thr, spread_pad, nt, og.astype(f32), dy, u, x, padded(e_head), padded(f_head), *gt2, s_in, s_end, lanes,
        bmap, cmap, mask.astype(f32), keep.astype(f32), opened.astype(f32), padded(step, 1.0),
        padded(jax.nn.sigmoid(raw)), jnp.broadcast_to(padded(decay_rate[None]), (8, 128)), gain_grad.reshape(-1, 128))
    lines = width // 128
    gain_sum = sums[:lines].reshape(-1)
    bias_sum, rate_sum, skip_sum = (sums[lines + k, :heads] for k in range(3))
    return (
        mixed[None],
        dx[None],
        dz[None],
        db[None],
        dc[None],
        dlogit[None],
        bias_sum,
        rate_sum,
        skip_sum,
        gain_sum,
        weight_grad.reshape(-1, weight_grad.shape[-1]),
    )


def solution(mesh):
    n = mesh.shape["seq"]

    def scan(state, thr, spread, reverse):
        return state_scan(n, state, thr, spread, reverse)

    def back(heads, *operands):
        return backward(n, heads, *operands)

    by_rows = P("dp", "seq", None)
    return jax.shard_map(
        functools.partial(per_device, scan, back),
        mesh=mesh,
        in_specs=(by_rows,) * 5 + (P(),) * 5 + (P("dp", None), by_rows),
        out_specs=(by_rows,) * 6 + (P(),) * 4 + (P("seq", None),),
        check_vma=False,
    )
```

```python
import functools

import jax
import jax.numpy as jnp
from jax import lax
from jax.experimental import pallas as pl
from jax.experimental.pallas import tpu as pltpu
from jax.sharding import PartitionSpec as P

MESH = pl.DeviceIdType.MESH
HIGHEST = lax.Precision.HIGHEST
VMEM_LIMIT = 63 * 1024 * 1024


def bdot(a, b, ca, cb):
    return lax.dot_general(
        a, b, (((ca,), (cb,)), ((), ())), preferred_element_type=jnp.float32
    )


def split(v):
    hi = v.astype(jnp.bfloat16)
    return hi, (v - hi.astype(jnp.float32)).astype(jnp.bfloat16)


def dot2(a, b, ca, cb):
    if isinstance(a, tuple) and isinstance(b, tuple):
        return bdot(a[0], b[0], ca, cb) + (bdot(a[0], b[1], ca, cb) + bdot(a[1], b[0], ca, cb))
    if isinstance(a, tuple):
        return bdot(a[0], b, ca, cb) + bdot(a[1], b, ca, cb)
    if isinstance(b, tuple):
        return bdot(a, b[0], ca, cb) + bdot(a, b[1], ca, cb)
    return bdot(a, b, ca, cb)


class Scan:
    def __init__(self, n, reverse, s_ref, thr_ref, spread_ref, out_ref, pair, mine, recv, stage, back, give,
                 thr_pair, thr_own, thr_buf, thr_wide, first_wide, sems):
        me = lax.axis_index("seq")
        self.chips, self.reverse = n // 2, reverse
        self.core, self.chip = lax.rem(me, 2), lax.div(me, 2)
        self.s_ref, self.thr_ref, self.spread_ref, self.out_ref = s_ref, thr_ref, spread_ref, out_ref
        self.pair, self.mine, self.recv, self.stage, self.back, self.give = pair, mine, recv, stage, back, give
        self.thr_pair, self.thr_own, self.thr_buf = thr_pair, thr_own, thr_buf
        self.thr_wide, self.first_wide = thr_wide, first_wide
        (self.ps, self.pr, self.ss, self.sr, self.ts, self.tr, self.bs, self.br, self.gs, self.gr, self.qs, self.qr) = sems
        ns, width = s_ref.shape
        self.rows, self.half = ns // self.chips, width // 2

    def lanes(self, core):
        return pl.ds(pl.multiple_of(core * self.half, 128), self.half)

    def band(self, k):
        return pl.ds(pl.multiple_of(k * self.rows, 8), self.rows)

    def copy(self, src, dst, ss, rs, to):
        return pltpu.make_async_remote_copy(src_ref=src, dst_ref=dst, send_sem=ss, recv_sem=rs,
                                            device_id={"seq": to}, device_id_type=MESH)

    def sibling(self):
        return self.chip * 2 + 1 - self.core

    def peer(self, k):
        return k * 2 + self.core

    def greet(self, barrier):
        pl.semaphore_signal(barrier, inc=1, device_id={"seq": self.sibling()}, device_id_type=MESH)

        def one(i, _):
            k = lax.rem(self.chip + 1 + i, self.chips)
            pl.semaphore_signal(barrier, inc=1, device_id={"seq": self.peer(k)}, device_id_type=MESH)
            return 0

        lax.fori_loop(0, self.chips - 1, one, 0)
        return self.chips

    def pair_copy(self, k):
        return self.copy(self.s_ref.at[self.band(k), self.lanes(1 - self.core)], self.pair.at[k],
                         self.ps.at[k], self.pr.at[k], self.sibling())

    def thr_pair_copy(self):
        return self.copy(self.thr_ref, self.thr_pair, self.qs, self.qr, self.sibling())

    def thr_copy(self, k, slot):
        return self.copy(self.thr_own, self.thr_buf.at[slot], self.ts.at[k], self.tr.at[slot], self.peer(k))

    def chunk_copy(self, k, slot):
        return self.copy(self.mine.at[k], self.recv.at[slot], self.ss.at[k], self.sr.at[slot], self.peer(k))

    def back_copy(self, k, slot):
        return self.copy(self.stage.at[k], self.back.at[slot], self.bs.at[k], self.br.at[slot], self.peer(k))

    def give_copy(self, k, core):
        return self.copy(self.give.at[k], self.out_ref.at[self.band(k), self.lanes(core)], self.gs.at[k], self.gr.at[k],
                         self.sibling())

    def begin(self):
        self.thr_pair_copy().start()

        def one(i, _):
            self.pair_copy(lax.rem(self.chip + 1 + i, self.chips)).start()
            return 0

        lax.fori_loop(0, self.chips, one, 0)

    def exchange(self):
        first = 1 if self.reverse else 0
        self.thr_pair_copy().wait_recv()
        mine_first = self.core == first
        thr_first = jnp.where(mine_first, self.thr_ref[...], self.thr_pair[...])
        thr_second = jnp.where(mine_first, self.thr_pair[...], self.thr_ref[...])
        self.thr_own[...] = thr_first * thr_second
        self.thr_buf[self.chip] = thr_first * thr_second

        def tell(i, _):
            self.thr_copy(lax.rem(self.chip + 1 + i, self.chips), self.chip).start()
            return 0

        lax.fori_loop(0, self.chips - 1, tell, 0)
        both = jnp.concatenate([thr_first, thr_second], axis=0)
        wide = jnp.dot(both, self.spread_ref[:, self.lanes(self.core)].astype(jnp.float32), precision=HIGHEST,
                       preferred_element_type=jnp.float32)
        self.first_wide[...] = wide[0:8]
        second_wide = wide[8:16]

        def one(i, _):
            k = lax.rem(self.chip + 1 + i, self.chips)
            self.pair_copy(k).wait_recv()
            own = self.s_ref[self.band(k), self.lanes(self.core)]
            other = self.pair[k]
            early = jnp.where(mine_first, own, other)
            late = jnp.where(mine_first, other, own)
            self.mine[k] = second_wide * early + late

            @pl.when(k != self.chip)
            def _():
                self.chunk_copy(k, self.chip).start()

            return 0

        lax.fori_loop(0, self.chips, one, 0)
        self.recv[self.chip] = self.mine[self.chip]

    def hops(self):
        def arrive(i, _):
            self.thr_copy(self.chip, lax.rem(self.chip + 1 + i, self.chips)).wait_recv()
            return 0

        lax.fori_loop(0, self.chips - 1, arrive, 0)
        self.thr_wide[...] = jnp.dot(self.thr_buf[:, 0, :], self.spread_ref[:, self.lanes(self.core)].astype(jnp.float32),
                                     precision=HIGHEST, preferred_element_type=jnp.float32)

        def hop(i, state):
            j = self.chips - 1 - i if self.reverse else i

            @pl.when(j != self.chip)
            def _():
                self.chunk_copy(self.chip, j).wait_recv()

            self.stage[j] = state

            @pl.when(j != self.chip)
            def _():
                self.back_copy(j, self.chip).start()

            return self.thr_wide[pl.ds(j, 1), :] * state + self.recv[j]

        lax.fori_loop(0, self.chips, hop, jnp.zeros((self.rows, self.half), jnp.float32))
        self.back[self.chip] = self.stage[self.chip]

    def deliver(self):
        mine_first = self.core == (1 if self.reverse else 0)

        def one(i, _):
            k = lax.rem(self.chip + i, self.chips)

            @pl.when(k != self.chip)
            def _():
                self.back_copy(self.chip, k).wait_recv()

            early = self.back[k]
            own = self.s_ref[self.band(k), self.lanes(self.core)]
            late = self.first_wide[...] * early + jnp.where(mine_first, own, self.pair[k])
            self.out_ref[self.band(k), self.lanes(self.core)] = jnp.where(mine_first, early, late)
            self.give[k] = jnp.where(mine_first, late, early)
            self.give_copy(k, self.core).start()
            return 0

        lax.fori_loop(0, self.chips, one, 0)

        def got(k, _):
            self.give_copy(k, 1 - self.core).wait_recv()
            return 0

        lax.fori_loop(0, self.chips, got, 0)

    def finish(self):
        self.thr_pair_copy().wait_send()

        def one(i, _):
            k = lax.rem(self.chip + 1 + i, self.chips)
            self.pair_copy(k).wait_send()
            self.give_copy(k, self.core).wait_send()

            @pl.when(k != self.chip)
            def _():
                self.thr_copy(k, self.chip).wait_send()
                self.chunk_copy(k, self.chip).wait_send()
                self.back_copy(k, self.chip).wait_send()

            return 0

        lax.fori_loop(0, self.chips, one, 0)


def scan_scratch(n, ns, width):
    chips = n // 2
    chunk = pltpu.VMEM((chips, ns // chips, width // 2), jnp.float32)
    tile = pltpu.VMEM((8, 128), jnp.float32)
    return [chunk] * 3 + [
        tile,
        tile,
        tile,
        pltpu.VMEM((chips, 8, 128), jnp.float32),
        pltpu.VMEM((chips, width // 2), jnp.float32),
        pltpu.VMEM((8, width // 2), jnp.float32),
    ] + [pltpu.SemaphoreType.DMA((chips,))] * 10 + [pltpu.SemaphoreType.DMA] * 2


SCAN_SCRATCH = 9 + 12


def make_scan(n, reverse, s_ref, spread_ref, out_ref, shared, scratch):
    mine, stage, give = shared
    pair, recv, back, thr_ref = scratch[:4]
    return Scan(n, reverse, s_ref, thr_ref, spread_ref, out_ref, pair, mine, recv, stage, back, give,
                *scratch[4:9], scratch[9:])


ORDERS = ((2, 1, 0), (1, 0, 2), (0, 2, 1))


class Ring:
    def __init__(self, og_ref, og_wide, nt_own, nt_send, out_ref, small, small_out, part, nt_got, og_got, agg1, full1, agg2, full2,
                 agg3, full3, slots_c, slots_a, total, sems):
        (self.cs, self.cr, self.ns, self.nr, self.rs, self.rr, self.xs, self.xr, self.ms, self.mr) = sems
        self.xi = lax.axis_index("dp")
        s = lax.axis_index("seq")
        self.core = lax.rem(s, 2)
        self.here = (lax.div(s, 8), lax.rem(lax.div(s, 2), 4), self.xi)
        self.sibling = {"seq": s + 1 - 2 * self.core}
        self.og_ref, self.og_wide, self.nt_own, self.nt_send = og_ref, og_wide, nt_own, nt_send
        self.out_ref = out_ref
        self.small, self.small_out = small, small_out
        self.part, self.nt_got, self.og_got = part, nt_got, og_got
        self.bufs = ((agg1, full1), (agg2, full2), (agg3, full3))
        self.slots_c, self.slots_a, self.total = slots_c, slots_a, total
        self.third = part.shape[-1] // 3
        self.half = self.third // 2
        self.started = []
        self.steps = {}

    def at(self, axis, index):
        if axis == 2:
            return {"dp": index}
        z, y = (index, self.here[1]) if axis == 0 else (self.here[0], index)
        return {"seq": (z * 4 + y) * 2 + self.core}

    def remote(self, src, dst, ss, rs, to):
        return pltpu.make_async_remote_copy(src_ref=src, dst_ref=dst, send_sem=ss, recv_sem=rs,
                                            device_id=to, device_id_type=MESH)

    def start(self, copies):
        for c in copies:
            c.start()
        self.started += copies
        return copies

    def og_begin(self):
        self.og_wide[...] = self.og_ref[...].astype(jnp.float32)
        self.og_copy = self.remote(self.og_wide, self.og_got, self.cs.at[0], self.cr.at[0], self.sibling)
        self.og_copy.start()

    def nt_copy(self, i, count):
        here = pl.ds(i * count, count)
        return self.remote(self.nt_send.at[here], self.nt_got.at[here], self.ns.at[i], self.nr.at[i], self.sibling)

    def own(self):
        def one(b, _):
            z, y = lax.div(b, 4), lax.rem(b, 4)
            self.part[z, y] = bdot(self.nt_own[b], self.og_ref[...], 1, 0).reshape(self.part.shape[2:])
            return 0

        lax.fori_loop(0, 16, one, 0)

    def theirs(self, parts):
        self.og_copy.wait_recv()
        og = self.og_got[...].astype(jnp.bfloat16)

        def got(i, _):
            self.nt_copy(i, 16 // parts).wait_recv()
            return 0

        lax.fori_loop(0, parts, got, 0)

        def one(b, _):
            z, y = lax.div(b, 4), lax.rem(b, 4)
            lhs = self.nt_got[b].astype(jnp.bfloat16)
            self.part[z, y] += bdot(lhs, og, 1, 0).reshape(self.part.shape[2:])
            return 0

        lax.fori_loop(0, 16, one, 0)

    def region(self, step, p, t, h=None):
        order = ORDERS[p]
        index = [slice(None)] * 3
        for done in order[:step]:
            index[done] = self.here[done]
        index[order[step]] = t
        lo = p * self.third + (0 if h in (None, 0) else self.half)
        return (*index, slice(None), pl.ds(lo, self.third if h is None else self.half))

    def ways(self, step, p):
        axis = ORDERS[p][step]
        me = self.here[axis]
        return axis, lax.rem(me + 1, 4), lax.rem(me + 3, 4), lax.rem(me + 2, 4)

    def begin(self, step):
        agg, full = self.bufs[step]
        first, second, last = [], [], []
        lo, hi = pl.ds(0, self.half), pl.ds(self.half, self.half)
        for p in range(3):
            axis, up, down, far = self.ways(step, p)

            def go(t, h, dst, k, to):
                return self.remote(self.part.at[self.region(step, p, t, h)], dst, self.rs.at[step, p, k],
                                   self.rr.at[step, p, k], self.at(axis, to))

            first.append([go(far, 0, agg.at[p, 0], 0, up), go(far, 1, agg.at[p, 1], 1, down)])
            second.append([go(up, 1, full.at[p, 0, ..., hi], 2, up), go(down, 0, full.at[p, 1, ..., lo], 3, down)])
            last.append([go(up, 0, full.at[p, 0, ..., lo], 4, up), go(down, 1, full.at[p, 1, ..., hi], 5, down)])
        for p in range(3):
            self.start(first[p])
        for p in range(3):
            self.start(second[p])
        self.steps[step] = (first, second, last)

    def middle(self, step):
        agg, _ = self.bufs[step]
        first, _, last = self.steps[step]
        for p in range(3):
            _, up, down, _ = self.ways(step, p)
            first[p][0].wait_recv()
            self.part[self.region(step, p, up, 0)] += agg[p, 0]
            self.start([last[p][0]])
            first[p][1].wait_recv()
            self.part[self.region(step, p, down, 1)] += agg[p, 1]
            self.start([last[p][1]])

    def end(self, step):
        _, full = self.bufs[step]
        _, second, last = self.steps[step]
        for p in range(3):
            for c in second[p] + last[p]:
                c.wait_recv()
            here = self.region(step, p, self.here[ORDERS[p][step]])
            self.part[here] += full[p, 0] + full[p, 1]

    def small_pair_begin(self):
        self.small_pair = self.start([
            self.remote(self.small, self.slots_c.at[self.core], self.cs.at[2], self.cr.at[2], self.sibling)])
        self.slots_c[self.core] = self.small[...]

    def small_pair_end(self):
        self.small_pair[0].wait_recv()
        self.total[0] = self.slots_c[0] + self.slots_c[1]

    def small_begin(self, k):
        axis = (2, 1, 0)[k]
        me = self.here[axis]
        self.smalls = self.start([
            self.remote(self.total.at[k], self.slots_a.at[k, me], self.ms.at[k, d - 1], self.mr.at[k, d - 1],
                        self.at(axis, lax.rem(me + d, 4)))
            for d in (1, 2, 3)])
        self.slots_a[k, me] = self.total[k]

    def small_end(self, k):
        for c in self.smalls:
            c.wait_recv()
        now = (self.slots_a[k, 0] + self.slots_a[k, 1]) + (self.slots_a[k, 2] + self.slots_a[k, 3])
        if k < 2:
            self.total[k + 1] = now
        else:
            self.small_out[...] = now

    def share_begin(self):
        z, y, x = self.here
        self.out_ref[x] = self.part[z, y, x]
        self.start([
            self.remote(self.out_ref.at[x], self.out_ref.at[x], self.xs.at[d - 1], self.xr.at[d - 1],
                        {"dp": lax.rem(x + d, 4)})
            for d in (1, 2, 3)])

    def share_end(self):
        for d in (1, 2, 3):
            came = lax.rem(self.xi + 4 - d, 4)
            self.remote(self.out_ref.at[came], self.out_ref.at[came], self.xs.at[d - 1], self.xr.at[d - 1],
                        {"dp": came}).wait_recv()

    def finish(self):
        for c in self.started:
            c.wait_send()


def ring_scratch(rows, cols, span, lines):
    f32 = jnp.float32
    quarter, third, half = rows // 4, cols // 3, cols // 6
    return [
        pltpu.VMEM((4, 4, 4, quarter, cols), f32),
        pltpu.VMEM((16, rows, span), f32),
        pltpu.VMEM((span, cols), f32),
        pltpu.VMEM((3, 2, 4, 4, quarter, half), f32),
        pltpu.VMEM((3, 2, 4, 4, quarter, third), f32),
        pltpu.VMEM((3, 2, 4, quarter, half), f32),
        pltpu.VMEM((3, 2, 4, quarter, third), f32),
        pltpu.VMEM((3, 2, quarter, half), f32),
        pltpu.VMEM((3, 2, quarter, third), f32),
        pltpu.VMEM((2, lines, 128), f32),
        pltpu.VMEM((3, 4, lines, 128), f32),
        pltpu.VMEM((3, lines, 128), f32),
        pltpu.SemaphoreType.DMA((3,)),
        pltpu.SemaphoreType.DMA((3,)),
        pltpu.SemaphoreType.DMA((8,)),
        pltpu.SemaphoreType.DMA((8,)),
        pltpu.SemaphoreType.DMA((3, 3, 6)),
        pltpu.SemaphoreType.DMA((3, 3, 6)),
        pltpu.SemaphoreType.DMA((3,)),
        pltpu.SemaphoreType.DMA((3,)),
        pltpu.SemaphoreType.DMA((3, 3)),
        pltpu.SemaphoreType.DMA((3, 3)),
    ]


BLOCK = 384
TAIL, LEAD, SKIP, THROUGH = range(4)


def softplus(v):
    return jnp.maximum(v, 0.0) + jnp.log1p(jnp.exp(-jnp.abs(v)))


def mixer_kernel(n, x_ref, z_ref, b_ref, c_ref, logit_ref, og_ref, par_ref, gain_ref, resets_ref, w_hbm,
                 w_out, small_out, dx_out, dz_out, db_out, dc_out, dlogit_out, mixed_out, *scratch):
    (dn, u, normed, s_buf, inc, sg, s_in, spread, lanes, w_buf, gm_hi, gm_lo, gt_hi, gt_lo, mask_ref, bk, bkt, co, cot,
     e_ref, f_ref, step_ref, sig_ref, keep_ref, open_ref, ms_acc, m2_acc, dg_acc, dc_acc, db_acc, a_acc, b_acc,
     skip_acc, end_acc, small, nt_own, nt_send, og_wide, mine, stage, give, w_sem) = scratch[:42]
    rest = scratch[42:]
    ahead = make_scan(n, False, s_buf, spread, inc, (mine, stage, give), rest[:SCAN_SCRATCH])
    behind = make_scan(n, True, sg, spread, inc, (mine, stage, give), rest[SCAN_SCRATCH : 2 * SCAN_SCRATCH])
    rest = rest[2 * SCAN_SCRATCH :]
    ring = Ring(og_ref, og_wide, nt_own, nt_send, w_out, small, small_out, *rest[:12], rest[12:])
    f32, bf16 = jnp.float32, jnp.bfloat16
    span, width = x_ref.shape
    blocks = width // BLOCK

    def w_copy(i):
        slot = lax.rem(i, 2)
        return pltpu.make_async_copy(w_hbm.at[pl.ds(i * BLOCK, BLOCK)], w_buf.at[slot], w_sem.at[slot])

    barrier = pltpu.get_barrier_semaphore()
    count = ahead.greet(barrier)
    for d in (1, 2, 3):
        pl.semaphore_signal(barrier, inc=1, device_id={"dp": lax.rem(ring.xi + d, 4)}, device_id_type=MESH)
    w_copy(0).start()

    start = lax.axis_index("seq") * span
    ri = lax.broadcasted_iota(jnp.int32, (span, span), 0)
    ci = lax.broadcasted_iota(jnp.int32, (span, span), 1)
    flag_c = jnp.zeros((span, span), f32)
    flag_r = jnp.zeros((span, span), f32)
    for k in range(resets_ref.shape[0]):
        at_reset = resets_ref[k, 0:1, :] - start
        flag_c = jnp.where(ci == at_reset, 1.0, flag_c)
        flag_r = jnp.where(ri == at_reset, 1.0, flag_r)
    count_col = jnp.sum(jnp.where(ri >= ci, flag_c, 0.0), axis=1, keepdims=True)
    count_row = jnp.sum(jnp.where(ri <= ci, flag_r, 0.0), axis=0, keepdims=True)
    all_col = jnp.sum(flag_c, axis=1, keepdims=True)
    all_row = jnp.sum(flag_r, axis=0, keepdims=True)
    below = jnp.where(ri >= ci, 1.0, 0.0)
    mask = jnp.where((ri >= ci) & (count_col == count_row), 1.0, 0.0)
    mask_ref[...] = mask
    keep = jnp.where(count_col == all_col, 1.0, 0.0)
    opened = jnp.where(count_col == 0.0, 1.0, 0.0)
    keep_ref[...] = jnp.broadcast_to(keep, keep_ref.shape)
    open_ref[...] = jnp.broadcast_to(opened, open_ref.shape)
    b_keep = b_ref[...].astype(f32) * keep
    c_open = c_ref[...].astype(f32) * opened
    bk[...] = b_keep.astype(bf16)
    bkt[...] = b_keep.T.astype(bf16)
    co[...] = c_open.astype(bf16)
    cot[...] = c_open.T.astype(bf16)
    gm = bdot(c_ref[...], b_ref[...], 1, 1) * mask
    gm_hi[...], gm_lo[...] = split(gm)
    gt_hi[...], gt_lo[...] = split(gm.T)
    raw = logit_ref[...].astype(f32) + par_ref[0:1]
    step = softplus(raw)
    step_ref[...] = step
    sig_ref[...] = jax.nn.sigmoid(raw)
    cum = jnp.dot(below, -par_ref[1:2] * step, precision=HIGHEST, preferred_element_type=f32)
    last = cum[span - 1 : span]
    mid = cum[span // 2 : span // 2 + 1]
    through = jnp.where(all_row[:, :128] == 0.0, jnp.exp(last), 0.0)
    e_ref[...] = jnp.exp(cum - mid)
    f_ref[...] = step * jnp.exp(mid - cum)
    thr = jnp.broadcast_to(through, (8, 128))
    ahead.thr_ref[...] = thr
    behind.thr_ref[...] = thr
    head_of = lax.broadcasted_iota(jnp.int32, spread.shape, 1) >> 6
    spread[...] = jnp.where(lax.broadcasted_iota(jnp.int32, spread.shape, 0) == head_of, 1.0, 0.0).astype(bf16)
    per_head = jnp.concatenate(
        [jnp.exp(last - mid), jnp.exp(mid), par_ref[2:3], through, jnp.zeros((4, 128), f32)], axis=0)
    lanes[...] = jnp.dot(per_head, spread[...].astype(f32), precision=HIGHEST, preferred_element_type=f32)
    for acc in (ms_acc, m2_acc, dg_acc, dc_acc, db_acc, a_acc, b_acc, skip_acc, end_acc, small):
        acc[...] = jnp.zeros_like(acc)

    def block(i):
        return pl.ds(pl.multiple_of(i * BLOCK, 128), BLOCK)

    def every(body):
        def one(i, _):
            body(i, block(i))
            return 0

        lax.fori_loop(0, blocks, one, 0)

    def e_of(at):
        return dot2(split(e_ref[...]), spread[:, at], 1, 0)

    def f_of(at):
        return dot2(split(f_ref[...]), spread[:, at], 1, 0)

    def row(k, at):
        return lanes[k : k + 1, at]

    def own_state(i, at):
        fx2 = split(f_of(at) * x_ref[:, at].astype(f32))
        s_buf[:, at] = row(TAIL, at) * dot2(bkt[...], fx2, 1, 0)

    def in_span(i, at):
        fx2 = split(f_of(at) * x_ref[:, at].astype(f32))
        u[:, at] = dot2((gm_hi[...], gm_lo[...]), fx2, 1, 0)

    def project_back(i, at):
        w_copy(i).wait()

        @pl.when(i + 1 < blocks)
        def _():
            w_copy(i + 1).start()

        dn[:, at] = bdot(og_ref[...], w_buf[lax.rem(i, 2)], 1, 1)

    def read_out(i, at):
        before = inc[:, at]
        s2 = split(row(LEAD, at) * before)
        s_in[:, at] = s2[0]
        s_buf[:, at] = row(THROUGH, at) * before + s_buf[:, at]
        now = u[:, at] + dot2(co[...], s2, 1, 0)
        u[:, at] = now
        y = e_of(at) * now + row(SKIP, at) * x_ref[:, at].astype(f32)
        zf = z_ref[:, at].astype(f32)
        g = y * (zf * jax.nn.sigmoid(zf))
        ms_acc[...] += jnp.broadcast_to(jnp.sum(g * g, axis=1, keepdims=True), ms_acc.shape)
        m2_acc[...] += jnp.broadcast_to(
            jnp.sum(dn[:, at] * gain_ref[0:1, at] * g, axis=1, keepdims=True), m2_acc.shape)

    def norm(i, at):
        e = e_of(at)
        y = e * u[:, at] + row(SKIP, at) * x_ref[:, at].astype(f32)
        zf = z_ref[:, at].astype(f32)
        sig = jax.nn.sigmoid(zf)
        silu = zf * sig
        r = lax.rsqrt(ms_acc[:, 0:1] * (1.0 / width) + 1e-05)
        ghat = y * silu * r
        gain = gain_ref[0:1, at]
        out = ghat * gain
        out_low = out.astype(bf16)
        normed[:, at] = out_low
        up = out_low.astype(f32).T.reshape(BLOCK // 192, 2, 96, span)
        here = pl.ds(i * (BLOCK // 192), BLOCK // 192)
        even = ring.core == 0
        nt_own[here] = jnp.where(even, up[:, 0], up[:, 1]).astype(bf16)
        nt_send[here] = jnp.where(even, up[:, 1], up[:, 0])
        ring.nt_copy(i, BLOCK // 192).start()
        d = dn[:, at]
        sums = jnp.sum(d * ghat, axis=0, keepdims=True)
        for k in range(BLOCK // 128):
            small[pl.ds(i * (BLOCK // 128) + k, 1)] = sums[:, k * 128 : (k + 1) * 128]
        dg = r * (d * gain - ghat * (r * m2_acc[:, 0:1] * (1.0 / width)))
        dy = dg * silu
        dz_out[:, at] = (dg * y * (sig * (1.0 + zf * (1.0 - sig)))).astype(bf16)
        dn[:, at] = dy
        sg[:, at] = row(LEAD, at) * dot2(cot[...], split(e * dy), 1, 0)

    def pass_one(i, at):
        sp = spread[:, at]
        dy, xb = dn[:, at], x_ref[:, at].astype(f32)
        du = e_of(at) * dy
        fx = (f_of(at) * xb).astype(bf16)
        du2 = split(du)
        b_acc[...] += dot2(split(du * u[:, at]), sp, 1, 1)
        u[:, at] = dot2((gt_hi[...], gt_lo[...]), du2, 1, 0)
        dg_acc[...] += dot2(du2, fx, 1, 1)
        dc_acc[...] += dot2(du2, s_in[:, at], 1, 1)
        line = jnp.broadcast_to(jnp.sum(dy * xb, axis=0, keepdims=True), (8, BLOCK))
        skip_acc[...] += dot2(split(line), sp, 1, 1)

    def pass_two(i, at):
        sp = spread[:, at]
        f = f_of(at)
        fx = f * x_ref[:, at].astype(f32)
        late = inc[:, at]
        ds2 = split(row(TAIL, at) * late)
        d = u[:, at] + dot2(bk[...], ds2, 1, 0)
        dx_out[:, at] = (f * d + row(SKIP, at) * dn[:, at]).astype(bf16)
        a_acc[...] += dot2(split(fx * d), sp, 1, 1)
        db_acc[...] += dot2(fx.astype(bf16), ds2, 1, 1)
        line = jnp.broadcast_to(jnp.sum(late * s_buf[:, at], axis=0, keepdims=True), (8, BLOCK))
        end_acc[...] += dot2(split(line), sp, 1, 1)

    def project(i, at):
        w_copy(i).wait()

        @pl.when(i + 1 < blocks)
        def _():
            w_copy(i + 1).start()

        og_wide[...] += bdot(normed[:, at], w_buf[lax.rem(i, 2)], 1, 0)

    every(own_state)
    pl.semaphore_wait(barrier, count + 3)
    ahead.begin()
    every(in_span)
    ahead.exchange()
    ring.og_begin()
    every(project_back)
    ahead.hops()
    ahead.deliver()
    ahead.finish()
    every(read_out)
    every(norm)
    behind.begin()
    ring.own()
    behind.exchange()
    ring.theirs(blocks)
    ring.begin(0)
    behind.hops()
    every(pass_one)
    behind.deliver()
    ring.middle(0)
    w_copy(0).start()
    every(pass_two)

    a = a_acc[...]
    upper = jnp.where(ri <= ci, 1.0, 0.0)
    d_decay = jnp.dot(upper, b_acc[...] - a, precision=HIGHEST, preferred_element_type=f32) + end_acc[0:1]
    dlogit = (a / step_ref[...] - par_ref[1:2] * d_decay) * sig_ref[...]
    dlogit_out[...] = dlogit[:, : dlogit_out.shape[1]].astype(bf16)
    lines = width // 128
    small[lines : lines + 1] = jnp.sum(dlogit, axis=0, keepdims=True)
    small[lines + 1 : lines + 2] = jnp.sum(-step_ref[...] * d_decay, axis=0, keepdims=True)
    small[lines + 2 : lines + 3] = skip_acc[0:1]
    ring.small_pair_begin()
    dg = dg_acc[...] * mask_ref[...]
    dc_out[...] = (dot2(split(dg), b_ref[...], 1, 0) + open_ref[...] * dc_acc[...]).astype(bf16)
    db_out[...] = (dot2(split(dg.T), c_ref[...], 1, 0) + keep_ref[...] * db_acc[...]).astype(bf16)
    ring.end(0)
    ring.begin(1)
    ring.small_pair_end()
    ring.small_begin(0)
    ring.og_copy.wait_send()
    og_wide[...] = jnp.zeros_like(og_wide)
    every(project)
    mixed_out[...] = og_wide[...].astype(bf16)
    ring.middle(1)
    ring.small_end(0)
    ring.small_begin(1)
    ring.end(1)
    ring.begin(2)
    ring.small_end(1)
    ring.small_begin(2)
    ring.middle(2)
    ring.end(2)
    ring.share_begin()
    ring.small_end(2)
    ring.share_end()
    ring.finish()

    def sent(i, _):
        ring.nt_copy(i, BLOCK // 192).wait_send()
        return 0

    lax.fori_loop(0, blocks, sent, 0)
    behind.finish()


def per_device(n, ssm_input, gate_input, input_map, output_map, step_logit, step_bias, decay_rate, skip_gain,
               norm_gain, out_weight, resets, out_grad):
    f32, bf16 = jnp.float32, jnp.bfloat16
    _, span, width = ssm_input.shape
    ns, heads, cols = input_map.shape[2], step_bias.shape[0], out_weight.shape[1]
    rows, lines = width // 32, width // 128 + 8
    logit = jnp.pad(step_logit[0], ((0, 0), (0, 128 - heads)))
    params = jnp.pad(jnp.stack([step_bias, decay_rate, skip_gain]), ((0, 5), (0, 128 - heads)))
    starts = jnp.broadcast_to(resets[0][:, None, None], (resets.shape[1], 8, span))
    vmem = pl.BlockSpec(memory_space=pltpu.VMEM)

    def wide(*shape):
        return pltpu.VMEM(shape, f32)

    def low(*shape):
        return pltpu.VMEM(shape, bf16)

    chunk = wide(n // 2, ns // (n // 2), width // 2)
    weight_grad, sums, dx, dz, db, dc, dlogit, mixed = pl.pallas_call(
        functools.partial(mixer_kernel, n),
        out_shape=(
            jax.ShapeDtypeStruct((4, rows // 4, cols), f32),
            jax.ShapeDtypeStruct((lines, 128), f32),
            jax.ShapeDtypeStruct((span, width), bf16),
            jax.ShapeDtypeStruct((span, width), bf16),
            jax.ShapeDtypeStruct((span, ns), bf16),
            jax.ShapeDtypeStruct((span, ns), bf16),
            jax.ShapeDtypeStruct((span, heads), bf16),
            jax.ShapeDtypeStruct((span, cols), bf16),
        ),
        in_specs=[vmem] * 9 + [pl.BlockSpec(memory_space=pl.ANY)],
        out_specs=(vmem,) * 8,
        scratch_shapes=[
            wide(span, width), wide(span, width), low(span, width), wide(ns, width), wide(ns, width), wide(ns, width),
            low(ns, width), low(128, width), wide(8, width), low(2, BLOCK, cols),
            low(span, span), low(span, span), low(span, span), low(span, span), wide(span, span),
            low(span, ns), low(ns, span), low(span, ns), low(ns, span),
            wide(span, 128), wide(span, 128), wide(span, 128), wide(span, 128), wide(span, ns), wide(span, ns),
            wide(span, 128), wide(span, 128), wide(span, span), wide(span, ns), wide(span, ns),
            wide(span, 128), wide(span, 128), wide(8, 128), wide(8, 128), wide(lines, 128),
            low(16, rows, span), wide(16, rows, span), wide(span, cols), chunk, chunk, chunk,
            pltpu.SemaphoreType.DMA((2,)),
        ] + scan_scratch(n, ns, width) * 2 + ring_scratch(rows, cols, span, lines),
        compiler_params=pltpu.CompilerParams(
            collective_id=1, has_side_effects=True, vmem_limit_bytes=VMEM_LIMIT),
        name="mixer",
    )(ssm_input[0], gate_input[0], input_map[0], output_map[0], logit, out_grad[0], params, norm_gain[None], starts,
      out_weight)
    first = width // 128
    bias_sum, rate_sum, skip_sum = (sums[first + k, :heads] for k in range(3))
    return (
        mixed[None],
        dx[None],
        dz[None],
        db[None],
        dc[None],
        dlogit[None],
        bias_sum,
        rate_sum,
        skip_sum,
        sums[:first].reshape(-1),
        weight_grad.reshape(rows, cols),
    )


def solution(mesh):
    by_rows = P("dp", "seq", None)
    return jax.shard_map(
        functools.partial(per_device, mesh.shape["seq"]),
        mesh=mesh,
        in_specs=(by_rows,) * 5 + (P(),) * 5 + (P("dp", None), by_rows),
        out_specs=(by_rows,) * 6 + (P(),) * 4 + (P("seq", None),),
        check_vma=False,
    )
```

```python
import functools

import jax
import jax.numpy as jnp
from jax import lax
from jax.experimental import pallas as pl
from jax.experimental.pallas import tpu as pltpu
from jax.sharding import PartitionSpec as P

MESH = pl.DeviceIdType.MESH
HIGHEST = lax.Precision.HIGHEST
VMEM_LIMIT = 63 * 1024 * 1024


def bdot(a, b, ca, cb):
    return lax.dot_general(
        a, b, (((ca,), (cb,)), ((), ())), preferred_element_type=jnp.float32
    )


def split(v):
    hi = v.astype(jnp.bfloat16)
    return hi, (v - hi.astype(jnp.float32)).astype(jnp.bfloat16)


def dot2(a, b, ca, cb):
    if isinstance(a, tuple) and isinstance(b, tuple):
        return bdot(a[0], b[0], ca, cb) + (bdot(a[0], b[1], ca, cb) + bdot(a[1], b[0], ca, cb))
    if isinstance(a, tuple):
        return bdot(a[0], b, ca, cb) + bdot(a[1], b, ca, cb)
    if isinstance(b, tuple):
        return bdot(a, b[0], ca, cb) + bdot(a, b[1], ca, cb)
    return bdot(a, b, ca, cb)


class Scan:
    def __init__(self, n, reverse, s_ref, thr_ref, spread_ref, out_ref, pair, mine, recv, stage, back, give,
                 thr_pair, thr_own, thr_buf, thr_wide, first_wide, sems):
        me = lax.axis_index("seq")
        self.chips, self.reverse = n // 2, reverse
        self.core, self.chip = lax.rem(me, 2), lax.div(me, 2)
        self.s_ref, self.thr_ref, self.spread_ref, self.out_ref = s_ref, thr_ref, spread_ref, out_ref
        self.pair, self.mine, self.recv, self.stage, self.back, self.give = pair, mine, recv, stage, back, give
        self.thr_pair, self.thr_own, self.thr_buf = thr_pair, thr_own, thr_buf
        self.thr_wide, self.first_wide = thr_wide, first_wide
        (self.ps, self.pr, self.ss, self.sr, self.ts, self.tr, self.bs, self.br, self.gs, self.gr, self.qs, self.qr) = sems
        ns, width = s_ref.shape
        self.rows, self.half = ns // self.chips, width // 2

    def lanes(self, core):
        return pl.ds(pl.multiple_of(core * self.half, 128), self.half)

    def band(self, k):
        return pl.ds(pl.multiple_of(k * self.rows, 8), self.rows)

    def copy(self, src, dst, ss, rs, to):
        return pltpu.make_async_remote_copy(src_ref=src, dst_ref=dst, send_sem=ss, recv_sem=rs,
                                            device_id={"seq": to}, device_id_type=MESH)

    def sibling(self):
        return self.chip * 2 + 1 - self.core

    def peer(self, k):
        return k * 2 + self.core

    def greet(self, barrier):
        pl.semaphore_signal(barrier, inc=1, device_id={"seq": self.sibling()}, device_id_type=MESH)

        def one(i, _):
            k = lax.rem(self.chip + 1 + i, self.chips)
            pl.semaphore_signal(barrier, inc=1, device_id={"seq": self.peer(k)}, device_id_type=MESH)
            return 0

        lax.fori_loop(0, self.chips - 1, one, 0)
        return self.chips

    def pair_copy(self, k):
        return self.copy(self.s_ref.at[self.band(k), self.lanes(1 - self.core)], self.pair.at[k],
                         self.ps.at[k], self.pr.at[k], self.sibling())

    def thr_pair_copy(self):
        return self.copy(self.thr_ref, self.thr_pair, self.qs, self.qr, self.sibling())

    def thr_copy(self, k, slot):
        return self.copy(self.thr_own, self.thr_buf.at[slot], self.ts.at[k], self.tr.at[slot], self.peer(k))

    def chunk_copy(self, k, slot):
        return self.copy(self.mine.at[k], self.recv.at[slot], self.ss.at[k], self.sr.at[slot], self.peer(k))

    def back_copy(self, k, slot):
        return self.copy(self.stage.at[k], self.back.at[slot], self.bs.at[k], self.br.at[slot], self.peer(k))

    def give_copy(self, k, core):
        return self.copy(self.give.at[k], self.out_ref.at[self.band(k), self.lanes(core)], self.gs.at[k], self.gr.at[k],
                         self.sibling())

    def begin(self):
        self.thr_pair_copy().start()

        def one(i, _):
            self.pair_copy(lax.rem(self.chip + 1 + i, self.chips)).start()
            return 0

        lax.fori_loop(0, self.chips, one, 0)

    def exchange(self):
        first = 1 if self.reverse else 0
        self.thr_pair_copy().wait_recv()
        mine_first = self.core == first
        thr_first = jnp.where(mine_first, self.thr_ref[...], self.thr_pair[...])
        thr_second = jnp.where(mine_first, self.thr_pair[...], self.thr_ref[...])
        self.thr_own[...] = thr_first * thr_second
        self.thr_buf[self.chip] = thr_first * thr_second

        def tell(i, _):
            self.thr_copy(lax.rem(self.chip + 1 + i, self.chips), self.chip).start()
            return 0

        lax.fori_loop(0, self.chips - 1, tell, 0)
        both = jnp.concatenate([thr_first, thr_second], axis=0)
        wide = jnp.dot(both, self.spread_ref[:, self.lanes(self.core)].astype(jnp.float32), precision=HIGHEST,
                       preferred_element_type=jnp.float32)
        self.first_wide[...] = wide[0:8]
        second_wide = wide[8:16]

        def one(i, _):
            k = lax.rem(self.chip + 1 + i, self.chips)
            self.pair_copy(k).wait_recv()
            own = self.s_ref[self.band(k), self.lanes(self.core)]
            other = self.pair[k]
            early = jnp.where(mine_first, own, other)
            late = jnp.where(mine_first, other, own)
            self.mine[k] = second_wide * early + late

            @pl.when(k != self.chip)
            def _():
                self.chunk_copy(k, self.chip).start()

            return 0

        lax.fori_loop(0, self.chips, one, 0)
        self.recv[self.chip] = self.mine[self.chip]

    def hops(self):
        def arrive(i, _):
            self.thr_copy(self.chip, lax.rem(self.chip + 1 + i, self.chips)).wait_recv()
            return 0

        lax.fori_loop(0, self.chips - 1, arrive, 0)
        self.thr_wide[...] = jnp.dot(self.thr_buf[:, 0, :], self.spread_ref[:, self.lanes(self.core)].astype(jnp.float32),
                                     precision=HIGHEST, preferred_element_type=jnp.float32)

        def hop(i, state):
            j = self.chips - 1 - i if self.reverse else i

            @pl.when(j != self.chip)
            def _():
                self.chunk_copy(self.chip, j).wait_recv()

            self.stage[j] = state

            @pl.when(j != self.chip)
            def _():
                self.back_copy(j, self.chip).start()

            return self.thr_wide[pl.ds(j, 1), :] * state + self.recv[j]

        lax.fori_loop(0, self.chips, hop, jnp.zeros((self.rows, self.half), jnp.float32))
        self.back[self.chip] = self.stage[self.chip]

    def deliver(self):
        mine_first = self.core == (1 if self.reverse else 0)

        def one(i, _):
            k = lax.rem(self.chip + i, self.chips)

            @pl.when(k != self.chip)
            def _():
                self.back_copy(self.chip, k).wait_recv()
                self.chunk_copy(k, self.chip).wait_send()

            early = self.back[k]
            own = self.s_ref[self.band(k), self.lanes(self.core)]
            late = self.first_wide[...] * early + jnp.where(mine_first, own, self.pair[k])
            self.out_ref[self.band(k), self.lanes(self.core)] = jnp.where(mine_first, early, late)
            self.give[k] = jnp.where(mine_first, late, early)
            self.give_copy(k, self.core).start()
            return 0

        lax.fori_loop(0, self.chips, one, 0)

        def got(k, _):
            self.give_copy(k, 1 - self.core).wait_recv()
            return 0

        lax.fori_loop(0, self.chips, got, 0)

    def finish(self):
        self.thr_pair_copy().wait_send()

        def one(i, _):
            k = lax.rem(self.chip + 1 + i, self.chips)
            self.pair_copy(k).wait_send()
            self.give_copy(k, self.core).wait_send()

            @pl.when(k != self.chip)
            def _():
                self.thr_copy(k, self.chip).wait_send()
                self.back_copy(k, self.chip).wait_send()

            return 0

        lax.fori_loop(0, self.chips, one, 0)


def scan_scratch(n, ns, width):
    chips = n // 2
    chunk = pltpu.VMEM((chips, ns // chips, width // 2), jnp.float32)
    tile = pltpu.VMEM((8, 128), jnp.float32)
    return [chunk] * 3 + [
        tile,
        tile,
        tile,
        pltpu.VMEM((chips, 8, 128), jnp.float32),
        pltpu.VMEM((chips, width // 2), jnp.float32),
        pltpu.VMEM((8, width // 2), jnp.float32),
    ] + [pltpu.SemaphoreType.DMA((chips,))] * 10 + [pltpu.SemaphoreType.DMA] * 2


SCAN_SCRATCH = 9 + 12


def make_scan(n, reverse, s_ref, spread_ref, out_ref, shared, scratch):
    mine, stage = shared
    give = mine
    pair, recv, back, thr_ref = scratch[:4]
    return Scan(n, reverse, s_ref, thr_ref, spread_ref, out_ref, pair, mine, recv, stage, back, give,
                *scratch[4:9], scratch[9:])


ORDERS = ((2, 1, 0), (1, 0, 2), (0, 2, 1))


class Ring:
    def __init__(self, og_ref, og_wide, nt_own, nt_send, out_ref, small, small_out, part, nt_got, og_got, og_theirs, agg1, full1, agg2, full2,
                 agg3, full3, slots_c, slots_a, total, sems):
        (self.cs, self.cr, self.ns, self.nr, self.rs, self.rr, self.xs, self.xr, self.ms, self.mr) = sems
        self.xi = lax.axis_index("dp")
        s = lax.axis_index("seq")
        self.core = lax.rem(s, 2)
        self.here = (lax.div(s, 8), lax.rem(lax.div(s, 2), 4), self.xi)
        self.sibling = {"seq": s + 1 - 2 * self.core}
        self.og_ref, self.og_wide, self.nt_own, self.nt_send = og_ref, og_wide, nt_own, nt_send
        self.out_ref = out_ref
        self.small, self.small_out = small, small_out
        self.part, self.nt_got, self.og_got, self.og_theirs = part, nt_got, og_got, og_theirs
        self.bufs = ((agg1, full1), (agg2, full2), (agg3, full3))
        self.slots_c, self.slots_a, self.total = slots_c, slots_a, total
        self.third = part.shape[-1] // 3
        self.half = self.third // 2
        self.started = []
        self.steps = {}

    def at(self, axis, index):
        if axis == 2:
            return {"dp": index}
        z, y = (index, self.here[1]) if axis == 0 else (self.here[0], index)
        return {"seq": (z * 4 + y) * 2 + self.core}

    def remote(self, src, dst, ss, rs, to):
        return pltpu.make_async_remote_copy(src_ref=src, dst_ref=dst, send_sem=ss, recv_sem=rs,
                                            device_id=to, device_id_type=MESH)

    def start(self, copies):
        for c in copies:
            c.start()
        self.started += copies
        return copies

    def og_begin(self):
        self.og_wide[...] = self.og_ref[...].astype(jnp.float32)
        self.og_copy = self.remote(self.og_wide, self.og_got, self.cs.at[0], self.cr.at[0], self.sibling)
        self.og_copy.start()

    def nt_copy(self, i, count):
        here = pl.ds(i * count, count)
        return self.remote(self.nt_send.at[here], self.nt_got.at[here], self.ns.at[i], self.nr.at[i], self.sibling)

    def og_end(self):
        self.og_copy.wait_recv()
        self.og_theirs[...] = self.og_got[...].astype(jnp.bfloat16)

    def product(self, parts):
        def got(i, _):
            self.nt_copy(i, 16 // parts).wait_recv()
            return 0

        lax.fori_loop(0, parts, got, 0)

        def one(b, _):
            z, y = lax.div(b, 4), lax.rem(b, 4)
            sums = bdot(self.nt_own[b], self.og_ref[...], 1, 0)
            sums += bdot(self.nt_got[b].astype(jnp.bfloat16), self.og_theirs[...], 1, 0)
            self.part[z, y] = sums.reshape(self.part.shape[2:])
            return 0

        lax.fori_loop(0, 16, one, 0)

    def region(self, step, p, t, h=None):
        order = ORDERS[p]
        index = [slice(None)] * 3
        for done in order[:step]:
            index[done] = self.here[done]
        index[order[step]] = t
        lo = p * self.third + (0 if h in (None, 0) else self.half)
        return (*index, slice(None), pl.ds(lo, self.third if h is None else self.half))

    def ways(self, step, p):
        axis = ORDERS[p][step]
        me = self.here[axis]
        return axis, lax.rem(me + 1, 4), lax.rem(me + 3, 4), lax.rem(me + 2, 4)

    def begin(self, step):
        agg, full = self.bufs[step]
        first, second, last = [], [], []
        lo, hi = pl.ds(0, self.half), pl.ds(self.half, self.half)
        for p in range(3):
            axis, up, down, far = self.ways(step, p)

            def go(t, h, dst, k, to):
                return self.remote(self.part.at[self.region(step, p, t, h)], dst, self.rs.at[step, p, k],
                                   self.rr.at[step, p, k], self.at(axis, to))

            first.append([go(far, 0, agg.at[p, 0], 0, up), go(far, 1, agg.at[p, 1], 1, down)])
            second.append([go(up, 1, full.at[p, 0, ..., hi], 2, up), go(down, 0, full.at[p, 1, ..., lo], 3, down)])
            last.append([go(up, 0, full.at[p, 0, ..., lo], 4, up), go(down, 1, full.at[p, 1, ..., hi], 5, down)])
        for p in range(3):
            self.start(first[p])
        for p in range(3):
            self.start(second[p])
        self.steps[step] = (first, second, last)

    def middle(self, step):
        agg, _ = self.bufs[step]
        first, _, last = self.steps[step]
        for p in range(3):
            _, up, down, _ = self.ways(step, p)
            first[p][0].wait_recv()
            self.part[self.region(step, p, up, 0)] += agg[p, 0]
            self.start([last[p][0]])
            first[p][1].wait_recv()
            self.part[self.region(step, p, down, 1)] += agg[p, 1]
            self.start([last[p][1]])

    def end(self, step):
        _, full = self.bufs[step]
        _, second, last = self.steps[step]
        for p in range(3):
            for c in second[p] + last[p]:
                c.wait_recv()
            here = self.region(step, p, self.here[ORDERS[p][step]])
            self.part[here] += full[p, 0] + full[p, 1]

    def small_pair_begin(self):
        self.small_pair = self.start([
            self.remote(self.small, self.slots_c.at[self.core], self.cs.at[2], self.cr.at[2], self.sibling)])
        self.slots_c[self.core] = self.small[...]

    def small_pair_end(self):
        self.small_pair[0].wait_recv()
        self.total[0] = self.slots_c[0] + self.slots_c[1]

    def small_begin(self, k):
        axis = (2, 1, 0)[k]
        me = self.here[axis]
        self.smalls = self.start([
            self.remote(self.total.at[k], self.slots_a.at[k, me], self.ms.at[k, d - 1], self.mr.at[k, d - 1],
                        self.at(axis, lax.rem(me + d, 4)))
            for d in (1, 2, 3)])
        self.slots_a[k, me] = self.total[k]

    def small_end(self, k):
        for c in self.smalls:
            c.wait_recv()
        now = (self.slots_a[k, 0] + self.slots_a[k, 1]) + (self.slots_a[k, 2] + self.slots_a[k, 3])
        if k < 2:
            self.total[k + 1] = now
        else:
            self.small_out[...] = now

    def share_begin(self):
        z, y, x = self.here
        self.out_ref[x] = self.part[z, y, x]
        self.start([
            self.remote(self.out_ref.at[x], self.out_ref.at[x], self.xs.at[d - 1], self.xr.at[d - 1],
                        {"dp": lax.rem(x + d, 4)})
            for d in (1, 2, 3)])

    def share_end(self):
        for d in (1, 2, 3):
            came = lax.rem(self.xi + 4 - d, 4)
            self.remote(self.out_ref.at[came], self.out_ref.at[came], self.xs.at[d - 1], self.xr.at[d - 1],
                        {"dp": came}).wait_recv()

    def finish(self):
        for c in self.started:
            c.wait_send()


def ring_scratch(rows, cols, span, lines):
    f32 = jnp.float32
    quarter, third, half = rows // 4, cols // 3, cols // 6
    return [
        pltpu.VMEM((4, 4, 4, quarter, cols), f32),
        pltpu.VMEM((16, rows, span), f32),
        pltpu.VMEM((span, cols), f32),
        pltpu.VMEM((span, cols), jnp.bfloat16),
        pltpu.VMEM((3, 2, 4, 4, quarter, half), f32),
        pltpu.VMEM((3, 2, 4, 4, quarter, third), f32),
        pltpu.VMEM((3, 2, 4, quarter, half), f32),
        pltpu.VMEM((3, 2, 4, quarter, third), f32),
        pltpu.VMEM((3, 2, quarter, half), f32),
        pltpu.VMEM((3, 2, quarter, third), f32),
        pltpu.VMEM((2, lines, 128), f32),
        pltpu.VMEM((3, 4, lines, 128), f32),
        pltpu.VMEM((3, lines, 128), f32),
        pltpu.SemaphoreType.DMA((3,)),
        pltpu.SemaphoreType.DMA((3,)),
        pltpu.SemaphoreType.DMA((8,)),
        pltpu.SemaphoreType.DMA((8,)),
        pltpu.SemaphoreType.DMA((3, 3, 6)),
        pltpu.SemaphoreType.DMA((3, 3, 6)),
        pltpu.SemaphoreType.DMA((3,)),
        pltpu.SemaphoreType.DMA((3,)),
        pltpu.SemaphoreType.DMA((3, 3)),
        pltpu.SemaphoreType.DMA((3, 3)),
    ]


BLOCK = 384
TAIL, LEAD, SKIP, THROUGH = range(4)


def softplus(v):
    return jnp.maximum(v, 0.0) + jnp.log1p(jnp.exp(-jnp.abs(v)))


def mixer_kernel(n, x_ref, z_ref, b_ref, c_ref, logit_in, og_ref, bias_in, rate_in, skip_in, gain_ref,
                 resets_ref, w_hbm,
                 w_out, small_out, dx_out, dz_out, db_out, dc_out, dlogit_out, mixed_out, *scratch):
    (dn, u, normed, s_buf, inc, sg, s_in, spread, lanes, w_buf, gm_hi, gm_lo, gt_hi, gt_lo, mask_ref, bk, bkt, co, cot,
     e_ref, f_ref, step_ref, sig_ref, keep_ref, open_ref, ms_acc, m2_acc, dg_acc, dc_acc, db_acc, a_acc, b_acc,
     skip_acc, end_acc, small, nt_own, nt_send, og_wide, mine, stage, par_ref, w_sem) = scratch[:42]
    rest = scratch[42:]
    ahead = make_scan(n, False, s_buf, spread, inc, (mine, stage), rest[:SCAN_SCRATCH])
    behind = make_scan(n, True, sg, spread, inc, (mine, stage), rest[SCAN_SCRATCH : 2 * SCAN_SCRATCH])
    rest = rest[2 * SCAN_SCRATCH :]
    ring = Ring(og_ref, og_wide, nt_own, nt_send, w_out, small, small_out, *rest[:13], rest[13:])
    f32, bf16 = jnp.float32, jnp.bfloat16
    span, width = x_ref.shape
    blocks = width // BLOCK

    def w_copy(i):
        slot = lax.rem(i, 2)
        return pltpu.make_async_copy(w_hbm.at[pl.ds(i * BLOCK, BLOCK)], w_buf.at[slot], w_sem.at[slot])

    barrier = pltpu.get_barrier_semaphore()
    count = ahead.greet(barrier)
    for d in (1, 2, 3):
        pl.semaphore_signal(barrier, inc=1, device_id={"dp": lax.rem(ring.xi + d, 4)}, device_id_type=MESH)
    w_copy(0).start()

    start = lax.axis_index("seq") * span
    ri = lax.broadcasted_iota(jnp.int32, (span, span), 0)
    ci = lax.broadcasted_iota(jnp.int32, (span, span), 1)
    flag_c = jnp.zeros((span, span), f32)
    flag_r = jnp.zeros((span, span), f32)
    for k in range(resets_ref.shape[1]):
        at_reset = resets_ref[0:1, k : k + 1] - start
        flag_c = jnp.where(ci == at_reset, 1.0, flag_c)
        flag_r = jnp.where(ri == at_reset, 1.0, flag_r)
    count_col = jnp.sum(jnp.where(ri >= ci, flag_c, 0.0), axis=1, keepdims=True)
    count_row = jnp.sum(jnp.where(ri <= ci, flag_r, 0.0), axis=0, keepdims=True)
    all_col = jnp.sum(flag_c, axis=1, keepdims=True)
    all_row = jnp.sum(flag_r, axis=0, keepdims=True)
    below = jnp.where(ri >= ci, 1.0, 0.0)
    mask = jnp.where((ri >= ci) & (count_col == count_row), 1.0, 0.0)
    mask_ref[...] = mask
    keep = jnp.where(count_col == all_col, 1.0, 0.0)
    opened = jnp.where(count_col == 0.0, 1.0, 0.0)
    keep_ref[...] = jnp.broadcast_to(keep, keep_ref.shape)
    open_ref[...] = jnp.broadcast_to(opened, open_ref.shape)
    b_keep = b_ref[...].astype(f32) * keep
    c_open = c_ref[...].astype(f32) * opened
    bk[...] = b_keep.astype(bf16)
    bkt[...] = b_keep.T.astype(bf16)
    co[...] = c_open.astype(bf16)
    cot[...] = c_open.T.astype(bf16)
    gm = bdot(c_ref[...], b_ref[...], 1, 1) * mask
    gm_hi[...], gm_lo[...] = split(gm)
    gt_hi[...], gt_lo[...] = split(gm.T)
    heads = logit_in.shape[1]
    sig_ref[...] = jnp.zeros_like(sig_ref)
    sig_ref[:, 0:heads] = logit_in[...].astype(f32)
    par_ref[...] = jnp.zeros_like(par_ref)
    par_ref[0:1, 0:heads] = bias_in[...]
    par_ref[1:2, 0:heads] = rate_in[...]
    par_ref[2:3, 0:heads] = skip_in[...]
    raw = sig_ref[...] + par_ref[0:1]
    step = softplus(raw)
    step_ref[...] = step
    sig_ref[...] = jax.nn.sigmoid(raw)
    cum = jnp.dot(below, -par_ref[1:2] * step, precision=HIGHEST, preferred_element_type=f32)
    last = cum[span - 1 : span]
    mid = cum[span // 2 : span // 2 + 1]
    through = jnp.where(all_row[:, :128] == 0.0, jnp.exp(last), 0.0)
    e_ref[...] = jnp.exp(cum - mid)
    f_ref[...] = step * jnp.exp(mid - cum)
    thr = jnp.broadcast_to(through, (8, 128))
    ahead.thr_ref[...] = thr
    behind.thr_ref[...] = thr
    head_of = lax.broadcasted_iota(jnp.int32, spread.shape, 1) >> 6
    spread[...] = jnp.where(lax.broadcasted_iota(jnp.int32, spread.shape, 0) == head_of, 1.0, 0.0).astype(bf16)
    per_head = jnp.concatenate(
        [jnp.exp(last - mid), jnp.exp(mid), par_ref[2:3], through, jnp.zeros((4, 128), f32)], axis=0)
    lanes[...] = jnp.dot(per_head, spread[...].astype(f32), precision=HIGHEST, preferred_element_type=f32)
    for acc in (ms_acc, m2_acc, dg_acc, dc_acc, db_acc, a_acc, b_acc, skip_acc, end_acc, small):
        acc[...] = jnp.zeros_like(acc)

    def block(i):
        return pl.ds(pl.multiple_of(i * BLOCK, 128), BLOCK)

    def every(body):
        def one(i, _):
            body(i, block(i))
            return 0

        lax.fori_loop(0, blocks, one, 0)

    def e_of(at):
        return dot2(split(e_ref[...]), spread[:, at], 1, 0)

    def f_of(at):
        return dot2(split(f_ref[...]), spread[:, at], 1, 0)

    def row(k, at):
        return lanes[k : k + 1, at]

    def own_state(i, at):
        fx2 = split(f_of(at) * x_ref[:, at].astype(f32))
        s_buf[:, at] = row(TAIL, at) * dot2(bkt[...], fx2, 1, 0)

    def in_span(i, at):
        fx2 = split(f_of(at) * x_ref[:, at].astype(f32))
        u[:, at] = dot2((gm_hi[...], gm_lo[...]), fx2, 1, 0)

    def project_back(i, at):
        w_copy(i).wait()

        @pl.when(i + 1 < blocks)
        def _():
            w_copy(i + 1).start()

        dn[:, at] = bdot(og_ref[...], w_buf[lax.rem(i, 2)], 1, 1)

    def read_out(i, at):
        before = inc[:, at]
        s2 = split(row(LEAD, at) * before)
        s_in[:, at] = s2[0]
        s_buf[:, at] = row(THROUGH, at) * before + s_buf[:, at]
        now = u[:, at] + dot2(co[...], s2, 1, 0)
        u[:, at] = now
        y = e_of(at) * now + row(SKIP, at) * x_ref[:, at].astype(f32)
        zf = z_ref[:, at].astype(f32)
        g = y * (zf * jax.nn.sigmoid(zf))
        ms_acc[...] += jnp.broadcast_to(jnp.sum(g * g, axis=1, keepdims=True), ms_acc.shape)
        m2_acc[...] += jnp.broadcast_to(
            jnp.sum(dn[:, at] * gain_ref[0:1, at] * g, axis=1, keepdims=True), m2_acc.shape)

    def norm(i, at):
        e = e_of(at)
        y = e * u[:, at] + row(SKIP, at) * x_ref[:, at].astype(f32)
        zf = z_ref[:, at].astype(f32)
        sig = jax.nn.sigmoid(zf)
        silu = zf * sig
        r = lax.rsqrt(ms_acc[:, 0:1] * (1.0 / width) + 1e-05)
        ghat = y * silu * r
        gain = gain_ref[0:1, at]
        out = ghat * gain
        out_low = out.astype(bf16)
        normed[:, at] = out_low
        up = out_low.astype(f32).T.reshape(BLOCK // 192, 2, 96, span)
        here = pl.ds(i * (BLOCK // 192), BLOCK // 192)
        even = ring.core == 0
        nt_own[here] = jnp.where(even, up[:, 0], up[:, 1]).astype(bf16)
        nt_send[here] = jnp.where(even, up[:, 1], up[:, 0])
        ring.nt_copy(i, BLOCK // 192).start()
        d = dn[:, at]
        sums = jnp.sum(d * ghat, axis=0, keepdims=True)
        for k in range(BLOCK // 128):
            small[pl.ds(i * (BLOCK // 128) + k, 1)] = sums[:, k * 128 : (k + 1) * 128]
        dg = r * (d * gain - ghat * (r * m2_acc[:, 0:1] * (1.0 / width)))
        dy = dg * silu
        dz_out[:, at] = (dg * y * (sig * (1.0 + zf * (1.0 - sig)))).astype(bf16)
        dn[:, at] = dy
        sg[:, at] = row(LEAD, at) * dot2(cot[...], split(e * dy), 1, 0)

    def pass_one(i, at):
        sp = spread[:, at]
        dy, xb = dn[:, at], x_ref[:, at].astype(f32)
        du = e_of(at) * dy
        fx = (f_of(at) * xb).astype(bf16)
        du2 = split(du)
        b_acc[...] += dot2(split(du * u[:, at]), sp, 1, 1)
        u[:, at] = dot2((gt_hi[...], gt_lo[...]), du2, 1, 0)
        dg_acc[...] += dot2(du2, fx, 1, 1)
        dc_acc[...] += dot2(du2, s_in[:, at], 1, 1)
        line = jnp.broadcast_to(jnp.sum(dy * xb, axis=0, keepdims=True), (8, BLOCK))
        skip_acc[...] += dot2(split(line), sp, 1, 1)

    def pass_two(i, at):
        sp = spread[:, at]
        f = f_of(at)
        fx = f * x_ref[:, at].astype(f32)
        late = inc[:, at]
        ds2 = split(row(TAIL, at) * late)
        d = u[:, at] + dot2(bk[...], ds2, 1, 0)
        dx_out[:, at] = (f * d + row(SKIP, at) * dn[:, at]).astype(bf16)
        a_acc[...] += dot2(split(fx * d), sp, 1, 1)
        db_acc[...] += dot2(fx.astype(bf16), ds2, 1, 1)
        line = jnp.broadcast_to(jnp.sum(late * s_buf[:, at], axis=0, keepdims=True), (8, BLOCK))
        end_acc[...] += dot2(split(line), sp, 1, 1)

    def project(i, at):
        w_copy(i).wait()

        @pl.when(i + 1 < blocks)
        def _():
            w_copy(i + 1).start()

        og_wide[...] += bdot(normed[:, at], w_buf[lax.rem(i, 2)], 1, 0)

    half = blocks // 2
    theirs_first = (1 - ring.core) * half

    def part_of(body, lo):
        def one(i, _):
            k = lax.rem(theirs_first + lo + i, blocks)
            body(k, block(k))
            return 0

        lax.fori_loop(0, half, one, 0)

    part_of(own_state, 0)
    pl.semaphore_wait(barrier, count + 3)
    ahead.begin()
    part_of(own_state, half)
    ahead.exchange()
    ring.og_begin()
    every(project_back)
    ahead.hops()
    every(in_span)
    ring.og_end()
    ahead.deliver()
    ahead.finish()
    every(read_out)
    part_of(norm, 0)
    behind.begin()
    part_of(norm, half)
    behind.exchange()
    ring.product(blocks)
    ring.begin(0)
    behind.hops()
    w_copy(0).start()
    ring.og_copy.wait_send()
    og_wide[...] = jnp.zeros_like(og_wide)
    every(pass_one)
    ring.middle(0)
    every(project)
    mixed_out[...] = og_wide[...].astype(bf16)
    behind.deliver()
    every(pass_two)

    a = a_acc[...]
    upper = jnp.where(ri <= ci, 1.0, 0.0)
    d_decay = jnp.dot(upper, b_acc[...] - a, precision=HIGHEST, preferred_element_type=f32) + end_acc[0:1]
    dlogit = (a / step_ref[...] - par_ref[1:2] * d_decay) * sig_ref[...]
    dlogit_out[...] = dlogit[:, : dlogit_out.shape[1]].astype(bf16)
    lines = width // 128
    small[lines : lines + 1] = jnp.sum(dlogit, axis=0, keepdims=True)
    small[lines + 1 : lines + 2] = jnp.sum(-step_ref[...] * d_decay, axis=0, keepdims=True)
    small[lines + 2 : lines + 3] = skip_acc[0:1]
    ring.small_pair_begin()
    ring.end(0)
    ring.begin(1)
    ring.small_pair_end()
    ring.small_begin(0)
    dg = dg_acc[...] * mask_ref[...]
    dc_out[...] = (dot2(split(dg), b_ref[...], 1, 0) + open_ref[...] * dc_acc[...]).astype(bf16)
    db_out[...] = (dot2(split(dg.T), c_ref[...], 1, 0) + keep_ref[...] * db_acc[...]).astype(bf16)
    ring.middle(1)
    ring.small_end(0)
    ring.small_begin(1)
    ring.end(1)
    ring.begin(2)
    ring.small_end(1)
    ring.small_begin(2)
    ring.middle(2)
    ring.end(2)
    ring.share_begin()
    ring.small_end(2)
    ring.share_end()
    ring.finish()

    def sent(i, _):
        ring.nt_copy(i, BLOCK // 192).wait_send()
        return 0

    lax.fori_loop(0, blocks, sent, 0)
    behind.finish()


def results_kernel(w, sums, dx, dz, db, dc, dlogit, mixed, mixed_to, dx_to, dz_to, db_to, dc_to, dlogit_to,
                   bias_to, rate_to, skip_to, gain_to, w_to, sems):
    pairs = ((dx, dx_to), (dz, dz_to), (mixed, mixed_to), (w, w_to), (db, db_to), (dc, dc_to), (dlogit, dlogit_to))
    copies = [pltpu.make_async_copy(a, b, sems.at[k]) for k, (a, b) in enumerate(pairs)]
    for c in copies:
        c.start()
    lines, heads = gain_to.shape[0], bias_to.shape[1]
    gain_to[...] = sums[0:lines]
    bias_to[...] = sums[lines : lines + 1, 0:heads]
    rate_to[...] = sums[lines + 1 : lines + 2, 0:heads]
    skip_to[...] = sums[lines + 2 : lines + 3, 0:heads]
    for c in copies:
        c.wait()


def per_device(n, ssm_input, gate_input, input_map, output_map, step_logit, step_bias, decay_rate, skip_gain,
               norm_gain, out_weight, resets, out_grad):
    f32, bf16 = jnp.float32, jnp.bfloat16
    _, span, width = ssm_input.shape
    ns, heads, cols = input_map.shape[2], step_bias.shape[0], out_weight.shape[1]
    rows, lines = width // 32, width // 128 + 8
    vmem = pl.BlockSpec(memory_space=pltpu.VMEM)

    def wide(*shape):
        return pltpu.VMEM(shape, f32)

    def low(*shape):
        return pltpu.VMEM(shape, bf16)

    chunk = wide(n // 2, ns // (n // 2), width // 2)
    weight_grad, sums, dx, dz, db, dc, dlogit, mixed = pl.pallas_call(
        functools.partial(mixer_kernel, n),
        out_shape=(
            jax.ShapeDtypeStruct((4, rows // 4, cols), f32),
            jax.ShapeDtypeStruct((lines, 128), f32),
            jax.ShapeDtypeStruct((span, width), bf16),
            jax.ShapeDtypeStruct((span, width), bf16),
            jax.ShapeDtypeStruct((span, ns), bf16),
            jax.ShapeDtypeStruct((span, ns), bf16),
            jax.ShapeDtypeStruct((span, heads), bf16),
            jax.ShapeDtypeStruct((span, cols), bf16),
        ),
        in_specs=[vmem] * 11 + [pl.BlockSpec(memory_space=pl.ANY)],
        out_specs=(vmem,) * 8,
        scratch_shapes=[
            wide(span, width), wide(span, width), low(span, width), wide(ns, width), wide(ns, width), wide(ns, width),
            low(ns, width), low(128, width), wide(8, width), low(2, BLOCK, cols),
            low(span, span), low(span, span), low(span, span), low(span, span), wide(span, span),
            low(span, ns), low(ns, span), low(span, ns), low(ns, span),
            wide(span, 128), wide(span, 128), wide(span, 128), wide(span, 128), wide(span, ns), wide(span, ns),
            wide(span, 128), wide(span, 128), wide(span, span), wide(span, ns), wide(span, ns),
            wide(span, 128), wide(span, 128), wide(8, 128), wide(8, 128), wide(lines, 128),
            low(16, rows, span), wide(16, rows, span), wide(span, cols), chunk, chunk,
            wide(8, 128),
            pltpu.SemaphoreType.DMA((2,)),
        ] + scan_scratch(n, ns, width) * 2 + ring_scratch(rows, cols, span, lines),
        compiler_params=pltpu.CompilerParams(
            collective_id=1, has_side_effects=True, vmem_limit_bytes=VMEM_LIMIT),
        name="mixer",
    )(ssm_input[0], gate_input[0], input_map[0], output_map[0], step_logit[0], out_grad[0], step_bias[None],
      decay_rate[None], skip_gain[None], norm_gain[None], resets, out_weight)
    anywhere = pl.BlockSpec(memory_space=pl.ANY)
    shapes = [(v.shape, bf16) for v in (mixed, dx, dz, db, dc, dlogit)] + [((1, heads), f32)] * 3
    shapes += [((width // 128, 128), f32), (weight_grad.shape, f32)]
    out = pl.pallas_call(
        results_kernel,
        out_shape=tuple(jax.ShapeDtypeStruct(*v) for v in shapes),
        in_specs=[anywhere, vmem] + [anywhere] * 6,
        out_specs=(anywhere,) * 6 + (vmem,) * 4 + (anywhere,),
        scratch_shapes=[pltpu.SemaphoreType.DMA((7,))],
        name="results",
    )(weight_grad, sums, dx, dz, db, dc, dlogit, mixed)
    return (
        *(v[None] for v in out[:6]),
        *(v.reshape(-1) for v in out[6:10]),
        out[10].reshape(rows, cols),
    )


def solution(mesh):
    by_rows = P("dp", "seq", None)
    return jax.shard_map(
        functools.partial(per_device, mesh.shape["seq"]),
        mesh=mesh,
        in_specs=(by_rows,) * 5 + (P(),) * 5 + (P("dp", None), by_rows),
        out_specs=(by_rows,) * 6 + (P(),) * 4 + (P("seq", None),),
        check_vma=False,
    )
```

```python
import functools

import jax
import jax.numpy as jnp
from jax import lax
from jax.experimental import pallas as pl
from jax.experimental.pallas import tpu as pltpu
from jax.sharding import PartitionSpec as P

MESH = pl.DeviceIdType.MESH
HIGHEST = lax.Precision.HIGHEST
VMEM_LIMIT = 63 * 1024 * 1024


def bdot(a, b, ca, cb):
    return lax.dot_general(
        a, b, (((ca,), (cb,)), ((), ())), preferred_element_type=jnp.float32
    )


def split(v):
    hi = v.astype(jnp.bfloat16)
    return hi, (v - hi.astype(jnp.float32)).astype(jnp.bfloat16)


def dot2(a, b, ca, cb):
    if isinstance(a, tuple) and isinstance(b, tuple):
        return bdot(a[0], b[0], ca, cb) + (bdot(a[0], b[1], ca, cb) + bdot(a[1], b[0], ca, cb))
    if isinstance(a, tuple):
        return bdot(a[0], b, ca, cb) + bdot(a[1], b, ca, cb)
    if isinstance(b, tuple):
        return bdot(a, b[0], ca, cb) + bdot(a, b[1], ca, cb)
    return bdot(a, b, ca, cb)


class Scan:
    def __init__(self, n, reverse, s_ref, thr_ref, spread_ref, out_ref, pair, mine, recv, stage, back, give,
                 thr_pair, thr_own, thr_buf, thr_wide, first_wide, sems):
        me = lax.axis_index("seq")
        self.chips, self.reverse = n // 2, reverse
        self.core, self.chip = lax.rem(me, 2), lax.div(me, 2)
        self.s_ref, self.thr_ref, self.spread_ref, self.out_ref = s_ref, thr_ref, spread_ref, out_ref
        self.pair, self.mine, self.recv, self.stage, self.back, self.give = pair, mine, recv, stage, back, give
        self.thr_pair, self.thr_own, self.thr_buf = thr_pair, thr_own, thr_buf
        self.thr_wide, self.first_wide = thr_wide, first_wide
        (self.ps, self.pr, self.ss, self.sr, self.ts, self.tr, self.bs, self.br, self.gs, self.gr, self.qs, self.qr) = sems
        ns, width = s_ref.shape
        self.rows, self.half = ns // self.chips, width // 2

    def lanes(self, core):
        return pl.ds(pl.multiple_of(core * self.half, 128), self.half)

    def band(self, k):
        return pl.ds(pl.multiple_of(k * self.rows, 8), self.rows)

    def copy(self, src, dst, ss, rs, to):
        return pltpu.make_async_remote_copy(src_ref=src, dst_ref=dst, send_sem=ss, recv_sem=rs,
                                            device_id={"seq": to}, device_id_type=MESH)

    def sibling(self):
        return self.chip * 2 + 1 - self.core

    def peer(self, k):
        return k * 2 + self.core

    def greet(self, barrier):
        pl.semaphore_signal(barrier, inc=1, device_id={"seq": self.sibling()}, device_id_type=MESH)

        def one(i, _):
            k = lax.rem(self.chip + 1 + i, self.chips)
            pl.semaphore_signal(barrier, inc=1, device_id={"seq": self.peer(k)}, device_id_type=MESH)
            return 0

        lax.fori_loop(0, self.chips - 1, one, 0)
        return self.chips

    def pair_copy(self, k):
        return self.copy(self.s_ref.at[self.band(k), self.lanes(1 - self.core)], self.pair.at[k],
                         self.ps.at[k], self.pr.at[k], self.sibling())

    def thr_pair_copy(self):
        return self.copy(self.thr_ref, self.thr_pair, self.qs, self.qr, self.sibling())

    def thr_copy(self, k, slot):
        return self.copy(self.thr_own, self.thr_buf.at[slot], self.ts.at[k], self.tr.at[slot], self.peer(k))

    def chunk_copy(self, k, slot):
        return self.copy(self.mine.at[k], self.recv.at[slot], self.ss.at[k], self.sr.at[slot], self.peer(k))

    def back_copy(self, k, slot):
        return self.copy(self.stage.at[k], self.back.at[slot], self.bs.at[k], self.br.at[slot], self.peer(k))

    def give_copy(self, k, core):
        return self.copy(self.give.at[k], self.out_ref.at[self.band(k), self.lanes(core)], self.gs.at[k], self.gr.at[k],
                         self.sibling())

    def begin(self):
        self.thr_pair_copy().start()

        def one(i, _):
            self.pair_copy(lax.rem(self.chip + 1 + i, self.chips)).start()
            return 0

        lax.fori_loop(0, self.chips, one, 0)

    def exchange(self):
        first = 1 if self.reverse else 0
        self.thr_pair_copy().wait_recv()
        mine_first = self.core == first
        thr_first = jnp.where(mine_first, self.thr_ref[...], self.thr_pair[...])
        thr_second = jnp.where(mine_first, self.thr_pair[...], self.thr_ref[...])
        self.thr_own[...] = thr_first * thr_second
        self.thr_buf[self.chip] = thr_first * thr_second

        def tell(i, _):
            self.thr_copy(lax.rem(self.chip + 1 + i, self.chips), self.chip).start()
            return 0

        lax.fori_loop(0, self.chips - 1, tell, 0)
        both = jnp.concatenate([thr_first, thr_second], axis=0)
        wide = jnp.dot(both, self.spread_ref[:, self.lanes(self.core)].astype(jnp.float32), precision=HIGHEST,
                       preferred_element_type=jnp.float32)
        self.first_wide[...] = wide[0:8]
        second_wide = wide[8:16]

        def one(i, _):
            k = lax.rem(self.chip + 1 + i, self.chips)
            self.pair_copy(k).wait_recv()
            own = self.s_ref[self.band(k), self.lanes(self.core)]
            other = self.pair[k]
            early = jnp.where(mine_first, own, other)
            late = jnp.where(mine_first, other, own)
            self.mine[k] = second_wide * early + late

            @pl.when(k != self.chip)
            def _():
                self.chunk_copy(k, self.chip).start()

            return 0

        lax.fori_loop(0, self.chips, one, 0)
        self.recv[self.chip] = self.mine[self.chip]

    def hops(self):
        def arrive(i, _):
            self.thr_copy(self.chip, lax.rem(self.chip + 1 + i, self.chips)).wait_recv()
            return 0

        lax.fori_loop(0, self.chips - 1, arrive, 0)
        self.thr_wide[...] = jnp.dot(self.thr_buf[:, 0, :], self.spread_ref[:, self.lanes(self.core)].astype(jnp.float32),
                                     precision=HIGHEST, preferred_element_type=jnp.float32)

        def hop(i, state):
            j = self.chips - 1 - i if self.reverse else i

            @pl.when(j != self.chip)
            def _():
                self.chunk_copy(self.chip, j).wait_recv()

            self.stage[j] = state

            @pl.when(j != self.chip)
            def _():
                self.back_copy(j, self.chip).start()

            return self.thr_wide[pl.ds(j, 1), :] * state + self.recv[j]

        lax.fori_loop(0, self.chips, hop, jnp.zeros((self.rows, self.half), jnp.float32))
        self.back[self.chip] = self.stage[self.chip]

    def deliver(self):
        mine_first = self.core == (1 if self.reverse else 0)

        def one(i, _):
            k = lax.rem(self.chip + i, self.chips)

            @pl.when(k != self.chip)
            def _():
                self.back_copy(self.chip, k).wait_recv()
                self.chunk_copy(k, self.chip).wait_send()

            early = self.back[k]
            own = self.s_ref[self.band(k), self.lanes(self.core)]
            late = self.first_wide[...] * early + jnp.where(mine_first, own, self.pair[k])
            self.out_ref[self.band(k), self.lanes(self.core)] = jnp.where(mine_first, early, late)
            self.give[k] = jnp.where(mine_first, late, early)
            self.give_copy(k, self.core).start()
            return 0

        lax.fori_loop(0, self.chips, one, 0)

        def got(k, _):
            self.give_copy(k, 1 - self.core).wait_recv()
            return 0

        lax.fori_loop(0, self.chips, got, 0)

    def finish(self):
        self.thr_pair_copy().wait_send()

        def one(i, _):
            k = lax.rem(self.chip + 1 + i, self.chips)
            self.pair_copy(k).wait_send()
            self.give_copy(k, self.core).wait_send()

            @pl.when(k != self.chip)
            def _():
                self.thr_copy(k, self.chip).wait_send()
                self.back_copy(k, self.chip).wait_send()

            return 0

        lax.fori_loop(0, self.chips, one, 0)


def scan_scratch(n, ns, width):
    chips = n // 2
    chunk = pltpu.VMEM((chips, ns // chips, width // 2), jnp.float32)
    tile = pltpu.VMEM((8, 128), jnp.float32)
    return [chunk] * 3 + [
        tile,
        tile,
        tile,
        pltpu.VMEM((chips, 8, 128), jnp.float32),
        pltpu.VMEM((chips, width // 2), jnp.float32),
        pltpu.VMEM((8, width // 2), jnp.float32),
    ] + [pltpu.SemaphoreType.DMA((chips,))] * 10 + [pltpu.SemaphoreType.DMA] * 2


SCAN_SCRATCH = 9 + 12


def make_scan(n, reverse, s_ref, spread_ref, out_ref, shared, scratch):
    mine, stage = shared
    give = mine
    pair, recv, back, thr_ref = scratch[:4]
    return Scan(n, reverse, s_ref, thr_ref, spread_ref, out_ref, pair, mine, recv, stage, back, give,
                *scratch[4:9], scratch[9:])


ORDERS = ((2, 1, 0), (1, 0, 2), (0, 2, 1))


class Ring:
    def __init__(self, og_ref, og_wide, nt_own, nt_send, out_ref, small, small_out, part, nt_got, og_got, og_theirs, agg1, full1, agg2, full2,
                 agg3, full3, slots_c, slots_a, total, sems):
        (self.cs, self.cr, self.ns, self.nr, self.rs, self.rr, self.xs, self.xr, self.ms, self.mr) = sems
        self.xi = lax.axis_index("dp")
        s = lax.axis_index("seq")
        self.core = lax.rem(s, 2)
        self.here = (lax.div(s, 8), lax.rem(lax.div(s, 2), 4), self.xi)
        self.sibling = {"seq": s + 1 - 2 * self.core}
        self.og_ref, self.og_wide, self.nt_own, self.nt_send = og_ref, og_wide, nt_own, nt_send
        self.out_ref = out_ref
        self.small, self.small_out = small, small_out
        self.part, self.nt_got, self.og_got, self.og_theirs = part, nt_got, og_got, og_theirs
        self.bufs = ((agg1, full1), (agg2, full2), (agg3, full3))
        self.slots_c, self.slots_a, self.total = slots_c, slots_a, total
        self.third = part.shape[-1] // 3
        self.half = self.third // 2
        self.started = []
        self.steps = {}

    def at(self, axis, index):
        if axis == 2:
            return {"dp": index}
        z, y = (index, self.here[1]) if axis == 0 else (self.here[0], index)
        return {"seq": (z * 4 + y) * 2 + self.core}

    def remote(self, src, dst, ss, rs, to):
        return pltpu.make_async_remote_copy(src_ref=src, dst_ref=dst, send_sem=ss, recv_sem=rs,
                                            device_id=to, device_id_type=MESH)

    def start(self, copies):
        for c in copies:
            c.start()
        self.started += copies
        return copies

    def og_begin(self):
        self.og_wide[...] = self.og_ref[...].astype(jnp.float32)
        self.og_copy = self.remote(self.og_wide, self.og_got, self.cs.at[0], self.cr.at[0], self.sibling)
        self.og_copy.start()

    def nt_copy(self, i, count):
        here = pl.ds(i * count, count)
        return self.remote(self.nt_send.at[here], self.nt_got.at[here], self.ns.at[i], self.nr.at[i], self.sibling)

    def og_end(self):
        self.og_copy.wait_recv()
        self.og_theirs[...] = self.og_got[...].astype(jnp.bfloat16)

    def product(self, parts):
        def got(i, _):
            self.nt_copy(i, 16 // parts).wait_recv()
            return 0

        lax.fori_loop(0, parts, got, 0)

        def one(b, _):
            z, y = lax.div(b, 4), lax.rem(b, 4)
            sums = bdot(self.nt_own[b], self.og_ref[...], 1, 0)
            sums += bdot(self.nt_got[b].astype(jnp.bfloat16), self.og_theirs[...], 1, 0)
            self.part[z, y] = sums.reshape(self.part.shape[2:])
            return 0

        lax.fori_loop(0, 16, one, 0, unroll=2)

    def region(self, step, p, t, h=None):
        order = ORDERS[p]
        index = [slice(None)] * 3
        for done in order[:step]:
            index[done] = self.here[done]
        index[order[step]] = t
        lo = p * self.third + (0 if h in (None, 0) else self.half)
        return (*index, slice(None), pl.ds(lo, self.third if h is None else self.half))

    def ways(self, step, p):
        axis = ORDERS[p][step]
        me = self.here[axis]
        return axis, lax.rem(me + 1, 4), lax.rem(me + 3, 4), lax.rem(me + 2, 4)

    def begin(self, step):
        agg, full = self.bufs[step]
        first, second, last = [], [], []
        lo, hi = pl.ds(0, self.half), pl.ds(self.half, self.half)
        for p in range(3):
            axis, up, down, far = self.ways(step, p)

            def go(t, h, dst, k, to):
                return self.remote(self.part.at[self.region(step, p, t, h)], dst, self.rs.at[step, p, k],
                                   self.rr.at[step, p, k], self.at(axis, to))

            first.append([go(far, 0, agg.at[p, 0], 0, up), go(far, 1, agg.at[p, 1], 1, down)])
            second.append([go(up, 1, full.at[p, 0, ..., hi], 2, up), go(down, 0, full.at[p, 1, ..., lo], 3, down)])
            last.append([go(up, 0, full.at[p, 0, ..., lo], 4, up), go(down, 1, full.at[p, 1, ..., hi], 5, down)])
        for p in range(3):
            self.start(first[p])
        for p in range(3):
            self.start(second[p])
        self.steps[step] = (first, second, last)

    def middle(self, step):
        agg, _ = self.bufs[step]
        first, _, last = self.steps[step]
        for p in range(3):
            _, up, down, _ = self.ways(step, p)
            first[p][0].wait_recv()
            self.part[self.region(step, p, up, 0)] += agg[p, 0]
            self.start([last[p][0]])
            first[p][1].wait_recv()
            self.part[self.region(step, p, down, 1)] += agg[p, 1]
            self.start([last[p][1]])

    def end(self, step):
        _, full = self.bufs[step]
        _, second, last = self.steps[step]
        for p in range(3):
            for c in second[p] + last[p]:
                c.wait_recv()
            here = self.region(step, p, self.here[ORDERS[p][step]])
            self.part[here] += full[p, 0] + full[p, 1]

    def small_pair_begin(self):
        self.small_pair = self.start([
            self.remote(self.small, self.slots_c.at[self.core], self.cs.at[2], self.cr.at[2], self.sibling)])
        self.slots_c[self.core] = self.small[...]

    def small_pair_end(self):
        self.small_pair[0].wait_recv()
        self.total[0] = self.slots_c[0] + self.slots_c[1]

    def small_begin(self, k):
        axis = (2, 1, 0)[k]
        me = self.here[axis]
        self.smalls = self.start([
            self.remote(self.total.at[k], self.slots_a.at[k, me], self.ms.at[k, d - 1], self.mr.at[k, d - 1],
                        self.at(axis, lax.rem(me + d, 4)))
            for d in (1, 2, 3)])
        self.slots_a[k, me] = self.total[k]

    def small_end(self, k):
        for c in self.smalls:
            c.wait_recv()
        now = (self.slots_a[k, 0] + self.slots_a[k, 1]) + (self.slots_a[k, 2] + self.slots_a[k, 3])
        if k < 2:
            self.total[k + 1] = now
        else:
            self.small_out[...] = now

    def share_begin(self):
        z, y, x = self.here
        self.out_ref[x] = self.part[z, y, x]
        self.start([
            self.remote(self.out_ref.at[x], self.out_ref.at[x], self.xs.at[d - 1], self.xr.at[d - 1],
                        {"dp": lax.rem(x + d, 4)})
            for d in (1, 2, 3)])

    def share_end(self):
        for d in (1, 2, 3):
            came = lax.rem(self.xi + 4 - d, 4)
            self.remote(self.out_ref.at[came], self.out_ref.at[came], self.xs.at[d - 1], self.xr.at[d - 1],
                        {"dp": came}).wait_recv()

    def finish(self):
        for c in self.started:
            c.wait_send()


def ring_scratch(rows, cols, span, lines):
    f32 = jnp.float32
    quarter, third, half = rows // 4, cols // 3, cols // 6
    return [
        pltpu.VMEM((4, 4, 4, quarter, cols), f32),
        pltpu.VMEM((16, rows, span), f32),
        pltpu.VMEM((span, cols), f32),
        pltpu.VMEM((span, cols), jnp.bfloat16),
        pltpu.VMEM((3, 2, 4, 4, quarter, half), f32),
        pltpu.VMEM((3, 2, 4, 4, quarter, third), f32),
        pltpu.VMEM((3, 2, 4, quarter, half), f32),
        pltpu.VMEM((3, 2, 4, quarter, third), f32),
        pltpu.VMEM((3, 2, quarter, half), f32),
        pltpu.VMEM((3, 2, quarter, third), f32),
        pltpu.VMEM((2, lines, 128), f32),
        pltpu.VMEM((3, 4, lines, 128), f32),
        pltpu.VMEM((3, lines, 128), f32),
        pltpu.SemaphoreType.DMA((3,)),
        pltpu.SemaphoreType.DMA((3,)),
        pltpu.SemaphoreType.DMA((8,)),
        pltpu.SemaphoreType.DMA((8,)),
        pltpu.SemaphoreType.DMA((3, 3, 6)),
        pltpu.SemaphoreType.DMA((3, 3, 6)),
        pltpu.SemaphoreType.DMA((3,)),
        pltpu.SemaphoreType.DMA((3,)),
        pltpu.SemaphoreType.DMA((3, 3)),
        pltpu.SemaphoreType.DMA((3, 3)),
    ]


BLOCK = 384
TAIL, LEAD, SKIP, THROUGH = range(4)


def softplus(v):
    return jnp.maximum(v, 0.0) + jnp.log1p(jnp.exp(-jnp.abs(v)))


def mixer_kernel(n, x_ref, z_ref, b_ref, c_ref, logit_in, og_ref, bias_in, rate_in, skip_in, gain_ref,
                 resets_ref, w_hbm,
                 w_out, small_out, dx_out, dz_out, db_out, dc_out, dlogit_out, mixed_out, *scratch):
    (dn, u, normed, s_buf, inc, sg, s_in, spread, lanes, w_buf, gm_hi, gm_lo, gt_hi, gt_lo, mask_ref, bk, bkt, co, cot,
     e_ref, f_ref, step_ref, sig_ref, keep_ref, open_ref, ms_acc, m2_acc, dg_acc, dc_acc, db_acc, a_acc, b_acc,
     skip_acc, end_acc, small, nt_own, nt_send, og_wide, mine, stage, par_ref, w_sem) = scratch[:42]
    rest = scratch[42:]
    ahead = make_scan(n, False, s_buf, spread, inc, (mine, stage), rest[:SCAN_SCRATCH])
    behind = make_scan(n, True, sg, spread, inc, (mine, stage), rest[SCAN_SCRATCH : 2 * SCAN_SCRATCH])
    rest = rest[2 * SCAN_SCRATCH :]
    ring = Ring(og_ref, og_wide, nt_own, nt_send, w_out, small, small_out, *rest[:13], rest[13:])
    f32, bf16 = jnp.float32, jnp.bfloat16
    span, width = x_ref.shape
    blocks = width // BLOCK

    def w_copy(i):
        slot = lax.rem(i, 2)
        return pltpu.make_async_copy(w_hbm.at[pl.ds(i * BLOCK, BLOCK)], w_buf.at[slot], w_sem.at[slot])

    barrier = pltpu.get_barrier_semaphore()
    count = ahead.greet(barrier)
    for d in (1, 2, 3):
        pl.semaphore_signal(barrier, inc=1, device_id={"dp": lax.rem(ring.xi + d, 4)}, device_id_type=MESH)
    w_copy(0).start()

    start = lax.axis_index("seq") * span
    ri = lax.broadcasted_iota(jnp.int32, (span, span), 0)
    ci = lax.broadcasted_iota(jnp.int32, (span, span), 1)
    flag_c = jnp.zeros((span, span), f32)
    flag_r = jnp.zeros((span, span), f32)
    for k in range(resets_ref.shape[1]):
        at_reset = resets_ref[0:1, k : k + 1] - start
        flag_c = jnp.where(ci == at_reset, 1.0, flag_c)
        flag_r = jnp.where(ri == at_reset, 1.0, flag_r)
    count_col = jnp.sum(jnp.where(ri >= ci, flag_c, 0.0), axis=1, keepdims=True)
    count_row = jnp.sum(jnp.where(ri <= ci, flag_r, 0.0), axis=0, keepdims=True)
    all_col = jnp.sum(flag_c, axis=1, keepdims=True)
    all_row = jnp.sum(flag_r, axis=0, keepdims=True)
    below = jnp.where(ri >= ci, 1.0, 0.0)
    mask = jnp.where((ri >= ci) & (count_col == count_row), 1.0, 0.0)
    mask_ref[...] = mask
    keep = jnp.where(count_col == all_col, 1.0, 0.0)
    opened = jnp.where(count_col == 0.0, 1.0, 0.0)
    keep_ref[...] = jnp.broadcast_to(keep, keep_ref.shape)
    open_ref[...] = jnp.broadcast_to(opened, open_ref.shape)
    b_keep = b_ref[...].astype(f32) * keep
    c_open = c_ref[...].astype(f32) * opened
    bk[...] = b_keep.astype(bf16)
    bkt[...] = b_keep.T.astype(bf16)
    co[...] = c_open.astype(bf16)
    cot[...] = c_open.T.astype(bf16)
    gm = bdot(c_ref[...], b_ref[...], 1, 1) * mask
    gm_hi[...], gm_lo[...] = split(gm)
    gt_hi[...], gt_lo[...] = split(gm.T)
    heads = logit_in.shape[1]
    sig_ref[...] = jnp.zeros_like(sig_ref)
    sig_ref[:, 0:heads] = logit_in[...].astype(f32)
    par_ref[...] = jnp.zeros_like(par_ref)
    par_ref[0:1, 0:heads] = bias_in[...]
    par_ref[1:2, 0:heads] = rate_in[...]
    par_ref[2:3, 0:heads] = skip_in[...]
    raw = sig_ref[...] + par_ref[0:1]
    step = softplus(raw)
    step_ref[...] = step
    sig_ref[...] = jax.nn.sigmoid(raw)
    cum = jnp.dot(below, -par_ref[1:2] * step, precision=HIGHEST, preferred_element_type=f32)
    last = cum[span - 1 : span]
    mid = cum[span // 2 : span // 2 + 1]
    through = jnp.where(all_row[:, :128] == 0.0, jnp.exp(last), 0.0)
    e_ref[...] = jnp.exp(cum - mid)
    f_ref[...] = step * jnp.exp(mid - cum)
    thr = jnp.broadcast_to(through, (8, 128))
    ahead.thr_ref[...] = thr
    behind.thr_ref[...] = thr
    head_of = lax.broadcasted_iota(jnp.int32, spread.shape, 1) >> 6
    spread[...] = jnp.where(lax.broadcasted_iota(jnp.int32, spread.shape, 0) == head_of, 1.0, 0.0).astype(bf16)
    per_head = jnp.concatenate(
        [jnp.exp(last - mid), jnp.exp(mid), par_ref[2:3], through, jnp.zeros((4, 128), f32)], axis=0)
    lanes[...] = jnp.dot(per_head, spread[...].astype(f32), precision=HIGHEST, preferred_element_type=f32)
    for acc in (ms_acc, m2_acc, dg_acc, dc_acc, db_acc, a_acc, b_acc, skip_acc, end_acc, small):
        acc[...] = jnp.zeros_like(acc)

    def block(i):
        return pl.ds(pl.multiple_of(i * BLOCK, 128), BLOCK)

    def every(body):
        def one(i, _):
            body(i, block(i))
            return 0

        lax.fori_loop(0, blocks, one, 0, unroll=2)

    def e_of(at):
        return dot2(split(e_ref[...]), spread[:, at], 1, 0)

    def f_of(at):
        return dot2(split(f_ref[...]), spread[:, at], 1, 0)

    def row(k, at):
        return lanes[k : k + 1, at]

    def own_state(i, at):
        fx2 = split(f_of(at) * x_ref[:, at].astype(f32))
        s_buf[:, at] = row(TAIL, at) * dot2(bkt[...], fx2, 1, 0)

    def in_span(i, at):
        fx2 = split(f_of(at) * x_ref[:, at].astype(f32))
        u[:, at] = dot2((gm_hi[...], gm_lo[...]), fx2, 1, 0)

    def project_back(i, at):
        w_copy(i).wait()

        @pl.when(i + 1 < blocks)
        def _():
            w_copy(i + 1).start()

        dn[:, at] = bdot(og_ref[...], w_buf[lax.rem(i, 2)], 1, 1)

    def read_out(i, at):
        before = inc[:, at]
        s2 = split(row(LEAD, at) * before)
        s_in[:, at] = s2[0]
        s_buf[:, at] = row(THROUGH, at) * before + s_buf[:, at]
        now = u[:, at] + dot2(co[...], s2, 1, 0)
        u[:, at] = now
        y = e_of(at) * now + row(SKIP, at) * x_ref[:, at].astype(f32)
        zf = z_ref[:, at].astype(f32)
        g = y * (zf * jax.nn.sigmoid(zf))
        ms_acc[...] += jnp.broadcast_to(jnp.sum(g * g, axis=1, keepdims=True), ms_acc.shape)
        m2_acc[...] += jnp.broadcast_to(
            jnp.sum(dn[:, at] * gain_ref[0:1, at] * g, axis=1, keepdims=True), m2_acc.shape)

    def norm(i, at):
        e = e_of(at)
        y = e * u[:, at] + row(SKIP, at) * x_ref[:, at].astype(f32)
        zf = z_ref[:, at].astype(f32)
        sig = jax.nn.sigmoid(zf)
        silu = zf * sig
        r = lax.rsqrt(ms_acc[:, 0:1] * (1.0 / width) + 1e-05)
        ghat = y * silu * r
        gain = gain_ref[0:1, at]
        out = ghat * gain
        out_low = out.astype(bf16)
        normed[:, at] = out_low
        up = out_low.astype(f32).T.reshape(BLOCK // 192, 2, 96, span)
        here = pl.ds(i * (BLOCK // 192), BLOCK // 192)
        even = ring.core == 0
        nt_own[here] = jnp.where(even, up[:, 0], up[:, 1]).astype(bf16)
        nt_send[here] = jnp.where(even, up[:, 1], up[:, 0])
        ring.nt_copy(i, BLOCK // 192).start()
        d = dn[:, at]
        sums = jnp.sum(d * ghat, axis=0, keepdims=True)
        for k in range(BLOCK // 128):
            small[pl.ds(i * (BLOCK // 128) + k, 1)] = sums[:, k * 128 : (k + 1) * 128]
        dg = r * (d * gain - ghat * (r * m2_acc[:, 0:1] * (1.0 / width)))
        dy = dg * silu
        dz_out[:, at] = (dg * y * (sig * (1.0 + zf * (1.0 - sig)))).astype(bf16)
        dn[:, at] = dy
        sg[:, at] = row(LEAD, at) * dot2(cot[...], split(e * dy), 1, 0)

    def pass_one(i, at):
        sp = spread[:, at]
        dy, xb = dn[:, at], x_ref[:, at].astype(f32)
        du = e_of(at) * dy
        fx = (f_of(at) * xb).astype(bf16)
        du2 = split(du)
        b_acc[...] += dot2(split(du * u[:, at]), sp, 1, 1)
        u[:, at] = dot2((gt_hi[...], gt_lo[...]), du2, 1, 0)
        dg_acc[...] += dot2(du2, fx, 1, 1)
        dc_acc[...] += dot2(du2, s_in[:, at], 1, 1)
        line = jnp.broadcast_to(jnp.sum(dy * xb, axis=0, keepdims=True), (8, BLOCK))
        skip_acc[...] += dot2(split(line), sp, 1, 1)

    def pass_two(i, at):
        sp = spread[:, at]
        f = f_of(at)
        fx = f * x_ref[:, at].astype(f32)
        late = inc[:, at]
        ds2 = split(row(TAIL, at) * late)
        d = u[:, at] + dot2(bk[...], ds2, 1, 0)
        dx_out[:, at] = (f * d + row(SKIP, at) * dn[:, at]).astype(bf16)
        a_acc[...] += dot2(split(fx * d), sp, 1, 1)
        db_acc[...] += dot2(fx.astype(bf16), ds2, 1, 1)
        line = jnp.broadcast_to(jnp.sum(late * s_buf[:, at], axis=0, keepdims=True), (8, BLOCK))
        end_acc[...] += dot2(split(line), sp, 1, 1)

    def project(i, at):
        w_copy(i).wait()

        @pl.when(i + 1 < blocks)
        def _():
            w_copy(i + 1).start()

        og_wide[...] += bdot(normed[:, at], w_buf[lax.rem(i, 2)], 1, 0)

    half = blocks // 2
    theirs_first = (1 - ring.core) * half

    def part_of(body, lo):
        def one(i, _):
            k = lax.rem(theirs_first + lo + i, blocks)
            body(k, block(k))
            return 0

        lax.fori_loop(0, half, one, 0, unroll=2)

    part_of(own_state, 0)
    pl.semaphore_wait(barrier, count + 3)
    ahead.begin()
    part_of(own_state, half)
    ahead.exchange()
    ring.og_begin()
    every(project_back)
    ahead.hops()
    every(in_span)
    ring.og_end()
    ahead.deliver()
    ahead.finish()
    every(read_out)
    part_of(norm, 0)
    behind.begin()
    part_of(norm, half)
    behind.exchange()
    ring.product(blocks)
    ring.begin(0)
    behind.hops()
    w_copy(0).start()
    ring.og_copy.wait_send()
    og_wide[...] = jnp.zeros_like(og_wide)
    every(pass_one)
    ring.middle(0)
    every(project)
    mixed_out[...] = og_wide[...].astype(bf16)
    behind.deliver()
    every(pass_two)

    a = a_acc[...]
    upper = jnp.where(ri <= ci, 1.0, 0.0)
    d_decay = jnp.dot(upper, b_acc[...] - a, precision=HIGHEST, preferred_element_type=f32) + end_acc[0:1]
    dlogit = (a / step_ref[...] - par_ref[1:2] * d_decay) * sig_ref[...]
    dlogit_out[...] = dlogit[:, : dlogit_out.shape[1]].astype(bf16)
    lines = width // 128
    small[lines : lines + 1] = jnp.sum(dlogit, axis=0, keepdims=True)
    small[lines + 1 : lines + 2] = jnp.sum(-step_ref[...] * d_decay, axis=0, keepdims=True)
    small[lines + 2 : lines + 3] = skip_acc[0:1]
    ring.small_pair_begin()
    ring.end(0)
    ring.begin(1)
    ring.small_pair_end()
    ring.small_begin(0)
    dg = dg_acc[...] * mask_ref[...]
    dc_out[...] = (dot2(split(dg), b_ref[...], 1, 0) + open_ref[...] * dc_acc[...]).astype(bf16)
    db_out[...] = (dot2(split(dg.T), c_ref[...], 1, 0) + keep_ref[...] * db_acc[...]).astype(bf16)
    ring.middle(1)
    ring.small_end(0)
    ring.small_begin(1)
    ring.end(1)
    ring.begin(2)
    ring.small_end(1)
    ring.small_begin(2)
    ring.middle(2)
    ring.end(2)
    ring.share_begin()
    ring.small_end(2)
    ring.share_end()
    ring.finish()

    def sent(i, _):
        ring.nt_copy(i, BLOCK // 192).wait_send()
        return 0

    lax.fori_loop(0, blocks, sent, 0)
    behind.finish()


def results_kernel(w, sums, dx, dz, db, dc, dlogit, mixed, mixed_to, dx_to, dz_to, db_to, dc_to, dlogit_to,
                   bias_to, rate_to, skip_to, gain_to, w_to, *scratch):
    pairs = ((dx, dx_to), (dz, dz_to), (mixed, mixed_to), (w, w_to), (db, db_to), (dc, dc_to), (dlogit, dlogit_to))
    held, (in_sem, out_sem) = scratch[:-2], scratch[-2:]
    into = [pltpu.make_async_copy(a, v, in_sem.at[k]) for k, ((a, _), v) in enumerate(zip(pairs, held))]
    out = [pltpu.make_async_copy(v, b, out_sem.at[k]) for k, ((_, b), v) in enumerate(zip(pairs, held))]
    for c in into:
        c.start()
    lines, heads = gain_to.shape[0], bias_to.shape[1]
    gain_to[...] = sums[0:lines]
    bias_to[...] = sums[lines : lines + 1, 0:heads]
    rate_to[...] = sums[lines + 1 : lines + 2, 0:heads]
    skip_to[...] = sums[lines + 2 : lines + 3, 0:heads]
    for a, b in zip(into, out):
        a.wait()
        b.start()
    for c in out:
        c.wait()


def per_device(n, ssm_input, gate_input, input_map, output_map, step_logit, step_bias, decay_rate, skip_gain,
               norm_gain, out_weight, resets, out_grad):
    f32, bf16 = jnp.float32, jnp.bfloat16
    _, span, width = ssm_input.shape
    ns, heads, cols = input_map.shape[2], step_bias.shape[0], out_weight.shape[1]
    rows, lines = width // 32, width // 128 + 8
    vmem = pl.BlockSpec(memory_space=pltpu.VMEM)

    def wide(*shape):
        return pltpu.VMEM(shape, f32)

    def low(*shape):
        return pltpu.VMEM(shape, bf16)

    chunk = wide(n // 2, ns // (n // 2), width // 2)
    weight_grad, sums, dx, dz, db, dc, dlogit, mixed = pl.pallas_call(
        functools.partial(mixer_kernel, n),
        out_shape=(
            jax.ShapeDtypeStruct((4, rows // 4, cols), f32),
            jax.ShapeDtypeStruct((lines, 128), f32),
            jax.ShapeDtypeStruct((span, width), bf16),
            jax.ShapeDtypeStruct((span, width), bf16),
            jax.ShapeDtypeStruct((span, ns), bf16),
            jax.ShapeDtypeStruct((span, ns), bf16),
            jax.ShapeDtypeStruct((span, heads), bf16),
            jax.ShapeDtypeStruct((span, cols), bf16),
        ),
        in_specs=[vmem] * 11 + [pl.BlockSpec(memory_space=pl.ANY)],
        out_specs=(vmem,) * 8,
        scratch_shapes=[
            wide(span, width), wide(span, width), low(span, width), wide(ns, width), wide(ns, width), wide(ns, width),
            low(ns, width), low(128, width), wide(8, width), low(2, BLOCK, cols),
            low(span, span), low(span, span), low(span, span), low(span, span), wide(span, span),
            low(span, ns), low(ns, span), low(span, ns), low(ns, span),
            wide(span, 128), wide(span, 128), wide(span, 128), wide(span, 128), wide(span, ns), wide(span, ns),
            wide(span, 128), wide(span, 128), wide(span, span), wide(span, ns), wide(span, ns),
            wide(span, 128), wide(span, 128), wide(8, 128), wide(8, 128), wide(lines, 128),
            low(16, rows, span), wide(16, rows, span), wide(span, cols), chunk, chunk,
            wide(8, 128),
            pltpu.SemaphoreType.DMA((2,)),
        ] + scan_scratch(n, ns, width) * 2 + ring_scratch(rows, cols, span, lines),
        compiler_params=pltpu.CompilerParams(
            collective_id=1, has_side_effects=True, vmem_limit_bytes=VMEM_LIMIT),
        name="mixer",
    )(ssm_input[0], gate_input[0], input_map[0], output_map[0], step_logit[0], out_grad[0], step_bias[None],
      decay_rate[None], skip_gain[None], norm_gain[None], resets, out_weight)
    anywhere = pl.BlockSpec(memory_space=pl.ANY)
    shapes = [(v.shape, bf16) for v in (mixed, dx, dz, db, dc, dlogit)] + [((1, heads), f32)] * 3
    shapes += [((width // 128, 128), f32), (weight_grad.shape, f32)]
    out = pl.pallas_call(
        results_kernel,
        out_shape=tuple(jax.ShapeDtypeStruct(*v) for v in shapes),
        in_specs=[anywhere, vmem] + [anywhere] * 6,
        out_specs=(anywhere,) * 6 + (vmem,) * 4 + (anywhere,),
        scratch_shapes=[pltpu.VMEM(v.shape, v.dtype) for v in (dx, dz, mixed, weight_grad, db, dc, dlogit)]
        + [pltpu.SemaphoreType.DMA((7,))] * 2,
        compiler_params=pltpu.CompilerParams(vmem_limit_bytes=16 * 1024 * 1024),
        name="results",
    )(weight_grad, sums, dx, dz, db, dc, dlogit, mixed)
    return (
        *(v[None] for v in out[:6]),
        *(v.reshape(-1) for v in out[6:10]),
        out[10].reshape(rows, cols),
    )


def solution(mesh):
    by_rows = P("dp", "seq", None)
    return jax.shard_map(
        functools.partial(per_device, mesh.shape["seq"]),
        mesh=mesh,
        in_specs=(by_rows,) * 5 + (P(),) * 5 + (P("dp", None), by_rows),
        out_specs=(by_rows,) * 6 + (P(),) * 4 + (P("seq", None),),
        check_vma=False,
    )
```

```python
import functools

import jax
import jax.numpy as jnp
from jax import lax
from jax.experimental import pallas as pl
from jax.experimental.pallas import tpu as pltpu
from jax.sharding import PartitionSpec as P

MESH = pl.DeviceIdType.MESH
HIGHEST = lax.Precision.HIGHEST
VMEM_LIMIT = 63 * 1024 * 1024


def bdot(a, b, ca, cb):
    return lax.dot_general(
        a, b, (((ca,), (cb,)), ((), ())), preferred_element_type=jnp.float32
    )


def split(v):
    hi = v.astype(jnp.bfloat16)
    return hi, (v - hi.astype(jnp.float32)).astype(jnp.bfloat16)


def dot2(a, b, ca, cb):
    if isinstance(a, tuple) and isinstance(b, tuple):
        return bdot(a[0], b[0], ca, cb) + (bdot(a[0], b[1], ca, cb) + bdot(a[1], b[0], ca, cb))
    if isinstance(a, tuple):
        return bdot(a[0], b, ca, cb) + bdot(a[1], b, ca, cb)
    if isinstance(b, tuple):
        return bdot(a, b[0], ca, cb) + bdot(a, b[1], ca, cb)
    return bdot(a, b, ca, cb)


class Scan:
    def __init__(self, n, reverse, s_ref, thr_ref, spread_ref, out_ref, pair, mine, recv, stage, back, give,
                 thr_pair, thr_own, thr_buf, thr_wide, first_wide, sems):
        me = lax.axis_index("seq")
        self.chips, self.reverse = n // 2, reverse
        self.core, self.chip = lax.rem(me, 2), lax.div(me, 2)
        self.s_ref, self.thr_ref, self.spread_ref, self.out_ref = s_ref, thr_ref, spread_ref, out_ref
        self.pair, self.mine, self.recv, self.stage, self.back, self.give = pair, mine, recv, stage, back, give
        self.thr_pair, self.thr_own, self.thr_buf = thr_pair, thr_own, thr_buf
        self.thr_wide, self.first_wide = thr_wide, first_wide
        (self.ps, self.pr, self.ss, self.sr, self.ts, self.tr, self.bs, self.br, self.gs, self.gr, self.qs, self.qr) = sems
        ns, width = s_ref.shape
        self.rows, self.half = ns // self.chips, width // 2

    def lanes(self, core):
        return pl.ds(pl.multiple_of(core * self.half, 128), self.half)

    def band(self, k):
        return pl.ds(pl.multiple_of(k * self.rows, 8), self.rows)

    def copy(self, src, dst, ss, rs, to):
        return pltpu.make_async_remote_copy(src_ref=src, dst_ref=dst, send_sem=ss, recv_sem=rs,
                                            device_id={"seq": to}, device_id_type=MESH)

    def sibling(self):
        return self.chip * 2 + 1 - self.core

    def peer(self, k):
        return k * 2 + self.core

    def greet(self, barrier):
        pl.semaphore_signal(barrier, inc=1, device_id={"seq": self.sibling()}, device_id_type=MESH)

        def one(i, _):
            k = lax.rem(self.chip + 1 + i, self.chips)
            pl.semaphore_signal(barrier, inc=1, device_id={"seq": self.peer(k)}, device_id_type=MESH)
            return 0

        lax.fori_loop(0, self.chips - 1, one, 0)
        return self.chips

    def pair_copy(self, k):
        return self.copy(self.s_ref.at[self.band(k), self.lanes(1 - self.core)], self.pair.at[k],
                         self.ps.at[k], self.pr.at[k], self.sibling())

    def thr_pair_copy(self):
        return self.copy(self.thr_ref, self.thr_pair, self.qs, self.qr, self.sibling())

    def thr_copy(self, k, slot):
        return self.copy(self.thr_own, self.thr_buf.at[slot], self.ts.at[k], self.tr.at[slot], self.peer(k))

    def chunk_copy(self, k, slot):
        return self.copy(self.mine.at[k], self.recv.at[slot], self.ss.at[k], self.sr.at[slot], self.peer(k))

    def back_copy(self, k, slot):
        return self.copy(self.stage.at[k], self.back.at[slot], self.bs.at[k], self.br.at[slot], self.peer(k))

    def give_copy(self, k, core):
        return self.copy(self.give.at[k], self.out_ref.at[self.band(k), self.lanes(core)], self.gs.at[k], self.gr.at[k],
                         self.sibling())

    def begin(self):
        self.thr_pair_copy().start()

        def one(i, _):
            self.pair_copy(lax.rem(self.chip + 1 + i, self.chips)).start()
            return 0

        lax.fori_loop(0, self.chips, one, 0)

    def exchange(self):
        first = 1 if self.reverse else 0
        self.thr_pair_copy().wait_recv()
        mine_first = self.core == first
        thr_first = jnp.where(mine_first, self.thr_ref[...], self.thr_pair[...])
        thr_second = jnp.where(mine_first, self.thr_pair[...], self.thr_ref[...])
        self.thr_own[...] = thr_first * thr_second
        self.thr_buf[self.chip] = thr_first * thr_second

        def tell(i, _):
            self.thr_copy(lax.rem(self.chip + 1 + i, self.chips), self.chip).start()
            return 0

        lax.fori_loop(0, self.chips - 1, tell, 0)
        both = jnp.concatenate([thr_first, thr_second], axis=0)
        wide = jnp.dot(both, self.spread_ref[:, self.lanes(self.core)].astype(jnp.float32), precision=HIGHEST,
                       preferred_element_type=jnp.float32)
        self.first_wide[...] = wide[0:8]
        second_wide = wide[8:16]

        def one(i, _):
            k = lax.rem(self.chip + 1 + i, self.chips)
            self.pair_copy(k).wait_recv()
            own = self.s_ref[self.band(k), self.lanes(self.core)]
            other = self.pair[k]
            early = jnp.where(mine_first, own, other)
            late = jnp.where(mine_first, other, own)
            self.mine[k] = second_wide * early + late

            @pl.when(k != self.chip)
            def _():
                self.chunk_copy(k, self.chip).start()

            return 0

        lax.fori_loop(0, self.chips, one, 0)
        self.recv[self.chip] = self.mine[self.chip]

    def hops(self):
        def arrive(i, _):
            self.thr_copy(self.chip, lax.rem(self.chip + 1 + i, self.chips)).wait_recv()
            return 0

        lax.fori_loop(0, self.chips - 1, arrive, 0)
        self.thr_wide[...] = jnp.dot(self.thr_buf[:, 0, :], self.spread_ref[:, self.lanes(self.core)].astype(jnp.float32),
                                     precision=HIGHEST, preferred_element_type=jnp.float32)

        def hop(i, state):
            j = self.chips - 1 - i if self.reverse else i

            @pl.when(j != self.chip)
            def _():
                self.chunk_copy(self.chip, j).wait_recv()

            self.stage[j] = state
            return self.thr_wide[pl.ds(j, 1), :] * state + self.recv[j]

        lax.fori_loop(0, self.chips, hop, jnp.zeros((self.rows, self.half), jnp.float32))
        self.back[self.chip] = self.stage[self.chip]

        def give_back(i, _):
            self.back_copy(lax.rem(self.chip + 1 + i, self.chips), self.chip).start()
            return 0

        lax.fori_loop(0, self.chips - 1, give_back, 0)

    def deliver(self):
        mine_first = self.core == (1 if self.reverse else 0)

        def one(i, _):
            k = lax.rem(self.chip + i, self.chips)

            @pl.when(k != self.chip)
            def _():
                self.back_copy(self.chip, k).wait_recv()
                self.chunk_copy(k, self.chip).wait_send()

            early = self.back[k]
            own = self.s_ref[self.band(k), self.lanes(self.core)]
            late = self.first_wide[...] * early + jnp.where(mine_first, own, self.pair[k])
            self.out_ref[self.band(k), self.lanes(self.core)] = jnp.where(mine_first, early, late)
            self.give[k] = jnp.where(mine_first, late, early)
            self.give_copy(k, self.core).start()
            return 0

        lax.fori_loop(0, self.chips, one, 0)

        def got(k, _):
            self.give_copy(k, 1 - self.core).wait_recv()
            return 0

        lax.fori_loop(0, self.chips, got, 0)

    def finish(self):
        self.thr_pair_copy().wait_send()

        def one(i, _):
            k = lax.rem(self.chip + 1 + i, self.chips)
            self.pair_copy(k).wait_send()
            self.give_copy(k, self.core).wait_send()

            @pl.when(k != self.chip)
            def _():
                self.thr_copy(k, self.chip).wait_send()
                self.back_copy(k, self.chip).wait_send()

            return 0

        lax.fori_loop(0, self.chips, one, 0)


def scan_scratch(n, ns, width):
    chips = n // 2
    chunk = pltpu.VMEM((chips, ns // chips, width // 2), jnp.float32)
    tile = pltpu.VMEM((8, 128), jnp.float32)
    return [chunk] * 3 + [
        tile,
        tile,
        tile,
        pltpu.VMEM((chips, 8, 128), jnp.float32),
        pltpu.VMEM((chips, width // 2), jnp.float32),
        pltpu.VMEM((8, width // 2), jnp.float32),
    ] + [pltpu.SemaphoreType.DMA((chips,))] * 10 + [pltpu.SemaphoreType.DMA] * 2


SCAN_SCRATCH = 9 + 12


def make_scan(n, reverse, s_ref, spread_ref, out_ref, shared, scratch):
    mine, stage = shared
    give = mine
    pair, recv, back, thr_ref = scratch[:4]
    return Scan(n, reverse, s_ref, thr_ref, spread_ref, out_ref, pair, mine, recv, stage, back, give,
                *scratch[4:9], scratch[9:])


ORDERS = ((2, 1, 0), (1, 0, 2), (0, 2, 1))


class Ring:
    def __init__(self, og_ref, og_wide, nt_own, nt_send, out_ref, small, small_out, part, nt_got, og_got, og_theirs, agg1, full1, agg2, full2,
                 agg3, full3, slots_c, slots_a, total, sems):
        (self.cs, self.cr, self.ns, self.nr, self.rs, self.rr, self.xs, self.xr, self.ms, self.mr) = sems
        self.xi = lax.axis_index("dp")
        s = lax.axis_index("seq")
        self.core = lax.rem(s, 2)
        self.here = (lax.div(s, 8), lax.rem(lax.div(s, 2), 4), self.xi)
        self.sibling = {"seq": s + 1 - 2 * self.core}
        self.og_ref, self.og_wide, self.nt_own, self.nt_send = og_ref, og_wide, nt_own, nt_send
        self.out_ref = out_ref
        self.small, self.small_out = small, small_out
        self.part, self.nt_got, self.og_got, self.og_theirs = part, nt_got, og_got, og_theirs
        self.bufs = ((agg1, full1), (agg2, full2), (agg3, full3))
        self.slots_c, self.slots_a, self.total = slots_c, slots_a, total
        self.third = part.shape[-1] // 3
        self.half = self.third // 2
        self.started = []
        self.steps = {}

    def at(self, axis, index):
        if axis == 2:
            return {"dp": index}
        z, y = (index, self.here[1]) if axis == 0 else (self.here[0], index)
        return {"seq": (z * 4 + y) * 2 + self.core}

    def remote(self, src, dst, ss, rs, to):
        return pltpu.make_async_remote_copy(src_ref=src, dst_ref=dst, send_sem=ss, recv_sem=rs,
                                            device_id=to, device_id_type=MESH)

    def start(self, copies):
        for c in copies:
            c.start()
        self.started += copies
        return copies

    def og_begin(self):
        self.og_wide[...] = self.og_ref[...].astype(jnp.float32)
        self.og_copy = self.remote(self.og_wide, self.og_got, self.cs.at[0], self.cr.at[0], self.sibling)
        self.og_copy.start()

    def nt_copy(self, i, count):
        here = pl.ds(i * count, count)
        return self.remote(self.nt_send.at[here], self.nt_got.at[here], self.ns.at[i], self.nr.at[i], self.sibling)

    def og_end(self):
        self.og_copy.wait_recv()
        self.og_theirs[...] = self.og_got[...].astype(jnp.bfloat16)

    def product(self, parts):
        def got(i, _):
            self.nt_copy(i, 16 // parts).wait_recv()
            return 0

        lax.fori_loop(0, parts, got, 0)

        def one(b, _):
            z, y = lax.div(b, 4), lax.rem(b, 4)
            sums = bdot(self.nt_own[b], self.og_ref[...], 1, 0)
            sums += bdot(self.nt_got[b].astype(jnp.bfloat16), self.og_theirs[...], 1, 0)
            self.part[z, y] = sums.reshape(self.part.shape[2:])
            return 0

        lax.fori_loop(0, 16, one, 0, unroll=2)

    def region(self, step, p, t, h=None):
        order = ORDERS[p]
        index = [slice(None)] * 3
        for done in order[:step]:
            index[done] = self.here[done]
        index[order[step]] = t
        lo = p * self.third + (0 if h in (None, 0) else self.half)
        return (*index, slice(None), pl.ds(lo, self.third if h is None else self.half))

    def ways(self, step, p):
        axis = ORDERS[p][step]
        me = self.here[axis]
        return axis, lax.rem(me + 1, 4), lax.rem(me + 3, 4), lax.rem(me + 2, 4)

    def copies_of(self, step, p):
        agg, full = self.bufs[step]
        lo, hi = pl.ds(0, self.half), pl.ds(self.half, self.half)
        axis, up, down, far = self.ways(step, p)

        def go(t, h, dst, k, to):
            return self.remote(self.part.at[self.region(step, p, t, h)], dst, self.rs.at[step, p, k],
                               self.rr.at[step, p, k], self.at(axis, to))

        first = [go(far, 0, agg.at[p, 0], 0, up), go(far, 1, agg.at[p, 1], 1, down)]
        second = [go(up, 1, full.at[p, 0, ..., hi], 2, up), go(down, 0, full.at[p, 1, ..., lo], 3, down)]
        last = [go(up, 0, full.at[p, 0, ..., lo], 4, up), go(down, 1, full.at[p, 1, ..., hi], 5, down)]
        return first, second, last

    def begin(self, step):
        for p in range(3):
            self.steps[step, p] = self.copies_of(step, p)
            self.start(self.steps[step, p][0])
        for p in range(3):
            self.start(self.steps[step, p][1])

    def middle(self, step):
        agg, _ = self.bufs[step]
        for p in range(3):
            first, _, last = self.steps[step, p]
            _, up, down, _ = self.ways(step, p)
            first[0].wait_recv()
            self.part[self.region(step, p, up, 0)] += agg[p, 0]
            self.start([last[0]])
            first[1].wait_recv()
            self.part[self.region(step, p, down, 1)] += agg[p, 1]
            self.start([last[1]])

    def end(self, step):
        _, full = self.bufs[step]
        for p in range(3):
            _, second, last = self.steps[step, p]
            for c in second + last:
                c.wait_recv()
            here = self.region(step, p, self.here[ORDERS[p][step]])
            self.part[here] += full[p, 0] + full[p, 1]
            if step < 2:
                self.steps[step + 1, p] = self.copies_of(step + 1, p)
                self.start(self.steps[step + 1, p][0] + self.steps[step + 1, p][1])

    def small_pair_begin(self):
        self.small_pair = self.start([
            self.remote(self.small, self.slots_c.at[self.core], self.cs.at[2], self.cr.at[2], self.sibling)])
        self.slots_c[self.core] = self.small[...]

    def small_pair_end(self):
        self.small_pair[0].wait_recv()
        self.total[0] = self.slots_c[0] + self.slots_c[1]

    def small_begin(self, k):
        axis = (2, 1, 0)[k]
        me = self.here[axis]
        self.smalls = self.start([
            self.remote(self.total.at[k], self.slots_a.at[k, me], self.ms.at[k, d - 1], self.mr.at[k, d - 1],
                        self.at(axis, lax.rem(me + d, 4)))
            for d in (1, 2, 3)])
        self.slots_a[k, me] = self.total[k]

    def small_end(self, k):
        for c in self.smalls:
            c.wait_recv()
        now = (self.slots_a[k, 0] + self.slots_a[k, 1]) + (self.slots_a[k, 2] + self.slots_a[k, 3])
        if k < 2:
            self.total[k + 1] = now
        else:
            self.small_out[...] = now

    def share_begin(self):
        z, y, x = self.here
        self.out_ref[x] = self.part[z, y, x]
        self.start([
            self.remote(self.out_ref.at[x], self.out_ref.at[x], self.xs.at[d - 1], self.xr.at[d - 1],
                        {"dp": lax.rem(x + d, 4)})
            for d in (1, 2, 3)])

    def share_end(self):
        for d in (1, 2, 3):
            came = lax.rem(self.xi + 4 - d, 4)
            self.remote(self.out_ref.at[came], self.out_ref.at[came], self.xs.at[d - 1], self.xr.at[d - 1],
                        {"dp": came}).wait_recv()

    def finish(self):
        for c in self.started:
            c.wait_send()


def ring_scratch(rows, cols, span, lines):
    f32 = jnp.float32
    quarter, third, half = rows // 4, cols // 3, cols // 6
    return [
        pltpu.VMEM((4, 4, 4, quarter, cols), f32),
        pltpu.VMEM((16, rows, span), f32),
        pltpu.VMEM((span, cols), f32),
        pltpu.VMEM((span, cols), jnp.bfloat16),
        pltpu.VMEM((3, 2, 4, 4, quarter, half), f32),
        pltpu.VMEM((3, 2, 4, 4, quarter, third), f32),
        pltpu.VMEM((3, 2, 4, quarter, half), f32),
        pltpu.VMEM((3, 2, 4, quarter, third), f32),
        pltpu.VMEM((3, 2, quarter, half), f32),
        pltpu.VMEM((3, 2, quarter, third), f32),
        pltpu.VMEM((2, lines, 128), f32),
        pltpu.VMEM((3, 4, lines, 128), f32),
        pltpu.VMEM((3, lines, 128), f32),
        pltpu.SemaphoreType.DMA((3,)),
        pltpu.SemaphoreType.DMA((3,)),
        pltpu.SemaphoreType.DMA((8,)),
        pltpu.SemaphoreType.DMA((8,)),
        pltpu.SemaphoreType.DMA((3, 3, 6)),
        pltpu.SemaphoreType.DMA((3, 3, 6)),
        pltpu.SemaphoreType.DMA((3,)),
        pltpu.SemaphoreType.DMA((3,)),
        pltpu.SemaphoreType.DMA((3, 3)),
        pltpu.SemaphoreType.DMA((3, 3)),
    ]


BLOCK = 384
TAIL, LEAD, SKIP, THROUGH = range(4)


def softplus(v):
    return jnp.maximum(v, 0.0) + jnp.log1p(jnp.exp(-jnp.abs(v)))


def mixer_kernel(n, x_ref, z_ref, b_ref, c_ref, logit_in, og_ref, bias_in, rate_in, skip_in, gain_ref,
                 resets_ref, w_hbm,
                 w_out, small_out, dx_out, dz_out, db_out, dc_out, dlogit_out, mixed_out, *scratch):
    (dn, u, normed, s_buf, inc, sg, s_in, spread, lanes, w_buf, gm_hi, gm_lo, gt_hi, gt_lo, mask_ref, bk, bkt, co, cot,
     e_ref, f_ref, step_ref, sig_ref, keep_ref, open_ref, ms_acc, m2_acc, dg_acc, dc_acc, db_acc, a_acc, b_acc,
     skip_acc, end_acc, small, nt_own, nt_send, og_wide, mine, stage, par_ref, w_sem) = scratch[:42]
    rest = scratch[42:]
    ahead = make_scan(n, False, s_buf, spread, inc, (mine, stage), rest[:SCAN_SCRATCH])
    behind = make_scan(n, True, sg, spread, inc, (mine, stage), rest[SCAN_SCRATCH : 2 * SCAN_SCRATCH])
    rest = rest[2 * SCAN_SCRATCH :]
    ring = Ring(og_ref, og_wide, nt_own, nt_send, w_out, small, small_out, *rest[:13], rest[13:])
    f32, bf16 = jnp.float32, jnp.bfloat16
    span, width = x_ref.shape
    blocks = width // BLOCK

    def w_copy(i):
        slot = lax.rem(i, 2)
        return pltpu.make_async_copy(w_hbm.at[pl.ds(i * BLOCK, BLOCK)], w_buf.at[slot], w_sem.at[slot])

    barrier = pltpu.get_barrier_semaphore()
    count = ahead.greet(barrier)
    for d in (1, 2, 3):
        pl.semaphore_signal(barrier, inc=1, device_id={"dp": lax.rem(ring.xi + d, 4)}, device_id_type=MESH)
    w_copy(0).start()

    start = lax.axis_index("seq") * span
    ri = lax.broadcasted_iota(jnp.int32, (span, span), 0)
    ci = lax.broadcasted_iota(jnp.int32, (span, span), 1)
    flag_c = jnp.zeros((span, span), f32)
    flag_r = jnp.zeros((span, span), f32)
    for k in range(resets_ref.shape[1]):
        at_reset = resets_ref[0:1, k : k + 1] - start
        flag_c = jnp.where(ci == at_reset, 1.0, flag_c)
        flag_r = jnp.where(ri == at_reset, 1.0, flag_r)
    count_col = jnp.sum(jnp.where(ri >= ci, flag_c, 0.0), axis=1, keepdims=True)
    count_row = jnp.sum(jnp.where(ri <= ci, flag_r, 0.0), axis=0, keepdims=True)
    all_col = jnp.sum(flag_c, axis=1, keepdims=True)
    all_row = jnp.sum(flag_r, axis=0, keepdims=True)
    below = jnp.where(ri >= ci, 1.0, 0.0)
    mask = jnp.where((ri >= ci) & (count_col == count_row), 1.0, 0.0)
    mask_ref[...] = mask
    keep = jnp.where(count_col == all_col, 1.0, 0.0)
    opened = jnp.where(count_col == 0.0, 1.0, 0.0)
    keep_ref[...] = jnp.broadcast_to(keep, keep_ref.shape)
    open_ref[...] = jnp.broadcast_to(opened, open_ref.shape)
    b_keep = b_ref[...].astype(f32) * keep
    c_open = c_ref[...].astype(f32) * opened
    bk[...] = b_keep.astype(bf16)
    bkt[...] = b_keep.T.astype(bf16)
    co[...] = c_open.astype(bf16)
    cot[...] = c_open.T.astype(bf16)
    gm = bdot(c_ref[...], b_ref[...], 1, 1) * mask
    gm_hi[...], gm_lo[...] = split(gm)
    gt_hi[...], gt_lo[...] = split(gm.T)
    heads = logit_in.shape[1]
    sig_ref[...] = jnp.zeros_like(sig_ref)
    sig_ref[:, 0:heads] = logit_in[...].astype(f32)
    par_ref[...] = jnp.zeros_like(par_ref)
    par_ref[0:1, 0:heads] = bias_in[...]
    par_ref[1:2, 0:heads] = rate_in[...]
    par_ref[2:3, 0:heads] = skip_in[...]
    raw = sig_ref[...] + par_ref[0:1]
    step = softplus(raw)
    step_ref[...] = step
    sig_ref[...] = jax.nn.sigmoid(raw)
    cum = jnp.dot(below, -par_ref[1:2] * step, precision=HIGHEST, preferred_element_type=f32)
    last = cum[span - 1 : span]
    mid = cum[span // 2 : span // 2 + 1]
    through = jnp.where(all_row[:, :128] == 0.0, jnp.exp(last), 0.0)
    e_ref[...] = jnp.exp(cum - mid)
    f_ref[...] = step * jnp.exp(mid - cum)
    thr = jnp.broadcast_to(through, (8, 128))
    ahead.thr_ref[...] = thr
    behind.thr_ref[...] = thr
    head_of = lax.broadcasted_iota(jnp.int32, spread.shape, 1) >> 6
    spread[...] = jnp.where(lax.broadcasted_iota(jnp.int32, spread.shape, 0) == head_of, 1.0, 0.0).astype(bf16)
    per_head = jnp.concatenate(
        [jnp.exp(last - mid), jnp.exp(mid), par_ref[2:3], through, jnp.zeros((4, 128), f32)], axis=0)
    lanes[...] = jnp.dot(per_head, spread[...].astype(f32), precision=HIGHEST, preferred_element_type=f32)
    for acc in (ms_acc, m2_acc, dg_acc, dc_acc, db_acc, a_acc, b_acc, skip_acc, end_acc, small):
        acc[...] = jnp.zeros_like(acc)

    def block(i):
        return pl.ds(pl.multiple_of(i * BLOCK, 128), BLOCK)

    def every(body):
        def one(i, _):
            body(i, block(i))
            return 0

        lax.fori_loop(0, blocks, one, 0, unroll=2)

    def e_of(at):
        return dot2(split(e_ref[...]), spread[:, at], 1, 0)

    def f_of(at):
        return dot2(split(f_ref[...]), spread[:, at], 1, 0)

    def row(k, at):
        return lanes[k : k + 1, at]

    def own_state(i, at):
        fx2 = split(f_of(at) * x_ref[:, at].astype(f32))
        s_buf[:, at] = row(TAIL, at) * dot2(bkt[...], fx2, 1, 0)

    def in_span(i, at):
        fx2 = split(f_of(at) * x_ref[:, at].astype(f32))
        u[:, at] = dot2((gm_hi[...], gm_lo[...]), fx2, 1, 0)

    def project_back(i, at):
        w_copy(i).wait()

        @pl.when(i + 1 < blocks)
        def _():
            w_copy(i + 1).start()

        dn[:, at] = bdot(og_ref[...], w_buf[lax.rem(i, 2)], 1, 1)

    def read_out(i, at):
        before = inc[:, at]
        s2 = split(row(LEAD, at) * before)
        s_in[:, at] = s2[0]
        s_buf[:, at] = row(THROUGH, at) * before + s_buf[:, at]
        now = u[:, at] + dot2(co[...], s2, 1, 0)
        u[:, at] = now
        y = e_of(at) * now + row(SKIP, at) * x_ref[:, at].astype(f32)
        zf = z_ref[:, at].astype(f32)
        g = y * (zf * jax.nn.sigmoid(zf))
        ms_acc[...] += jnp.broadcast_to(jnp.sum(g * g, axis=1, keepdims=True), ms_acc.shape)
        m2_acc[...] += jnp.broadcast_to(
            jnp.sum(dn[:, at] * gain_ref[0:1, at] * g, axis=1, keepdims=True), m2_acc.shape)

    def norm(i, at):
        e = e_of(at)
        y = e * u[:, at] + row(SKIP, at) * x_ref[:, at].astype(f32)
        zf = z_ref[:, at].astype(f32)
        sig = jax.nn.sigmoid(zf)
        silu = zf * sig
        r = lax.rsqrt(ms_acc[:, 0:1] * (1.0 / width) + 1e-05)
        ghat = y * silu * r
        gain = gain_ref[0:1, at]
        out = ghat * gain
        out_low = out.astype(bf16)
        normed[:, at] = out_low
        up = out_low.astype(f32).T.reshape(BLOCK // 192, 2, 96, span)
        here = pl.ds(i * (BLOCK // 192), BLOCK // 192)
        even = ring.core == 0
        nt_own[here] = jnp.where(even, up[:, 0], up[:, 1]).astype(bf16)
        nt_send[here] = jnp.where(even, up[:, 1], up[:, 0])
        ring.nt_copy(i, BLOCK // 192).start()
        d = dn[:, at]
        sums = jnp.sum(d * ghat, axis=0, keepdims=True)
        for k in range(BLOCK // 128):
            small[pl.ds(i * (BLOCK // 128) + k, 1)] = sums[:, k * 128 : (k + 1) * 128]
        dg = r * (d * gain - ghat * (r * m2_acc[:, 0:1] * (1.0 / width)))
        dy = dg * silu
        dz_out[:, at] = (dg * y * (sig * (1.0 + zf * (1.0 - sig)))).astype(bf16)
        dn[:, at] = dy
        sg[:, at] = row(LEAD, at) * dot2(cot[...], split(e * dy), 1, 0)

    def pass_one(i, at):
        sp = spread[:, at]
        dy, xb = dn[:, at], x_ref[:, at].astype(f32)
        du = e_of(at) * dy
        fx = (f_of(at) * xb).astype(bf16)
        du2 = split(du)
        b_acc[...] += dot2(split(du * u[:, at]), sp, 1, 1)
        u[:, at] = dot2((gt_hi[...], gt_lo[...]), du2, 1, 0)
        dg_acc[...] += dot2(du2, fx, 1, 1)
        dc_acc[...] += dot2(du2, s_in[:, at], 1, 1)
        line = jnp.broadcast_to(jnp.sum(dy * xb, axis=0, keepdims=True), (8, BLOCK))
        skip_acc[...] += dot2(split(line), sp, 1, 1)

    def pass_two(i, at):
        sp = spread[:, at]
        f = f_of(at)
        fx = f * x_ref[:, at].astype(f32)
        late = inc[:, at]
        ds2 = split(row(TAIL, at) * late)
        d = u[:, at] + dot2(bk[...], ds2, 1, 0)
        dx_out[:, at] = (f * d + row(SKIP, at) * dn[:, at]).astype(bf16)
        a_acc[...] += dot2(split(fx * d), sp, 1, 1)
        db_acc[...] += dot2(fx.astype(bf16), ds2, 1, 1)
        line = jnp.broadcast_to(jnp.sum(late * s_buf[:, at], axis=0, keepdims=True), (8, BLOCK))
        end_acc[...] += dot2(split(line), sp, 1, 1)

    def project(i, at):
        w_copy(i).wait()

        @pl.when(i + 1 < blocks)
        def _():
            w_copy(i + 1).start()

        og_wide[...] += bdot(normed[:, at], w_buf[lax.rem(i, 2)], 1, 0)

    half = blocks // 2
    theirs_first = (1 - ring.core) * half

    def part_of(body, lo):
        def one(i, _):
            k = lax.rem(theirs_first + lo + i, blocks)
            body(k, block(k))
            return 0

        lax.fori_loop(0, half, one, 0, unroll=2)

    part_of(own_state, 0)
    pl.semaphore_wait(barrier, count + 3)
    ahead.begin()
    part_of(own_state, half)
    ahead.exchange()
    ring.og_begin()
    every(project_back)
    ahead.hops()
    every(in_span)
    ring.og_end()
    ahead.deliver()
    ahead.finish()
    every(read_out)
    part_of(norm, 0)
    behind.begin()
    part_of(norm, half)
    behind.exchange()
    ring.product(blocks)
    ring.begin(0)
    behind.hops()
    w_copy(0).start()
    ring.og_copy.wait_send()
    og_wide[...] = jnp.zeros_like(og_wide)
    every(pass_one)
    ring.middle(0)
    every(project)
    mixed_out[...] = og_wide[...].astype(bf16)
    behind.deliver()
    every(pass_two)

    a = a_acc[...]
    upper = jnp.where(ri <= ci, 1.0, 0.0)
    d_decay = jnp.dot(upper, b_acc[...] - a, precision=HIGHEST, preferred_element_type=f32) + end_acc[0:1]
    dlogit = (a / step_ref[...] - par_ref[1:2] * d_decay) * sig_ref[...]
    dlogit_out[...] = dlogit[:, : dlogit_out.shape[1]].astype(bf16)
    lines = width // 128
    small[lines : lines + 1] = jnp.sum(dlogit, axis=0, keepdims=True)
    small[lines + 1 : lines + 2] = jnp.sum(-step_ref[...] * d_decay, axis=0, keepdims=True)
    small[lines + 2 : lines + 3] = skip_acc[0:1]
    ring.small_pair_begin()
    ring.end(0)
    ring.small_pair_end()
    ring.small_begin(0)
    dg = dg_acc[...] * mask_ref[...]
    dc_out[...] = (dot2(split(dg), b_ref[...], 1, 0) + open_ref[...] * dc_acc[...]).astype(bf16)
    db_out[...] = (dot2(split(dg.T), c_ref[...], 1, 0) + keep_ref[...] * db_acc[...]).astype(bf16)
    ring.middle(1)
    ring.small_end(0)
    ring.small_begin(1)
    ring.end(1)
    ring.small_end(1)
    ring.small_begin(2)
    ring.middle(2)
    ring.end(2)
    ring.share_begin()
    ring.small_end(2)
    ring.share_end()
    ring.finish()

    def sent(i, _):
        ring.nt_copy(i, BLOCK // 192).wait_send()
        return 0

    lax.fori_loop(0, blocks, sent, 0)
    behind.finish()


def results_kernel(w, sums, dx, dz, db, dc, dlogit, mixed, mixed_to, dx_to, dz_to, db_to, dc_to, dlogit_to,
                   bias_to, rate_to, skip_to, gain_to, w_to, *scratch):
    pairs = ((dx, dx_to), (dz, dz_to), (mixed, mixed_to), (w, w_to), (db, db_to), (dc, dc_to), (dlogit, dlogit_to))
    held, (in_sem, out_sem) = scratch[:-2], scratch[-2:]
    into = [pltpu.make_async_copy(a, v, in_sem.at[k]) for k, ((a, _), v) in enumerate(zip(pairs, held))]
    out = [pltpu.make_async_copy(v, b, out_sem.at[k]) for k, ((_, b), v) in enumerate(zip(pairs, held))]
    for c in into:
        c.start()
    lines, heads = gain_to.shape[0], bias_to.shape[1]
    gain_to[...] = sums[0:lines]
    bias_to[...] = sums[lines : lines + 1, 0:heads]
    rate_to[...] = sums[lines + 1 : lines + 2, 0:heads]
    skip_to[...] = sums[lines + 2 : lines + 3, 0:heads]
    for a, b in zip(into, out):
        a.wait()
        b.start()
    for c in out:
        c.wait()


def per_device(n, ssm_input, gate_input, input_map, output_map, step_logit, step_bias, decay_rate, skip_gain,
               norm_gain, out_weight, resets, out_grad):
    f32, bf16 = jnp.float32, jnp.bfloat16
    _, span, width = ssm_input.shape
    ns, heads, cols = input_map.shape[2], step_bias.shape[0], out_weight.shape[1]
    rows, lines = width // 32, width // 128 + 8
    vmem = pl.BlockSpec(memory_space=pltpu.VMEM)

    def wide(*shape):
        return pltpu.VMEM(shape, f32)

    def low(*shape):
        return pltpu.VMEM(shape, bf16)

    chunk = wide(n // 2, ns // (n // 2), width // 2)
    weight_grad, sums, dx, dz, db, dc, dlogit, mixed = pl.pallas_call(
        functools.partial(mixer_kernel, n),
        out_shape=(
            jax.ShapeDtypeStruct((4, rows // 4, cols), f32),
            jax.ShapeDtypeStruct((lines, 128), f32),
            jax.ShapeDtypeStruct((span, width), bf16),
            jax.ShapeDtypeStruct((span, width), bf16),
            jax.ShapeDtypeStruct((span, ns), bf16),
            jax.ShapeDtypeStruct((span, ns), bf16),
            jax.ShapeDtypeStruct((span, heads), bf16),
            jax.ShapeDtypeStruct((span, cols), bf16),
        ),
        in_specs=[vmem] * 11 + [pl.BlockSpec(memory_space=pl.ANY)],
        out_specs=(vmem,) * 8,
        scratch_shapes=[
            wide(span, width), wide(span, width), low(span, width), wide(ns, width), wide(ns, width), wide(ns, width),
            low(ns, width), low(128, width), wide(8, width), low(2, BLOCK, cols),
            low(span, span), low(span, span), low(span, span), low(span, span), wide(span, span),
            low(span, ns), low(ns, span), low(span, ns), low(ns, span),
            wide(span, 128), wide(span, 128), wide(span, 128), wide(span, 128), wide(span, ns), wide(span, ns),
            wide(span, 128), wide(span, 128), wide(span, span), wide(span, ns), wide(span, ns),
            wide(span, 128), wide(span, 128), wide(8, 128), wide(8, 128), wide(lines, 128),
            low(16, rows, span), wide(16, rows, span), wide(span, cols), chunk, chunk,
            wide(8, 128),
            pltpu.SemaphoreType.DMA((2,)),
        ] + scan_scratch(n, ns, width) * 2 + ring_scratch(rows, cols, span, lines),
        compiler_params=pltpu.CompilerParams(
            collective_id=1, has_side_effects=True, vmem_limit_bytes=VMEM_LIMIT),
        name="mixer",
    )(ssm_input[0], gate_input[0], input_map[0], output_map[0], step_logit[0], out_grad[0], step_bias[None],
      decay_rate[None], skip_gain[None], norm_gain[None], resets, out_weight)
    anywhere = pl.BlockSpec(memory_space=pl.ANY)
    shapes = [(v.shape, bf16) for v in (mixed, dx, dz, db, dc, dlogit)] + [((1, heads), f32)] * 3
    shapes += [((width // 128, 128), f32), (weight_grad.shape, f32)]
    out = pl.pallas_call(
        results_kernel,
        out_shape=tuple(jax.ShapeDtypeStruct(*v) for v in shapes),
        in_specs=[anywhere, vmem] + [anywhere] * 6,
        out_specs=(anywhere,) * 6 + (vmem,) * 4 + (anywhere,),
        scratch_shapes=[pltpu.VMEM(v.shape, v.dtype) for v in (dx, dz, mixed, weight_grad, db, dc, dlogit)]
        + [pltpu.SemaphoreType.DMA((7,))] * 2,
        compiler_params=pltpu.CompilerParams(vmem_limit_bytes=VMEM_LIMIT),
        name="results",
    )(weight_grad, sums, dx, dz, db, dc, dlogit, mixed)
    return (
        *(v[None] for v in out[:6]),
        *(v.reshape(-1) for v in out[6:10]),
        out[10].reshape(rows, cols),
    )


def solution(mesh):
    by_rows = P("dp", "seq", None)
    return jax.shard_map(
        functools.partial(per_device, mesh.shape["seq"]),
        mesh=mesh,
        in_specs=(by_rows,) * 5 + (P(),) * 5 + (P("dp", None), by_rows),
        out_specs=(by_rows,) * 6 + (P(),) * 4 + (P("seq", None),),
        check_vma=False,
    )
```

```python
import functools

import jax
import jax.numpy as jnp
from jax import lax
from jax.experimental import pallas as pl
from jax.experimental.pallas import tpu as pltpu
from jax.sharding import PartitionSpec as P

MESH = pl.DeviceIdType.MESH
HIGHEST = lax.Precision.HIGHEST
VMEM_LIMIT = 63 * 1024 * 1024


def bdot(a, b, ca, cb):
    return lax.dot_general(
        a, b, (((ca,), (cb,)), ((), ())), preferred_element_type=jnp.float32
    )


def split(v):
    hi = v.astype(jnp.bfloat16)
    return hi, (v - hi.astype(jnp.float32)).astype(jnp.bfloat16)


def dot2(a, b, ca, cb):
    if isinstance(a, tuple) and isinstance(b, tuple):
        return bdot(a[0], b[0], ca, cb) + (bdot(a[0], b[1], ca, cb) + bdot(a[1], b[0], ca, cb))
    if isinstance(a, tuple):
        return bdot(a[0], b, ca, cb) + bdot(a[1], b, ca, cb)
    if isinstance(b, tuple):
        return bdot(a, b[0], ca, cb) + bdot(a, b[1], ca, cb)
    return bdot(a, b, ca, cb)


class Scan:
    def __init__(self, n, reverse, s_ref, thr_ref, spread_ref, out_ref, pair, mine, recv, stage, back, give,
                 thr_pair, thr_own, thr_buf, thr_wide, first_wide, sems):
        me = lax.axis_index("seq")
        self.chips, self.reverse = n // 2, reverse
        self.core, self.chip = lax.rem(me, 2), lax.div(me, 2)
        self.s_ref, self.thr_ref, self.spread_ref, self.out_ref = s_ref, thr_ref, spread_ref, out_ref
        self.pair, self.mine, self.recv, self.stage, self.back, self.give = pair, mine, recv, stage, back, give
        self.thr_pair, self.thr_own, self.thr_buf = thr_pair, thr_own, thr_buf
        self.thr_wide, self.first_wide = thr_wide, first_wide
        (self.ps, self.pr, self.ss, self.sr, self.ts, self.tr, self.bs, self.br, self.gs, self.gr, self.qs, self.qr) = sems
        ns, width = s_ref.shape
        self.rows, self.half = ns // self.chips, width // 2

    def lanes(self, core):
        return pl.ds(pl.multiple_of(core * self.half, 128), self.half)

    def band(self, k):
        return pl.ds(pl.multiple_of(k * self.rows, 8), self.rows)

    def copy(self, src, dst, ss, rs, to):
        return pltpu.make_async_remote_copy(src_ref=src, dst_ref=dst, send_sem=ss, recv_sem=rs,
                                            device_id={"seq": to}, device_id_type=MESH)

    def sibling(self):
        return self.chip * 2 + 1 - self.core

    def peer(self, k):
        return k * 2 + self.core

    def greet(self, barrier):
        pl.semaphore_signal(barrier, inc=1, device_id={"seq": self.sibling()}, device_id_type=MESH)

        def one(i, _):
            k = lax.rem(self.chip + 1 + i, self.chips)
            pl.semaphore_signal(barrier, inc=1, device_id={"seq": self.peer(k)}, device_id_type=MESH)
            return 0

        lax.fori_loop(0, self.chips - 1, one, 0)
        return self.chips

    def pair_copy(self, k):
        return self.copy(self.s_ref.at[self.band(k), self.lanes(1 - self.core)], self.pair.at[k],
                         self.ps.at[k], self.pr.at[k], self.sibling())

    def thr_pair_copy(self):
        return self.copy(self.thr_ref, self.thr_pair, self.qs, self.qr, self.sibling())

    def thr_copy(self, k, slot):
        return self.copy(self.thr_own, self.thr_buf.at[slot], self.ts.at[k], self.tr.at[slot], self.peer(k))

    def chunk_copy(self, k, slot):
        return self.copy(self.mine.at[k], self.recv.at[slot], self.ss.at[k], self.sr.at[slot], self.peer(k))

    def back_copy(self, k, slot):
        return self.copy(self.stage.at[k], self.back.at[slot], self.bs.at[k], self.br.at[slot], self.peer(k))

    def give_copy(self, k, core):
        return self.copy(self.give.at[k], self.out_ref.at[self.band(k), self.lanes(core)], self.gs.at[k], self.gr.at[k],
                         self.sibling())

    def begin(self):
        self.thr_pair_copy().start()

        def one(i, _):
            self.pair_copy(lax.rem(self.chip + 1 + i, self.chips)).start()
            return 0

        lax.fori_loop(0, self.chips, one, 0)

    def exchange(self):
        first = 1 if self.reverse else 0
        self.thr_pair_copy().wait_recv()
        mine_first = self.core == first
        thr_first = jnp.where(mine_first, self.thr_ref[...], self.thr_pair[...])
        thr_second = jnp.where(mine_first, self.thr_pair[...], self.thr_ref[...])
        self.thr_own[...] = thr_first * thr_second
        self.thr_buf[self.chip] = thr_first * thr_second

        def tell(i, _):
            self.thr_copy(lax.rem(self.chip + 1 + i, self.chips), self.chip).start()
            return 0

        lax.fori_loop(0, self.chips - 1, tell, 0)
        both = jnp.concatenate([thr_first, thr_second], axis=0)
        wide = jnp.dot(both, self.spread_ref[:, self.lanes(self.core)].astype(jnp.float32), precision=HIGHEST,
                       preferred_element_type=jnp.float32)
        self.first_wide[...] = wide[0:8]
        second_wide = wide[8:16]

        def one(i, _):
            k = lax.rem(self.chip + 1 + i, self.chips)
            self.pair_copy(k).wait_recv()
            own = self.s_ref[self.band(k), self.lanes(self.core)]
            other = self.pair[k]
            early = jnp.where(mine_first, own, other)
            late = jnp.where(mine_first, other, own)
            self.mine[k] = second_wide * early + late

            @pl.when(k != self.chip)
            def _():
                self.chunk_copy(k, self.chip).start()

            return 0

        lax.fori_loop(0, self.chips, one, 0)
        self.recv[self.chip] = self.mine[self.chip]

    def hops(self):
        def arrive(i, _):
            self.thr_copy(self.chip, lax.rem(self.chip + 1 + i, self.chips)).wait_recv()
            return 0

        lax.fori_loop(0, self.chips - 1, arrive, 0)
        self.thr_wide[...] = jnp.dot(self.thr_buf[:, 0, :], self.spread_ref[:, self.lanes(self.core)].astype(jnp.float32),
                                     precision=HIGHEST, preferred_element_type=jnp.float32)

        def hop(i, state):
            j = self.chips - 1 - i if self.reverse else i

            @pl.when(j != self.chip)
            def _():
                self.chunk_copy(self.chip, j).wait_recv()

            self.stage[j] = state
            return self.thr_wide[pl.ds(j, 1), :] * state + self.recv[j]

        lax.fori_loop(0, self.chips, hop, jnp.zeros((self.rows, self.half), jnp.float32))
        self.back[self.chip] = self.stage[self.chip]

        def give_back(i, _):
            self.back_copy(lax.rem(self.chip + 1 + i, self.chips), self.chip).start()
            return 0

        lax.fori_loop(0, self.chips - 1, give_back, 0)

    def deliver(self):
        mine_first = self.core == (1 if self.reverse else 0)

        def one(i, _):
            k = lax.rem(self.chip + i, self.chips)

            @pl.when(k != self.chip)
            def _():
                self.back_copy(self.chip, k).wait_recv()
                self.chunk_copy(k, self.chip).wait_send()

            early = self.back[k]
            own = self.s_ref[self.band(k), self.lanes(self.core)]
            late = self.first_wide[...] * early + jnp.where(mine_first, own, self.pair[k])
            self.out_ref[self.band(k), self.lanes(self.core)] = jnp.where(mine_first, early, late)
            self.give[k] = jnp.where(mine_first, late, early)
            self.give_copy(k, self.core).start()
            return 0

        lax.fori_loop(0, self.chips, one, 0)

        def got(k, _):
            self.give_copy(k, 1 - self.core).wait_recv()
            return 0

        lax.fori_loop(0, self.chips, got, 0)

    def finish(self):
        self.thr_pair_copy().wait_send()

        def one(i, _):
            k = lax.rem(self.chip + 1 + i, self.chips)
            self.pair_copy(k).wait_send()
            self.give_copy(k, self.core).wait_send()

            @pl.when(k != self.chip)
            def _():
                self.thr_copy(k, self.chip).wait_send()
                self.back_copy(k, self.chip).wait_send()

            return 0

        lax.fori_loop(0, self.chips, one, 0)


def scan_scratch(n, ns, width):
    chips = n // 2
    chunk = pltpu.VMEM((chips, ns // chips, width // 2), jnp.float32)
    tile = pltpu.VMEM((8, 128), jnp.float32)
    return [chunk] * 3 + [
        tile,
        tile,
        tile,
        pltpu.VMEM((chips, 8, 128), jnp.float32),
        pltpu.VMEM((chips, width // 2), jnp.float32),
        pltpu.VMEM((8, width // 2), jnp.float32),
    ] + [pltpu.SemaphoreType.DMA((chips,))] * 10 + [pltpu.SemaphoreType.DMA] * 2


SCAN_SCRATCH = 9 + 12


def make_scan(n, reverse, s_ref, spread_ref, out_ref, shared, scratch):
    mine, stage = shared
    give = mine
    pair, recv, back, thr_ref = scratch[:4]
    return Scan(n, reverse, s_ref, thr_ref, spread_ref, out_ref, pair, mine, recv, stage, back, give,
                *scratch[4:9], scratch[9:])


ORDERS = ((2, 1, 0), (1, 0, 2), (0, 2, 1))


class Ring:
    def __init__(self, og_ref, og_wide, nt_own, nt_send, out_ref, small, small_out, part, nt_got, og_got, og_theirs, agg1, full1, agg2, full2,
                 agg3, full3, slots_c, slots_a, total, sems):
        (self.cs, self.cr, self.ns, self.nr, self.rs, self.rr, self.xs, self.xr, self.ms, self.mr) = sems
        self.xi = lax.axis_index("dp")
        s = lax.axis_index("seq")
        self.core = lax.rem(s, 2)
        self.here = (lax.div(s, 8), lax.rem(lax.div(s, 2), 4), self.xi)
        self.sibling = {"seq": s + 1 - 2 * self.core}
        self.og_ref, self.og_wide, self.nt_own, self.nt_send = og_ref, og_wide, nt_own, nt_send
        self.out_ref = out_ref
        self.small, self.small_out = small, small_out
        self.part, self.nt_got, self.og_got, self.og_theirs = part, nt_got, og_got, og_theirs
        self.bufs = ((agg1, full1), (agg2, full2), (agg3, full3))
        self.slots_c, self.slots_a, self.total = slots_c, slots_a, total
        self.third = part.shape[-1] // 3
        self.half = self.third // 2
        self.started = []
        self.steps = {}

    def at(self, axis, index):
        if axis == 2:
            return {"dp": index}
        z, y = (index, self.here[1]) if axis == 0 else (self.here[0], index)
        return {"seq": (z * 4 + y) * 2 + self.core}

    def remote(self, src, dst, ss, rs, to):
        return pltpu.make_async_remote_copy(src_ref=src, dst_ref=dst, send_sem=ss, recv_sem=rs,
                                            device_id=to, device_id_type=MESH)

    def start(self, copies):
        for c in copies:
            c.start()
        self.started += copies
        return copies

    def og_begin(self):
        self.og_wide[...] = self.og_ref[...].astype(jnp.float32)
        self.og_copy = self.remote(self.og_wide, self.og_got, self.cs.at[0], self.cr.at[0], self.sibling)
        self.og_copy.start()

    def nt_copy(self, i, count):
        here = pl.ds(i * count, count)
        return self.remote(self.nt_send.at[here], self.nt_got.at[here], self.ns.at[i], self.nr.at[i], self.sibling)

    def og_end(self):
        self.og_copy.wait_recv()
        self.og_theirs[...] = self.og_got[...].astype(jnp.bfloat16)

    def product(self, parts):
        def got(i, _):
            self.nt_copy(i, 16 // parts).wait_recv()
            return 0

        lax.fori_loop(0, parts, got, 0)

        def one(b, _):
            z, y = lax.div(b, 4), lax.rem(b, 4)
            sums = bdot(self.nt_own[b], self.og_ref[...], 1, 0)
            sums += bdot(self.nt_got[b].astype(jnp.bfloat16), self.og_theirs[...], 1, 0)
            self.part[z, y] = sums.reshape(self.part.shape[2:])
            return 0

        lax.fori_loop(0, 16, one, 0, unroll=2)

    def region(self, step, p, t, h=None):
        order = ORDERS[p]
        index = [slice(None)] * 3
        for done in order[:step]:
            index[done] = self.here[done]
        index[order[step]] = t
        lo = p * self.third + (0 if h in (None, 0) else self.half)
        return (*index, slice(None), pl.ds(lo, self.third if h is None else self.half))

    def ways(self, step, p):
        axis = ORDERS[p][step]
        me = self.here[axis]
        return axis, lax.rem(me + 1, 4), lax.rem(me + 3, 4), lax.rem(me + 2, 4)

    def copies_of(self, step, p):
        agg, full = self.bufs[step]
        lo, hi = pl.ds(0, self.half), pl.ds(self.half, self.half)
        axis, up, down, far = self.ways(step, p)

        def go(t, h, dst, k, to):
            return self.remote(self.part.at[self.region(step, p, t, h)], dst, self.rs.at[step, p, k],
                               self.rr.at[step, p, k], self.at(axis, to))

        first = [go(far, 0, agg.at[p, 0], 0, up), go(far, 1, agg.at[p, 1], 1, down)]
        second = [go(up, 1, full.at[p, 0, ..., hi], 2, up), go(down, 0, full.at[p, 1, ..., lo], 3, down)]
        last = [go(up, 0, full.at[p, 0, ..., lo], 4, up), go(down, 1, full.at[p, 1, ..., hi], 5, down)]
        return first, second, last

    def begin(self, step):
        for p in range(3):
            self.steps[step, p] = self.copies_of(step, p)
            self.start(self.steps[step, p][0])
        for p in range(3):
            self.start(self.steps[step, p][1])

    def middle(self, step):
        agg, _ = self.bufs[step]
        for p in range(3):
            first, _, last = self.steps[step, p]
            _, up, down, _ = self.ways(step, p)
            first[0].wait_recv()
            self.part[self.region(step, p, up, 0)] += agg[p, 0]
            self.start([last[0]])
            first[1].wait_recv()
            self.part[self.region(step, p, down, 1)] += agg[p, 1]
            self.start([last[1]])

    def end(self, step):
        _, full = self.bufs[step]
        for p in range(3):
            _, second, last = self.steps[step, p]
            for c in second + last:
                c.wait_recv()
            here = self.region(step, p, self.here[ORDERS[p][step]])
            self.part[here] += full[p, 0] + full[p, 1]
            if step < 2:
                self.steps[step + 1, p] = self.copies_of(step + 1, p)
                self.start(self.steps[step + 1, p][0] + self.steps[step + 1, p][1])

    def small_pair_begin(self):
        self.small_pair = self.start([
            self.remote(self.small, self.slots_c.at[self.core], self.cs.at[2], self.cr.at[2], self.sibling)])
        self.slots_c[self.core] = self.small[...]

    def small_pair_end(self):
        self.small_pair[0].wait_recv()
        self.total[0] = self.slots_c[0] + self.slots_c[1]

    def small_begin(self, k):
        axis = (2, 1, 0)[k]
        me = self.here[axis]
        self.smalls = self.start([
            self.remote(self.total.at[k], self.slots_a.at[k, me], self.ms.at[k, d - 1], self.mr.at[k, d - 1],
                        self.at(axis, lax.rem(me + d, 4)))
            for d in (1, 2, 3)])
        self.slots_a[k, me] = self.total[k]

    def small_end(self, k):
        for c in self.smalls:
            c.wait_recv()
        now = (self.slots_a[k, 0] + self.slots_a[k, 1]) + (self.slots_a[k, 2] + self.slots_a[k, 3])
        if k < 2:
            self.total[k + 1] = now
        else:
            self.small_out[...] = now

    def share_begin(self):
        z, y, x = self.here
        self.out_ref[x] = self.part[z, y, x]
        self.start([
            self.remote(self.out_ref.at[x], self.out_ref.at[x], self.xs.at[d - 1], self.xr.at[d - 1],
                        {"dp": lax.rem(x + d, 4)})
            for d in (1, 2, 3)])

    def share_end(self):
        for d in (1, 2, 3):
            came = lax.rem(self.xi + 4 - d, 4)
            self.remote(self.out_ref.at[came], self.out_ref.at[came], self.xs.at[d - 1], self.xr.at[d - 1],
                        {"dp": came}).wait_recv()

    def finish(self):
        for c in self.started:
            c.wait_send()


def ring_scratch(rows, cols, span, lines):
    f32 = jnp.float32
    quarter, third, half = rows // 4, cols // 3, cols // 6
    return [
        pltpu.VMEM((4, 4, 4, quarter, cols), f32),
        pltpu.VMEM((16, rows, span), f32),
        pltpu.VMEM((span, cols), f32),
        pltpu.VMEM((span, cols), jnp.bfloat16),
        pltpu.VMEM((3, 2, 4, 4, quarter, half), f32),
        pltpu.VMEM((3, 2, 4, 4, quarter, third), f32),
        pltpu.VMEM((3, 2, 4, quarter, half), f32),
        pltpu.VMEM((3, 2, 4, quarter, third), f32),
        pltpu.VMEM((3, 2, quarter, half), f32),
        pltpu.VMEM((3, 2, quarter, third), f32),
        pltpu.VMEM((2, lines, 128), f32),
        pltpu.VMEM((3, 4, lines, 128), f32),
        pltpu.VMEM((3, lines, 128), f32),
        pltpu.SemaphoreType.DMA((3,)),
        pltpu.SemaphoreType.DMA((3,)),
        pltpu.SemaphoreType.DMA((8,)),
        pltpu.SemaphoreType.DMA((8,)),
        pltpu.SemaphoreType.DMA((3, 3, 6)),
        pltpu.SemaphoreType.DMA((3, 3, 6)),
        pltpu.SemaphoreType.DMA((3,)),
        pltpu.SemaphoreType.DMA((3,)),
        pltpu.SemaphoreType.DMA((3, 3)),
        pltpu.SemaphoreType.DMA((3, 3)),
    ]


BLOCK = 384
TAIL, LEAD, SKIP, THROUGH = range(4)


def softplus(v):
    return jnp.maximum(v, 0.0) + jnp.log1p(jnp.exp(-jnp.abs(v)))


def mixer_kernel(n, x_ref, z_ref, b_ref, c_ref, logit_in, og_ref, bias_in, rate_in, skip_in, gain_ref,
                 resets_ref, w_hbm,
                 w_out, small_out, dx_out, dz_out, db_out, dc_out, dlogit_out, mixed_out, *scratch):
    (dn, u, normed, s_buf, inc, sg, s_in, spread, lanes, w_buf, gm_hi, gm_lo, gt_hi, gt_lo, mask_ref, bk, bkt, co, cot,
     e_ref, f_ref, step_ref, sig_ref, keep_ref, open_ref, ms_acc, m2_acc, dg_acc, dc_acc, db_acc, a_acc, b_acc,
     skip_acc, end_acc, small, nt_own, nt_send, og_wide, mine, stage, par_ref, w_sem) = scratch[:42]
    rest = scratch[42:]
    ahead = make_scan(n, False, s_buf, spread, inc, (mine, stage), rest[:SCAN_SCRATCH])
    behind = make_scan(n, True, sg, spread, inc, (mine, stage), rest[SCAN_SCRATCH : 2 * SCAN_SCRATCH])
    rest = rest[2 * SCAN_SCRATCH :]
    ring = Ring(og_ref, og_wide, nt_own, nt_send, w_out, small, small_out, *rest[:13], rest[13:])
    f32, bf16 = jnp.float32, jnp.bfloat16
    span, width = x_ref.shape
    blocks = width // BLOCK

    def w_copy(i):
        slot = lax.rem(i, 2)
        return pltpu.make_async_copy(w_hbm.at[pl.ds(i * BLOCK, BLOCK)], w_buf.at[slot], w_sem.at[slot])

    barrier = pltpu.get_barrier_semaphore()
    count = ahead.greet(barrier)
    for d in (1, 2, 3):
        pl.semaphore_signal(barrier, inc=1, device_id={"dp": lax.rem(ring.xi + d, 4)}, device_id_type=MESH)
    w_copy(0).start()

    start = lax.axis_index("seq") * span
    ri = lax.broadcasted_iota(jnp.int32, (span, span), 0)
    ci = lax.broadcasted_iota(jnp.int32, (span, span), 1)
    flag_c = jnp.zeros((span, span), f32)
    flag_r = jnp.zeros((span, span), f32)
    for k in range(resets_ref.shape[1]):
        at_reset = resets_ref[0:1, k : k + 1] - start
        flag_c = jnp.where(ci == at_reset, 1.0, flag_c)
        flag_r = jnp.where(ri == at_reset, 1.0, flag_r)
    count_col = jnp.sum(jnp.where(ri >= ci, flag_c, 0.0), axis=1, keepdims=True)
    count_row = jnp.sum(jnp.where(ri <= ci, flag_r, 0.0), axis=0, keepdims=True)
    all_col = jnp.sum(flag_c, axis=1, keepdims=True)
    all_row = jnp.sum(flag_r, axis=0, keepdims=True)
    below = jnp.where(ri >= ci, 1.0, 0.0)
    mask = jnp.where((ri >= ci) & (count_col == count_row), 1.0, 0.0)
    mask_ref[...] = mask
    keep = jnp.where(count_col == all_col, 1.0, 0.0)
    opened = jnp.where(count_col == 0.0, 1.0, 0.0)
    keep_ref[...] = jnp.broadcast_to(keep, keep_ref.shape)
    open_ref[...] = jnp.broadcast_to(opened, open_ref.shape)
    b_keep = b_ref[...].astype(f32) * keep
    c_open = c_ref[...].astype(f32) * opened
    bk[...] = b_keep.astype(bf16)
    bkt[...] = b_keep.T.astype(bf16)
    co[...] = c_open.astype(bf16)
    cot[...] = c_open.T.astype(bf16)
    gm = bdot(c_ref[...], b_ref[...], 1, 1) * mask
    gm_hi[...], gm_lo[...] = split(gm)
    gt_hi[...], gt_lo[...] = split(gm.T)
    heads = logit_in.shape[0]
    u[0:128, 0:span] = jnp.zeros((128, span), f32)
    u[0:heads, 0:span] = logit_in[...].astype(f32)
    par_ref[...] = jnp.zeros_like(par_ref)
    par_ref[0:1, 0:heads] = bias_in[...]
    par_ref[1:2, 0:heads] = rate_in[...]
    par_ref[2:3, 0:heads] = skip_in[...]
    raw = u[0:128, 0:span].T + par_ref[0:1]
    step = softplus(raw)
    step_ref[...] = step
    sig_ref[...] = jax.nn.sigmoid(raw)
    cum = jnp.dot(below, -par_ref[1:2] * step, precision=HIGHEST, preferred_element_type=f32)
    last = cum[span - 1 : span]
    mid = cum[span // 2 : span // 2 + 1]
    through = jnp.where(all_row[:, :128] == 0.0, jnp.exp(last), 0.0)
    e_ref[...] = jnp.exp(cum - mid)
    f_ref[...] = step * jnp.exp(mid - cum)
    thr = jnp.broadcast_to(through, (8, 128))
    ahead.thr_ref[...] = thr
    behind.thr_ref[...] = thr
    head_of = lax.broadcasted_iota(jnp.int32, spread.shape, 1) >> 6
    spread[...] = jnp.where(lax.broadcasted_iota(jnp.int32, spread.shape, 0) == head_of, 1.0, 0.0).astype(bf16)
    per_head = jnp.concatenate(
        [jnp.exp(last - mid), jnp.exp(mid), par_ref[2:3], through, jnp.zeros((4, 128), f32)], axis=0)
    lanes[...] = jnp.dot(per_head, spread[...].astype(f32), precision=HIGHEST, preferred_element_type=f32)
    for acc in (ms_acc, m2_acc, dg_acc, dc_acc, db_acc, a_acc, b_acc, skip_acc, end_acc, small):
        acc[...] = jnp.zeros_like(acc)

    def block(i):
        return pl.ds(pl.multiple_of(i * BLOCK, 128), BLOCK)

    def every(body):
        def one(i, _):
            body(i, block(i))
            return 0

        lax.fori_loop(0, blocks, one, 0, unroll=2)

    def e_of(at):
        return dot2(split(e_ref[...]), spread[:, at], 1, 0)

    def f_of(at):
        return dot2(split(f_ref[...]), spread[:, at], 1, 0)

    def row(k, at):
        return lanes[k : k + 1, at]

    def own_state(i, at):
        fx2 = split(f_of(at) * x_ref[:, at].astype(f32))
        s_buf[:, at] = row(TAIL, at) * dot2(bkt[...], fx2, 1, 0)

    def in_span(i, at):
        fx2 = split(f_of(at) * x_ref[:, at].astype(f32))
        u[:, at] = dot2((gm_hi[...], gm_lo[...]), fx2, 1, 0)

    def project_back(i, at):
        w_copy(i).wait()

        @pl.when(i + 1 < blocks)
        def _():
            w_copy(i + 1).start()

        dn[:, at] = bdot(og_ref[...], w_buf[lax.rem(i, 2)], 1, 1)

    def read_out(i, at):
        before = inc[:, at]
        s2 = split(row(LEAD, at) * before)
        s_in[:, at] = s2[0]
        s_buf[:, at] = row(THROUGH, at) * before + s_buf[:, at]
        now = u[:, at] + dot2(co[...], s2, 1, 0)
        u[:, at] = now
        y = e_of(at) * now + row(SKIP, at) * x_ref[:, at].astype(f32)
        zf = z_ref[:, at].astype(f32)
        g = y * (zf * jax.nn.sigmoid(zf))
        ms_acc[...] += jnp.broadcast_to(jnp.sum(g * g, axis=1, keepdims=True), ms_acc.shape)
        m2_acc[...] += jnp.broadcast_to(
            jnp.sum(dn[:, at] * gain_ref[0:1, at] * g, axis=1, keepdims=True), m2_acc.shape)

    def norm(i, at):
        e = e_of(at)
        y = e * u[:, at] + row(SKIP, at) * x_ref[:, at].astype(f32)
        zf = z_ref[:, at].astype(f32)
        sig = jax.nn.sigmoid(zf)
        silu = zf * sig
        r = lax.rsqrt(ms_acc[:, 0:1] * (1.0 / width) + 1e-05)
        ghat = y * silu * r
        gain = gain_ref[0:1, at]
        out = ghat * gain
        out_low = out.astype(bf16)
        normed[:, at] = out_low
        up = out_low.astype(f32).T.reshape(BLOCK // 192, 2, 96, span)
        here = pl.ds(i * (BLOCK // 192), BLOCK // 192)
        even = ring.core == 0
        nt_own[here] = jnp.where(even, up[:, 0], up[:, 1]).astype(bf16)
        nt_send[here] = jnp.where(even, up[:, 1], up[:, 0])
        ring.nt_copy(i, BLOCK // 192).start()
        d = dn[:, at]
        sums = jnp.sum(d * ghat, axis=0, keepdims=True)
        for k in range(BLOCK // 128):
            small[pl.ds(i * (BLOCK // 128) + k, 1)] = sums[:, k * 128 : (k + 1) * 128]
        dg = r * (d * gain - ghat * (r * m2_acc[:, 0:1] * (1.0 / width)))
        dy = dg * silu
        dz_out[:, at] = (dg * y * (sig * (1.0 + zf * (1.0 - sig)))).astype(bf16)
        dn[:, at] = dy
        sg[:, at] = row(LEAD, at) * dot2(cot[...], split(e * dy), 1, 0)

    def pass_one(i, at):
        sp = spread[:, at]
        dy, xb = dn[:, at], x_ref[:, at].astype(f32)
        du = e_of(at) * dy
        fx = (f_of(at) * xb).astype(bf16)
        du2 = split(du)
        b_acc[...] += dot2(split(du * u[:, at]), sp, 1, 1)
        u[:, at] = dot2((gt_hi[...], gt_lo[...]), du2, 1, 0)
        dg_acc[...] += dot2(du2, fx, 1, 1)
        dc_acc[...] += dot2(du2, s_in[:, at], 1, 1)
        line = jnp.broadcast_to(jnp.sum(dy * xb, axis=0, keepdims=True), (8, BLOCK))
        skip_acc[...] += dot2(split(line), sp, 1, 1)

    def pass_two(i, at):
        sp = spread[:, at]
        f = f_of(at)
        fx = f * x_ref[:, at].astype(f32)
        late = inc[:, at]
        ds2 = split(row(TAIL, at) * late)
        d = u[:, at] + dot2(bk[...], ds2, 1, 0)
        dx_out[:, at] = (f * d + row(SKIP, at) * dn[:, at]).astype(bf16)
        a_acc[...] += dot2(split(fx * d), sp, 1, 1)
        db_acc[...] += dot2(fx.astype(bf16), ds2, 1, 1)
        line = jnp.broadcast_to(jnp.sum(late * s_buf[:, at], axis=0, keepdims=True), (8, BLOCK))
        end_acc[...] += dot2(split(line), sp, 1, 1)

    def project(i, at):
        w_copy(i).wait()

        @pl.when(i + 1 < blocks)
        def _():
            w_copy(i + 1).start()

        og_wide[...] += bdot(normed[:, at], w_buf[lax.rem(i, 2)], 1, 0)

    half = blocks // 2
    theirs_first = (1 - ring.core) * half

    def part_of(body, lo):
        def one(i, _):
            k = lax.rem(theirs_first + lo + i, blocks)
            body(k, block(k))
            return 0

        lax.fori_loop(0, half, one, 0, unroll=2)

    part_of(own_state, 0)
    pl.semaphore_wait(barrier, count + 3)
    ahead.begin()
    part_of(own_state, half)
    ahead.exchange()
    ring.og_begin()
    every(project_back)
    ahead.hops()
    every(in_span)
    ring.og_end()
    ahead.deliver()
    ahead.finish()
    every(read_out)
    part_of(norm, 0)
    behind.begin()
    part_of(norm, half)
    behind.exchange()
    ring.product(blocks)
    ring.begin(0)
    behind.hops()
    w_copy(0).start()
    ring.og_copy.wait_send()
    og_wide[...] = jnp.zeros_like(og_wide)
    every(pass_one)
    ring.middle(0)
    every(project)
    mixed_out[...] = og_wide[...].astype(bf16)
    behind.deliver()
    every(pass_two)

    a = a_acc[...]
    upper = jnp.where(ri <= ci, 1.0, 0.0)
    d_decay = jnp.dot(upper, b_acc[...] - a, precision=HIGHEST, preferred_element_type=f32) + end_acc[0:1]
    dlogit = (a / step_ref[...] - par_ref[1:2] * d_decay) * sig_ref[...]
    dlogit_out[...] = dlogit.T[: dlogit_out.shape[0]].astype(bf16)
    lines = width // 128
    small[lines : lines + 1] = jnp.sum(dlogit, axis=0, keepdims=True)
    small[lines + 1 : lines + 2] = jnp.sum(-step_ref[...] * d_decay, axis=0, keepdims=True)
    small[lines + 2 : lines + 3] = skip_acc[0:1]
    ring.small_pair_begin()
    ring.end(0)
    ring.small_pair_end()
    ring.small_begin(0)
    dg = dg_acc[...] * mask_ref[...]
    dc_out[...] = (dot2(split(dg), b_ref[...], 1, 0) + open_ref[...] * dc_acc[...]).astype(bf16)
    db_out[...] = (dot2(split(dg.T), c_ref[...], 1, 0) + keep_ref[...] * db_acc[...]).astype(bf16)
    ring.middle(1)
    ring.small_end(0)
    ring.small_begin(1)
    ring.end(1)
    ring.small_end(1)
    ring.small_begin(2)
    ring.middle(2)
    ring.end(2)
    ring.share_begin()
    ring.small_end(2)
    ring.share_end()
    ring.finish()

    def sent(i, _):
        ring.nt_copy(i, BLOCK // 192).wait_send()
        return 0

    lax.fori_loop(0, blocks, sent, 0)
    behind.finish()


def results_kernel(w, sums, dx, dz, db, dc, dlogit, mixed, mixed_to, dx_to, dz_to, db_to, dc_to, dlogit_to,
                   bias_to, rate_to, skip_to, gain_to, w_to, *scratch):
    pairs = ((dx, dx_to), (dz, dz_to), (mixed, mixed_to), (w, w_to), (db, db_to), (dc, dc_to), (dlogit, dlogit_to))
    held, (in_sem, out_sem) = scratch[:-2], scratch[-2:]
    into = [pltpu.make_async_copy(a, v, in_sem.at[k]) for k, ((a, _), v) in enumerate(zip(pairs, held))]
    out = [pltpu.make_async_copy(v, b, out_sem.at[k]) for k, ((_, b), v) in enumerate(zip(pairs, held))]
    for c in into:
        c.start()
    lines, heads = gain_to.shape[0], bias_to.shape[1]
    gain_to[...] = sums[0:lines]
    bias_to[...] = sums[lines : lines + 1, 0:heads]
    rate_to[...] = sums[lines + 1 : lines + 2, 0:heads]
    skip_to[...] = sums[lines + 2 : lines + 3, 0:heads]
    for a, b in zip(into, out):
        a.wait()
        b.start()
    for c in out:
        c.wait()


def per_device(n, ssm_input, gate_input, input_map, output_map, step_logit, step_bias, decay_rate, skip_gain,
               norm_gain, out_weight, resets, out_grad):
    f32, bf16 = jnp.float32, jnp.bfloat16
    _, span, width = ssm_input.shape
    ns, heads, cols = input_map.shape[2], step_bias.shape[0], out_weight.shape[1]
    rows, lines = width // 32, width // 128 + 8
    vmem = pl.BlockSpec(memory_space=pltpu.VMEM)

    def wide(*shape):
        return pltpu.VMEM(shape, f32)

    def low(*shape):
        return pltpu.VMEM(shape, bf16)

    chunk = wide(n // 2, ns // (n // 2), width // 2)
    weight_grad, sums, dx, dz, db, dc, dlogit, mixed = pl.pallas_call(
        functools.partial(mixer_kernel, n),
        out_shape=(
            jax.ShapeDtypeStruct((4, rows // 4, cols), f32),
            jax.ShapeDtypeStruct((lines, 128), f32),
            jax.ShapeDtypeStruct((span, width), bf16),
            jax.ShapeDtypeStruct((span, width), bf16),
            jax.ShapeDtypeStruct((span, ns), bf16),
            jax.ShapeDtypeStruct((span, ns), bf16),
            jax.ShapeDtypeStruct((heads, span), bf16),
            jax.ShapeDtypeStruct((span, cols), bf16),
        ),
        in_specs=[vmem] * 11 + [pl.BlockSpec(memory_space=pl.ANY)],
        out_specs=(vmem,) * 8,
        scratch_shapes=[
            wide(span, width), wide(span, width), low(span, width), wide(ns, width), wide(ns, width), wide(ns, width),
            low(ns, width), low(128, width), wide(8, width), low(2, BLOCK, cols),
            low(span, span), low(span, span), low(span, span), low(span, span), wide(span, span),
            low(span, ns), low(ns, span), low(span, ns), low(ns, span),
            wide(span, 128), wide(span, 128), wide(span, 128), wide(span, 128), wide(span, ns), wide(span, ns),
            wide(span, 128), wide(span, 128), wide(span, span), wide(span, ns), wide(span, ns),
            wide(span, 128), wide(span, 128), wide(8, 128), wide(8, 128), wide(lines, 128),
            low(16, rows, span), wide(16, rows, span), wide(span, cols), chunk, chunk,
            wide(8, 128),
            pltpu.SemaphoreType.DMA((2,)),
        ] + scan_scratch(n, ns, width) * 2 + ring_scratch(rows, cols, span, lines),
        compiler_params=pltpu.CompilerParams(
            collective_id=1, has_side_effects=True, vmem_limit_bytes=VMEM_LIMIT),
        name="mixer",
    )(ssm_input[0], gate_input[0], input_map[0], output_map[0], step_logit[0].T, out_grad[0], step_bias[None],
      decay_rate[None], skip_gain[None], norm_gain[None], resets, out_weight)
    anywhere = pl.BlockSpec(memory_space=pl.ANY)
    shapes = [(v.shape, bf16) for v in (mixed, dx, dz, db, dc, dlogit)] + [((1, heads), f32)] * 3
    shapes += [((width // 128, 128), f32), (weight_grad.shape, f32)]
    out = pl.pallas_call(
        results_kernel,
        out_shape=tuple(jax.ShapeDtypeStruct(*v) for v in shapes),
        in_specs=[anywhere, vmem] + [anywhere] * 6,
        out_specs=(anywhere,) * 6 + (vmem,) * 4 + (anywhere,),
        scratch_shapes=[pltpu.VMEM(v.shape, v.dtype) for v in (dx, dz, mixed, weight_grad, db, dc, dlogit)]
        + [pltpu.SemaphoreType.DMA((7,))] * 2,
        compiler_params=pltpu.CompilerParams(vmem_limit_bytes=VMEM_LIMIT),
        name="results",
    )(weight_grad, sums, dx, dz, db, dc, dlogit, mixed)
    return (
        *(v[None] for v in out[:5]),
        out[5].T[None],
        *(v.reshape(-1) for v in out[6:10]),
        out[10].reshape(rows, cols),
    )


def solution(mesh):
    by_rows = P("dp", "seq", None)
    return jax.shard_map(
        functools.partial(per_device, mesh.shape["seq"]),
        mesh=mesh,
        in_specs=(by_rows,) * 5 + (P(),) * 5 + (P("dp", None), by_rows),
        out_specs=(by_rows,) * 6 + (P(),) * 4 + (P("seq", None),),
        check_vma=False,
    )
```

```python
import functools

import jax
import jax.numpy as jnp
from jax import lax
from jax.experimental import pallas as pl
from jax.experimental.pallas import tpu as pltpu
from jax.sharding import PartitionSpec as P

MESH = pl.DeviceIdType.MESH
HIGHEST = lax.Precision.HIGHEST
VMEM_LIMIT = 63 * 1024 * 1024


def bdot(a, b, ca, cb):
    return lax.dot_general(
        a, b, (((ca,), (cb,)), ((), ())), preferred_element_type=jnp.float32
    )


def split(v):
    hi = v.astype(jnp.bfloat16)
    return hi, (v - hi.astype(jnp.float32)).astype(jnp.bfloat16)


def dot2(a, b, ca, cb):
    if isinstance(a, tuple) and isinstance(b, tuple):
        return bdot(a[0], b[0], ca, cb) + (bdot(a[0], b[1], ca, cb) + bdot(a[1], b[0], ca, cb))
    if isinstance(a, tuple):
        return bdot(a[0], b, ca, cb) + bdot(a[1], b, ca, cb)
    if isinstance(b, tuple):
        return bdot(a, b[0], ca, cb) + bdot(a, b[1], ca, cb)
    return bdot(a, b, ca, cb)


class Scan:
    def __init__(self, n, reverse, s_ref, thr_ref, spread_ref, out_ref, pair, mine, recv, stage, back, give,
                 thr_pair, thr_own, thr_buf, thr_wide, first_wide, sems):
        me = lax.axis_index("seq")
        self.chips, self.reverse = n // 2, reverse
        self.core, self.chip = lax.rem(me, 2), lax.div(me, 2)
        self.s_ref, self.thr_ref, self.spread_ref, self.out_ref = s_ref, thr_ref, spread_ref, out_ref
        self.pair, self.mine, self.recv, self.stage, self.back, self.give = pair, mine, recv, stage, back, give
        self.thr_pair, self.thr_own, self.thr_buf = thr_pair, thr_own, thr_buf
        self.thr_wide, self.first_wide = thr_wide, first_wide
        (self.ps, self.pr, self.ss, self.sr, self.ts, self.tr, self.bs, self.br, self.gs, self.gr, self.qs, self.qr) = sems
        ns, width = s_ref.shape
        self.rows, self.half = ns // self.chips, width // 2

    def lanes(self, core):
        return pl.ds(pl.multiple_of(core * self.half, 128), self.half)

    def band(self, k):
        return pl.ds(pl.multiple_of(k * self.rows, 8), self.rows)

    def copy(self, src, dst, ss, rs, to):
        return pltpu.make_async_remote_copy(src_ref=src, dst_ref=dst, send_sem=ss, recv_sem=rs,
                                            device_id={"seq": to}, device_id_type=MESH)

    def sibling(self):
        return self.chip * 2 + 1 - self.core

    def peer(self, k):
        return k * 2 + self.core

    def greet(self, barrier):
        pl.semaphore_signal(barrier, inc=1, device_id={"seq": self.sibling()}, device_id_type=MESH)

        def one(i, _):
            k = lax.rem(self.chip + 1 + i, self.chips)
            pl.semaphore_signal(barrier, inc=1, device_id={"seq": self.peer(k)}, device_id_type=MESH)
            return 0

        lax.fori_loop(0, self.chips - 1, one, 0)
        return self.chips

    def pair_copy(self, k):
        return self.copy(self.s_ref.at[self.band(k), self.lanes(1 - self.core)], self.pair.at[k],
                         self.ps.at[k], self.pr.at[k], self.sibling())

    def thr_pair_copy(self):
        return self.copy(self.thr_ref, self.thr_pair, self.qs, self.qr, self.sibling())

    def thr_copy(self, k, slot):
        return self.copy(self.thr_own, self.thr_buf.at[slot], self.ts.at[k], self.tr.at[slot], self.peer(k))

    def chunk_copy(self, k, slot):
        return self.copy(self.mine.at[k], self.recv.at[slot], self.ss.at[k], self.sr.at[slot], self.peer(k))

    def back_copy(self, k, slot):
        return self.copy(self.stage.at[k], self.back.at[slot], self.bs.at[k], self.br.at[slot], self.peer(k))

    def give_copy(self, k, core):
        return self.copy(self.give.at[k], self.out_ref.at[self.band(k), self.lanes(core)], self.gs.at[k], self.gr.at[k],
                         self.sibling())

    def begin(self):
        self.thr_pair_copy().start()

        def one(i, _):
            self.pair_copy(lax.rem(self.chip + 1 + i, self.chips)).start()
            return 0

        lax.fori_loop(0, self.chips, one, 0)

    def exchange(self):
        first = 1 if self.reverse else 0
        self.thr_pair_copy().wait_recv()
        mine_first = self.core == first
        thr_first = jnp.where(mine_first, self.thr_ref[...], self.thr_pair[...])
        thr_second = jnp.where(mine_first, self.thr_pair[...], self.thr_ref[...])
        self.thr_own[...] = thr_first * thr_second
        self.thr_buf[self.chip] = thr_first * thr_second

        def tell(i, _):
            self.thr_copy(lax.rem(self.chip + 1 + i, self.chips), self.chip).start()
            return 0

        lax.fori_loop(0, self.chips - 1, tell, 0)
        both = jnp.concatenate([thr_first, thr_second], axis=0)
        wide = jnp.dot(both, self.spread_ref[:, self.lanes(self.core)].astype(jnp.float32), precision=HIGHEST,
                       preferred_element_type=jnp.float32)
        self.first_wide[...] = wide[0:8]
        second_wide = wide[8:16]

        def one(i, _):
            k = lax.rem(self.chip + 1 + i, self.chips)
            self.pair_copy(k).wait_recv()
            own = self.s_ref[self.band(k), self.lanes(self.core)]
            other = self.pair[k]
            early = jnp.where(mine_first, own, other)
            late = jnp.where(mine_first, other, own)
            self.mine[k] = second_wide * early + late

            @pl.when(k != self.chip)
            def _():
                self.chunk_copy(k, self.chip).start()

            return 0

        lax.fori_loop(0, self.chips, one, 0)
        self.recv[self.chip] = self.mine[self.chip]

    def hops(self):
        def arrive(i, _):
            self.thr_copy(self.chip, lax.rem(self.chip + 1 + i, self.chips)).wait_recv()
            return 0

        lax.fori_loop(0, self.chips - 1, arrive, 0)
        self.thr_wide[...] = jnp.dot(self.thr_buf[:, 0, :], self.spread_ref[:, self.lanes(self.core)].astype(jnp.float32),
                                     precision=HIGHEST, preferred_element_type=jnp.float32)

        def hop(i, state):
            j = self.chips - 1 - i if self.reverse else i

            @pl.when(j != self.chip)
            def _():
                self.chunk_copy(self.chip, j).wait_recv()

            self.stage[j] = state
            return self.thr_wide[pl.ds(j, 1), :] * state + self.recv[j]

        lax.fori_loop(0, self.chips, hop, jnp.zeros((self.rows, self.half), jnp.float32))
        self.back[self.chip] = self.stage[self.chip]

        def give_back(i, _):
            self.back_copy(lax.rem(self.chip + 1 + i, self.chips), self.chip).start()
            return 0

        lax.fori_loop(0, self.chips - 1, give_back, 0)

    def deliver(self):
        mine_first = self.core == (1 if self.reverse else 0)

        def one(i, _):
            k = lax.rem(self.chip + i, self.chips)

            @pl.when(k != self.chip)
            def _():
                self.back_copy(self.chip, k).wait_recv()
                self.chunk_copy(k, self.chip).wait_send()

            early = self.back[k]
            own = self.s_ref[self.band(k), self.lanes(self.core)]
            late = self.first_wide[...] * early + jnp.where(mine_first, own, self.pair[k])
            self.out_ref[self.band(k), self.lanes(self.core)] = jnp.where(mine_first, early, late)
            self.give[k] = jnp.where(mine_first, late, early)
            self.give_copy(k, self.core).start()
            return 0

        lax.fori_loop(0, self.chips, one, 0)

        def got(k, _):
            self.give_copy(k, 1 - self.core).wait_recv()
            return 0

        lax.fori_loop(0, self.chips, got, 0)

    def finish(self):
        self.thr_pair_copy().wait_send()

        def one(i, _):
            k = lax.rem(self.chip + 1 + i, self.chips)
            self.pair_copy(k).wait_send()
            self.give_copy(k, self.core).wait_send()

            @pl.when(k != self.chip)
            def _():
                self.thr_copy(k, self.chip).wait_send()
                self.back_copy(k, self.chip).wait_send()

            return 0

        lax.fori_loop(0, self.chips, one, 0)


def scan_scratch(n, ns, width):
    chips = n // 2
    chunk = pltpu.VMEM((chips, ns // chips, width // 2), jnp.float32)
    tile = pltpu.VMEM((8, 128), jnp.float32)
    return [chunk] * 3 + [
        tile,
        tile,
        tile,
        pltpu.VMEM((chips, 8, 128), jnp.float32),
        pltpu.VMEM((chips, width // 2), jnp.float32),
        pltpu.VMEM((8, width // 2), jnp.float32),
    ] + [pltpu.SemaphoreType.DMA((chips,))] * 10 + [pltpu.SemaphoreType.DMA] * 2


SCAN_SCRATCH = 9 + 12


def make_scan(n, reverse, s_ref, spread_ref, out_ref, shared, scratch):
    mine, stage = shared
    give = mine
    pair, recv, back, thr_ref = scratch[:4]
    return Scan(n, reverse, s_ref, thr_ref, spread_ref, out_ref, pair, mine, recv, stage, back, give,
                *scratch[4:9], scratch[9:])


ORDERS = ((2, 1, 0), (1, 0, 2), (0, 2, 1))


class Ring:
    def __init__(self, og_ref, og_wide, nt_own, nt_send, out_ref, small, small_out, part, nt_got, og_got, og_theirs, agg1, full1, agg2, full2,
                 agg3, full3, slots_c, slots_a, total, sems):
        (self.cs, self.cr, self.ns, self.nr, self.rs, self.rr, self.xs, self.xr, self.ms, self.mr) = sems
        self.xi = lax.axis_index("dp")
        s = lax.axis_index("seq")
        self.core = lax.rem(s, 2)
        self.here = (lax.div(s, 8), lax.rem(lax.div(s, 2), 4), self.xi)
        self.sibling = {"seq": s + 1 - 2 * self.core}
        self.og_ref, self.og_wide, self.nt_own, self.nt_send = og_ref, og_wide, nt_own, nt_send
        self.out_ref = out_ref
        self.small, self.small_out = small, small_out
        self.part, self.nt_got, self.og_got, self.og_theirs = part, nt_got, og_got, og_theirs
        self.bufs = ((agg1, full1), (agg2, full2), (agg3, full3))
        self.slots_c, self.slots_a, self.total = slots_c, slots_a, total
        self.third = part.shape[-1] // 3
        self.half = self.third // 2
        self.started = []
        self.steps = {}

    def at(self, axis, index):
        if axis == 2:
            return {"dp": index}
        z, y = (index, self.here[1]) if axis == 0 else (self.here[0], index)
        return {"seq": (z * 4 + y) * 2 + self.core}

    def remote(self, src, dst, ss, rs, to):
        return pltpu.make_async_remote_copy(src_ref=src, dst_ref=dst, send_sem=ss, recv_sem=rs,
                                            device_id=to, device_id_type=MESH)

    def start(self, copies):
        for c in copies:
            c.start()
        self.started += copies
        return copies

    def og_begin(self):
        self.og_wide[...] = self.og_ref[...].astype(jnp.float32)
        self.og_copy = self.remote(self.og_wide, self.og_got, self.cs.at[0], self.cr.at[0], self.sibling)
        self.og_copy.start()

    def nt_copy(self, i, count):
        here = pl.ds(i * count, count)
        return self.remote(self.nt_send.at[here], self.nt_got.at[here], self.ns.at[i], self.nr.at[i], self.sibling)

    def og_end(self):
        self.og_copy.wait_recv()
        self.og_theirs[...] = self.og_got[...].astype(jnp.bfloat16)

    def product(self, parts):
        def got(i, _):
            self.nt_copy(i, 16 // parts).wait_recv()
            return 0

        lax.fori_loop(0, parts, got, 0)

        def one(b, _):
            z, y = lax.div(b, 4), lax.rem(b, 4)
            sums = bdot(self.nt_own[b], self.og_ref[...], 1, 0)
            sums += bdot(self.nt_got[b].astype(jnp.bfloat16), self.og_theirs[...], 1, 0)
            self.part[z, y] = sums.reshape(self.part.shape[2:])
            return 0

        lax.fori_loop(0, 16, one, 0, unroll=2)

    def region(self, step, p, t, h=None):
        order = ORDERS[p]
        index = [slice(None)] * 3
        for done in order[:step]:
            index[done] = self.here[done]
        index[order[step]] = t
        lo = p * self.third + (0 if h in (None, 0) else self.half)
        return (*index, slice(None), pl.ds(lo, self.third if h is None else self.half))

    def ways(self, step, p):
        axis = ORDERS[p][step]
        me = self.here[axis]
        return axis, lax.rem(me + 1, 4), lax.rem(me + 3, 4), lax.rem(me + 2, 4)

    def copies_of(self, step, p):
        agg, full = self.bufs[step]
        lo, hi = pl.ds(0, self.half), pl.ds(self.half, self.half)
        axis, up, down, far = self.ways(step, p)

        def go(t, h, dst, k, to):
            return self.remote(self.part.at[self.region(step, p, t, h)], dst, self.rs.at[step, p, k],
                               self.rr.at[step, p, k], self.at(axis, to))

        first = [go(far, 0, agg.at[p, 0], 0, up), go(far, 1, agg.at[p, 1], 1, down)]
        second = [go(up, 1, full.at[p, 0, ..., hi], 2, up), go(down, 0, full.at[p, 1, ..., lo], 3, down)]
        last = [go(up, 0, full.at[p, 0, ..., lo], 4, up), go(down, 1, full.at[p, 1, ..., hi], 5, down)]
        return first, second, last

    def begin(self, step):
        for p in range(3):
            self.steps[step, p] = self.copies_of(step, p)
            self.start(self.steps[step, p][0])
        for p in range(3):
            self.start(self.steps[step, p][1])

    def middle(self, step):
        agg, _ = self.bufs[step]
        for p in range(3):
            first, _, last = self.steps[step, p]
            _, up, down, _ = self.ways(step, p)
            first[0].wait_recv()
            self.part[self.region(step, p, up, 0)] += agg[p, 0]
            self.start([last[0]])
            first[1].wait_recv()
            self.part[self.region(step, p, down, 1)] += agg[p, 1]
            self.start([last[1]])

    def end(self, step):
        _, full = self.bufs[step]
        for p in range(3):
            _, second, last = self.steps[step, p]
            for c in second + last:
                c.wait_recv()
            here = self.region(step, p, self.here[ORDERS[p][step]])
            self.part[here] += full[p, 0] + full[p, 1]
            if step < 2:
                self.steps[step + 1, p] = self.copies_of(step + 1, p)
                self.start(self.steps[step + 1, p][0] + self.steps[step + 1, p][1])

    def small_pair_begin(self):
        self.small_pair = self.start([
            self.remote(self.small, self.slots_c.at[self.core], self.cs.at[2], self.cr.at[2], self.sibling)])
        self.slots_c[self.core] = self.small[...]

    def small_pair_end(self):
        self.small_pair[0].wait_recv()
        self.total[0] = self.slots_c[0] + self.slots_c[1]

    def small_begin(self, k):
        axis = (2, 1, 0)[k]
        me = self.here[axis]
        self.smalls = self.start([
            self.remote(self.total.at[k], self.slots_a.at[k, me], self.ms.at[k, d - 1], self.mr.at[k, d - 1],
                        self.at(axis, lax.rem(me + d, 4)))
            for d in (1, 2, 3)])
        self.slots_a[k, me] = self.total[k]

    def small_end(self, k):
        for c in self.smalls:
            c.wait_recv()
        now = (self.slots_a[k, 0] + self.slots_a[k, 1]) + (self.slots_a[k, 2] + self.slots_a[k, 3])
        if k < 2:
            self.total[k + 1] = now
        else:
            self.small_out[...] = now

    def share_begin(self):
        z, y, x = self.here
        self.out_ref[x] = self.part[z, y, x]
        self.start([
            self.remote(self.out_ref.at[x], self.out_ref.at[x], self.xs.at[d - 1], self.xr.at[d - 1],
                        {"dp": lax.rem(x + d, 4)})
            for d in (1, 2, 3)])

    def share_end(self):
        for d in (1, 2, 3):
            came = lax.rem(self.xi + 4 - d, 4)
            self.remote(self.out_ref.at[came], self.out_ref.at[came], self.xs.at[d - 1], self.xr.at[d - 1],
                        {"dp": came}).wait_recv()

    def finish(self):
        for c in self.started:
            c.wait_send()


def ring_scratch(rows, cols, span, lines):
    f32 = jnp.float32
    quarter, third, half = rows // 4, cols // 3, cols // 6
    return [
        pltpu.VMEM((4, 4, 4, quarter, cols), f32),
        pltpu.VMEM((16, rows, span), f32),
        pltpu.VMEM((span, cols), f32),
        pltpu.VMEM((span, cols), jnp.bfloat16),
        pltpu.VMEM((3, 2, 4, 4, quarter, half), f32),
        pltpu.VMEM((3, 2, 4, 4, quarter, third), f32),
        pltpu.VMEM((3, 2, 4, quarter, half), f32),
        pltpu.VMEM((3, 2, 4, quarter, third), f32),
        pltpu.VMEM((3, 2, quarter, half), f32),
        pltpu.VMEM((3, 2, quarter, third), f32),
        pltpu.VMEM((2, lines, 128), f32),
        pltpu.VMEM((3, 4, lines, 128), f32),
        pltpu.VMEM((3, lines, 128), f32),
        pltpu.SemaphoreType.DMA((3,)),
        pltpu.SemaphoreType.DMA((3,)),
        pltpu.SemaphoreType.DMA((8,)),
        pltpu.SemaphoreType.DMA((8,)),
        pltpu.SemaphoreType.DMA((3, 3, 6)),
        pltpu.SemaphoreType.DMA((3, 3, 6)),
        pltpu.SemaphoreType.DMA((3,)),
        pltpu.SemaphoreType.DMA((3,)),
        pltpu.SemaphoreType.DMA((3, 3)),
        pltpu.SemaphoreType.DMA((3, 3)),
    ]


BLOCK = 384
TAIL, LEAD, SKIP, THROUGH = range(4)


def softplus(v):
    return jnp.maximum(v, 0.0) + jnp.log1p(jnp.exp(-jnp.abs(v)))


def mixer_kernel(n, x_ref, z_ref, b_ref, c_ref, logit_in, og_ref, bias_in, rate_in, skip_in, gain_ref,
                 resets_ref, w_hbm,
                 w_out, small_out, dx_out, dz_out, db_out, dc_out, dlogit_out, mixed_out, *scratch):
    (dn, u, normed, s_buf, inc, sg, s_in, spread, lanes, w_buf, gm_hi, gm_lo, gt_hi, gt_lo, mask_ref, bk, bkt, co, cot,
     e_ref, f_ref, step_ref, sig_ref, keep_ref, open_ref, ms_acc, m2_acc, dg_acc, dc_acc, db_acc, a_acc, b_acc,
     skip_acc, end_acc, small, nt_own, nt_send, og_wide, mine, stage, par_ref, w_sem) = scratch[:42]
    rest = scratch[42:]
    ahead = make_scan(n, False, s_buf, spread, inc, (mine, stage), rest[:SCAN_SCRATCH])
    behind = make_scan(n, True, sg, spread, inc, (mine, stage), rest[SCAN_SCRATCH : 2 * SCAN_SCRATCH])
    rest = rest[2 * SCAN_SCRATCH :]
    ring = Ring(og_ref, og_wide, nt_own, nt_send, w_out, small, small_out, *rest[:13], rest[13:])
    f32, bf16 = jnp.float32, jnp.bfloat16
    span, width = x_ref.shape
    blocks = width // BLOCK

    def w_copy(i):
        slot = lax.rem(i, 2)
        return pltpu.make_async_copy(w_hbm.at[pl.ds(i * BLOCK, BLOCK)], w_buf.at[slot], w_sem.at[slot])

    barrier = pltpu.get_barrier_semaphore()
    count = ahead.greet(barrier)
    for d in (1, 2, 3):
        pl.semaphore_signal(barrier, inc=1, device_id={"dp": lax.rem(ring.xi + d, 4)}, device_id_type=MESH)
    w_copy(0).start()

    start = lax.axis_index("seq") * span
    ri = lax.broadcasted_iota(jnp.int32, (span, span), 0)
    ci = lax.broadcasted_iota(jnp.int32, (span, span), 1)
    flag_c = jnp.zeros((span, span), f32)
    flag_r = jnp.zeros((span, span), f32)
    for k in range(resets_ref.shape[1]):
        at_reset = resets_ref[0:1, k : k + 1] - start
        flag_c = jnp.where(ci == at_reset, 1.0, flag_c)
        flag_r = jnp.where(ri == at_reset, 1.0, flag_r)
    count_col = jnp.sum(jnp.where(ri >= ci, flag_c, 0.0), axis=1, keepdims=True)
    count_row = jnp.sum(jnp.where(ri <= ci, flag_r, 0.0), axis=0, keepdims=True)
    all_col = jnp.sum(flag_c, axis=1, keepdims=True)
    all_row = jnp.sum(flag_r, axis=0, keepdims=True)
    below = jnp.where(ri >= ci, 1.0, 0.0)
    mask = jnp.where((ri >= ci) & (count_col == count_row), 1.0, 0.0)
    mask_ref[...] = mask
    keep = jnp.where(count_col == all_col, 1.0, 0.0)
    opened = jnp.where(count_col == 0.0, 1.0, 0.0)
    keep_ref[...] = jnp.broadcast_to(keep, keep_ref.shape)
    open_ref[...] = jnp.broadcast_to(opened, open_ref.shape)
    b_keep = b_ref[...].astype(f32) * keep
    c_open = c_ref[...].astype(f32) * opened
    bk[...] = b_keep.astype(bf16)
    bkt[...] = b_keep.T.astype(bf16)
    co[...] = c_open.astype(bf16)
    cot[...] = c_open.T.astype(bf16)
    gm = bdot(c_ref[...], b_ref[...], 1, 1) * mask
    gm_hi[...], gm_lo[...] = split(gm)
    gt_hi[...], gt_lo[...] = split(gm.T)
    heads = logit_in.shape[0]
    u[0:128, 0:span] = jnp.zeros((128, span), f32)
    u[0:heads, 0:span] = logit_in[...].astype(f32)
    par_ref[...] = jnp.zeros_like(par_ref)
    par_ref[0:1, 0:heads] = bias_in[...]
    par_ref[1:2, 0:heads] = rate_in[...]
    par_ref[2:3, 0:heads] = skip_in[...]
    raw = u[0:128, 0:span].T + par_ref[0:1]
    step = softplus(raw)
    step_ref[...] = step
    sig_ref[...] = jax.nn.sigmoid(raw)
    cum = jnp.dot(below, -par_ref[1:2] * step, precision=HIGHEST, preferred_element_type=f32)
    last = cum[span - 1 : span]
    mid = cum[span // 2 : span // 2 + 1]
    through = jnp.where(all_row[:, :128] == 0.0, jnp.exp(last), 0.0)
    e_ref[...] = jnp.exp(cum - mid)
    f_ref[...] = step * jnp.exp(mid - cum)
    thr = jnp.broadcast_to(through, (8, 128))
    ahead.thr_ref[...] = thr
    behind.thr_ref[...] = thr
    head_of = lax.broadcasted_iota(jnp.int32, spread.shape, 1) >> 6
    spread[...] = jnp.where(lax.broadcasted_iota(jnp.int32, spread.shape, 0) == head_of, 1.0, 0.0).astype(bf16)
    per_head = jnp.concatenate(
        [jnp.exp(last - mid), jnp.exp(mid), par_ref[2:3], through, jnp.zeros((4, 128), f32)], axis=0)
    lanes[...] = jnp.dot(per_head, spread[...].astype(f32), precision=HIGHEST, preferred_element_type=f32)
    for acc in (ms_acc, m2_acc, dg_acc, dc_acc, db_acc, a_acc, b_acc, skip_acc, end_acc, small):
        acc[...] = jnp.zeros_like(acc)

    def block(i):
        return pl.ds(pl.multiple_of(i * BLOCK, 128), BLOCK)

    def every(body):
        def one(i, _):
            body(i, block(i))
            return 0

        lax.fori_loop(0, blocks, one, 0, unroll=2)

    def e_of(at):
        return dot2(split(e_ref[...]), spread[:, at], 1, 0)

    def f_of(at):
        return dot2(split(f_ref[...]), spread[:, at], 1, 0)

    def row(k, at):
        return lanes[k : k + 1, at]

    def own_state(i, at):
        fx2 = split(f_of(at) * x_ref[:, at].astype(f32))
        s_buf[:, at] = row(TAIL, at) * dot2(bkt[...], fx2, 1, 0)

    def in_span(i, at):
        fx2 = split(f_of(at) * x_ref[:, at].astype(f32))
        u[:, at] = dot2((gm_hi[...], gm_lo[...]), fx2, 1, 0)

    def project_back(i, at):
        w_copy(i).wait()

        @pl.when(i + 1 < blocks)
        def _():
            w_copy(i + 1).start()

        dn[:, at] = bdot(og_ref[...], w_buf[lax.rem(i, 2)], 1, 1)

    def read_out(i, at):
        before = inc[:, at]
        s2 = split(row(LEAD, at) * before)
        s_in[:, at] = s2[0]
        s_buf[:, at] = row(THROUGH, at) * before + s_buf[:, at]
        now = u[:, at] + dot2(co[...], s2, 1, 0)
        u[:, at] = now
        y = e_of(at) * now + row(SKIP, at) * x_ref[:, at].astype(f32)
        zf = z_ref[:, at].astype(f32)
        g = y * (zf * jax.nn.sigmoid(zf))
        ms_acc[...] += jnp.broadcast_to(jnp.sum(g * g, axis=1, keepdims=True), ms_acc.shape)
        m2_acc[...] += jnp.broadcast_to(
            jnp.sum(dn[:, at] * gain_ref[0:1, at] * g, axis=1, keepdims=True), m2_acc.shape)

    def norm(i, at):
        e = e_of(at)
        y = e * u[:, at] + row(SKIP, at) * x_ref[:, at].astype(f32)
        zf = z_ref[:, at].astype(f32)
        sig = jax.nn.sigmoid(zf)
        silu = zf * sig
        r = lax.rsqrt(ms_acc[:, 0:1] * (1.0 / width) + 1e-05)
        ghat = y * silu * r
        gain = gain_ref[0:1, at]
        out = ghat * gain
        out_low = out.astype(bf16)
        normed[:, at] = out_low
        up = out_low.astype(f32).T.reshape(BLOCK // 192, 2, 96, span)
        here = pl.ds(i * (BLOCK // 192), BLOCK // 192)
        even = ring.core == 0
        nt_own[here] = jnp.where(even, up[:, 0], up[:, 1]).astype(bf16)
        nt_send[here] = jnp.where(even, up[:, 1], up[:, 0])
        ring.nt_copy(i, BLOCK // 192).start()
        d = dn[:, at]
        sums = jnp.sum(d * ghat, axis=0, keepdims=True)
        for k in range(BLOCK // 128):
            small[pl.ds(i * (BLOCK // 128) + k, 1)] = sums[:, k * 128 : (k + 1) * 128]
        dg = r * (d * gain - ghat * (r * m2_acc[:, 0:1] * (1.0 / width)))
        dy = dg * silu
        dz_out[:, at] = (dg * y * (sig * (1.0 + zf * (1.0 - sig)))).astype(bf16)
        dn[:, at] = dy
        sg[:, at] = row(LEAD, at) * dot2(cot[...], split(e * dy), 1, 0)

    def pass_one(i, at):
        sp = spread[:, at]
        dy, xb = dn[:, at], x_ref[:, at].astype(f32)
        du = e_of(at) * dy
        fx = (f_of(at) * xb).astype(bf16)
        du2 = split(du)
        b_acc[...] += dot2(split(du * u[:, at]), sp, 1, 1)
        u[:, at] = dot2((gt_hi[...], gt_lo[...]), du2, 1, 0)
        dg_acc[...] += dot2(du2, fx, 1, 1)
        dc_acc[...] += dot2(du2, s_in[:, at], 1, 1)
        line = jnp.broadcast_to(jnp.sum(dy * xb, axis=0, keepdims=True), (8, BLOCK))
        skip_acc[...] += dot2(split(line), sp, 1, 1)

    def pass_two(i, at):
        sp = spread[:, at]
        f = f_of(at)
        fx = f * x_ref[:, at].astype(f32)
        late = inc[:, at]
        ds2 = split(row(TAIL, at) * late)
        d = u[:, at] + dot2(bk[...], ds2, 1, 0)
        dx_out[:, at] = (f * d + row(SKIP, at) * dn[:, at]).astype(bf16)
        a_acc[...] += dot2(split(fx * d), sp, 1, 1)
        db_acc[...] += dot2(fx.astype(bf16), ds2, 1, 1)
        line = jnp.broadcast_to(jnp.sum(late * s_buf[:, at], axis=0, keepdims=True), (8, BLOCK))
        end_acc[...] += dot2(split(line), sp, 1, 1)

    def project(i, at):
        w_copy(i).wait()

        @pl.when(i + 1 < blocks)
        def _():
            w_copy(i + 1).start()

        og_wide[...] += bdot(normed[:, at], w_buf[lax.rem(i, 2)], 1, 0)

    half = blocks // 2
    theirs_first = (1 - ring.core) * half

    def part_of(body, lo):
        def one(i, _):
            k = lax.rem(theirs_first + lo + i, blocks)
            body(k, block(k))
            return 0

        lax.fori_loop(0, half, one, 0, unroll=2)

    part_of(own_state, 0)
    pl.semaphore_wait(barrier, count + 3)
    ahead.begin()
    part_of(own_state, half)
    ahead.exchange()
    ring.og_begin()
    every(project_back)
    ahead.hops()
    every(in_span)
    ring.og_end()
    ahead.deliver()
    ahead.finish()
    every(read_out)
    part_of(norm, 0)
    behind.begin()
    part_of(norm, half)
    behind.exchange()
    ring.product(blocks)
    ring.begin(0)
    behind.hops()
    w_copy(0).start()
    ring.og_copy.wait_send()
    og_wide[...] = jnp.zeros_like(og_wide)
    every(pass_one)
    ring.middle(0)
    every(project)
    mixed_out[...] = og_wide[...].astype(bf16)
    behind.deliver()
    every(pass_two)

    a = a_acc[...]
    upper = jnp.where(ri <= ci, 1.0, 0.0)
    d_decay = jnp.dot(upper, b_acc[...] - a, precision=HIGHEST, preferred_element_type=f32) + end_acc[0:1]
    dlogit = (a / step_ref[...] - par_ref[1:2] * d_decay) * sig_ref[...]
    dlogit_out[...] = dlogit.T[: dlogit_out.shape[0]].astype(bf16)
    lines = width // 128
    small[lines : lines + 1] = jnp.sum(dlogit, axis=0, keepdims=True)
    small[lines + 1 : lines + 2] = jnp.sum(-step_ref[...] * d_decay, axis=0, keepdims=True)
    small[lines + 2 : lines + 3] = skip_acc[0:1]
    ring.small_pair_begin()
    ring.end(0)
    ring.small_pair_end()
    ring.small_begin(0)
    dg = dg_acc[...] * mask_ref[...]
    dc_out[...] = (dot2(split(dg), b_ref[...], 1, 0) + open_ref[...] * dc_acc[...]).astype(bf16)
    db_out[...] = (dot2(split(dg.T), c_ref[...], 1, 0) + keep_ref[...] * db_acc[...]).astype(bf16)
    ring.middle(1)
    ring.small_end(0)
    ring.small_begin(1)
    ring.end(1)
    ring.small_end(1)
    ring.small_begin(2)
    ring.middle(2)
    ring.end(2)
    ring.share_begin()
    ring.small_end(2)
    ring.share_end()
    ring.finish()

    def sent(i, _):
        ring.nt_copy(i, BLOCK // 192).wait_send()
        return 0

    lax.fori_loop(0, blocks, sent, 0)
    behind.finish()


def results_kernel(w, sums, dx, dz, db, dc, dlogit, mixed, mixed_to, dx_to, dz_to, db_to, dc_to, dlogit_to,
                   bias_to, rate_to, skip_to, gain_to, w_to, *scratch):
    pairs = ((dx, dx_to), (dz, dz_to), (mixed, mixed_to), (w, w_to), (db, db_to), (dc, dc_to), (dlogit, dlogit_to))
    held, (in_sem, out_sem) = scratch[:-2], scratch[-2:]
    pieces = []
    for (a, b), v in zip(pairs, held):
        if len(v.shape) == 2 and v.shape[0] % 64 == 0 and v.shape[1] > 128:
            cuts = [pl.ds(lo, 64) for lo in range(0, v.shape[0], 64)]
            pieces += [(a.at[cut], v.at[cut], b.at[cut]) for cut in cuts]
        else:
            pieces.append((a, v, b))
    into = [pltpu.make_async_copy(a, v, in_sem.at[k]) for k, (a, v, _) in enumerate(pieces)]
    out = [pltpu.make_async_copy(v, b, out_sem.at[k]) for k, (_, v, b) in enumerate(pieces)]
    for c in into:
        c.start()
    lines, heads = gain_to.shape[0], bias_to.shape[1]
    gain_to[...] = sums[0:lines]
    bias_to[...] = sums[lines : lines + 1, 0:heads]
    rate_to[...] = sums[lines + 1 : lines + 2, 0:heads]
    skip_to[...] = sums[lines + 2 : lines + 3, 0:heads]
    for a, b in zip(into, out):
        a.wait()
        b.start()
    for c in out:
        c.wait()


def per_device(n, ssm_input, gate_input, input_map, output_map, step_logit, step_bias, decay_rate, skip_gain,
               norm_gain, out_weight, resets, out_grad):
    f32, bf16 = jnp.float32, jnp.bfloat16
    _, span, width = ssm_input.shape
    ns, heads, cols = input_map.shape[2], step_bias.shape[0], out_weight.shape[1]
    rows, lines = width // 32, width // 128 + 8
    vmem = pl.BlockSpec(memory_space=pltpu.VMEM)

    def wide(*shape):
        return pltpu.VMEM(shape, f32)

    def low(*shape):
        return pltpu.VMEM(shape, bf16)

    chunk = wide(n // 2, ns // (n // 2), width // 2)
    weight_grad, sums, dx, dz, db, dc, dlogit, mixed = pl.pallas_call(
        functools.partial(mixer_kernel, n),
        out_shape=(
            jax.ShapeDtypeStruct((4, rows // 4, cols), f32),
            jax.ShapeDtypeStruct((lines, 128), f32),
            jax.ShapeDtypeStruct((span, width), bf16),
            jax.ShapeDtypeStruct((span, width), bf16),
            jax.ShapeDtypeStruct((span, ns), bf16),
            jax.ShapeDtypeStruct((span, ns), bf16),
            jax.ShapeDtypeStruct((heads, span), bf16),
            jax.ShapeDtypeStruct((span, cols), bf16),
        ),
        in_specs=[vmem] * 11 + [pl.BlockSpec(memory_space=pl.ANY)],
        out_specs=(vmem,) * 8,
        scratch_shapes=[
            wide(span, width), wide(span, width), low(span, width), wide(ns, width), wide(ns, width), wide(ns, width),
            low(ns, width), low(128, width), wide(8, width), low(2, BLOCK, cols),
            low(span, span), low(span, span), low(span, span), low(span, span), wide(span, span),
            low(span, ns), low(ns, span), low(span, ns), low(ns, span),
            wide(span, 128), wide(span, 128), wide(span, 128), wide(span, 128), wide(span, ns), wide(span, ns),
            wide(span, 128), wide(span, 128), wide(span, span), wide(span, ns), wide(span, ns),
            wide(span, 128), wide(span, 128), wide(8, 128), wide(8, 128), wide(lines, 128),
            low(16, rows, span), wide(16, rows, span), wide(span, cols), chunk, chunk,
            wide(8, 128),
            pltpu.SemaphoreType.DMA((2,)),
        ] + scan_scratch(n, ns, width) * 2 + ring_scratch(rows, cols, span, lines),
        compiler_params=pltpu.CompilerParams(
            collective_id=1, has_side_effects=True, vmem_limit_bytes=VMEM_LIMIT),
        name="mixer",
    )(ssm_input[0], gate_input[0], input_map[0], output_map[0], step_logit[0].T, out_grad[0], step_bias[None],
      decay_rate[None], skip_gain[None], norm_gain[None], resets, out_weight)
    anywhere = pl.BlockSpec(memory_space=pl.ANY)
    shapes = [(v.shape, bf16) for v in (mixed, dx, dz, db, dc, dlogit)] + [((1, heads), f32)] * 3
    shapes += [((width // 128, 128), f32), (weight_grad.shape, f32)]
    out = pl.pallas_call(
        results_kernel,
        out_shape=tuple(jax.ShapeDtypeStruct(*v) for v in shapes),
        in_specs=[anywhere, vmem] + [anywhere] * 6,
        out_specs=(anywhere,) * 6 + (vmem,) * 4 + (anywhere,),
        scratch_shapes=[pltpu.VMEM(v.shape, v.dtype) for v in (dx, dz, mixed, weight_grad, db, dc, dlogit)]
        + [pltpu.SemaphoreType.DMA((16,))] * 2,
        compiler_params=pltpu.CompilerParams(vmem_limit_bytes=VMEM_LIMIT),
        name="results",
    )(weight_grad, sums, dx, dz, db, dc, dlogit, mixed)
    return (
        *(v[None] for v in out[:5]),
        out[5].T[None],
        *(v.reshape(-1) for v in out[6:10]),
        out[10].reshape(rows, cols),
    )


def solution(mesh):
    by_rows = P("dp", "seq", None)
    return jax.shard_map(
        functools.partial(per_device, mesh.shape["seq"]),
        mesh=mesh,
        in_specs=(by_rows,) * 5 + (P(),) * 5 + (P("dp", None), by_rows),
        out_specs=(by_rows,) * 6 + (P(),) * 4 + (P("seq", None),),
        check_vma=False,
    )
```
